512 devices in a mesh: tok: 128 (over y, z, core), head: 4 (over x).
Axes of the slice: x: 4, y: 8, z: 8, core: 2. Of those that a mesh axis runs over, the one named last changes fastest.
Arguments:
- teacher_q: bfloat16 [16384, 5120], P('tok', 'head'), may hold values from -24 to 24
- teacher_k: bfloat16 [16384, 5120], P('tok', 'head'), may hold values from -24 to 24
- teacher_v: bfloat16 [16384, 5120], P('tok', 'head'), may hold values from -24 to 24
- student_q: bfloat16 [16384, 1536], P('tok', 'head'), may hold values from -24 to 24
- student_k: bfloat16 [16384, 1536], P('tok', 'head'), may hold values from -24 to 24
- student_v: bfloat16 [16384, 1536], P('tok', 'head'), may hold values from -24 to 24
- doc_ids: int32 [16384], replicated, may hold values from 0 to 127, never falling along the last dimension, each value on 1 to 384 neighbouring positions
- row_weight: float32 [16384], replicated, may hold values from 4 to 64
Outputs:
- grad_q: float32 [16384, 1536], P('tok', 'head')
- grad_k: float32 [16384, 1536], P('tok', 'head')
- grad_v: float32 [16384, 1536], P('tok', 'head')
- loss: float32 [], replicated
The draws below stay inside these ranges and needn't reach their ends.
Inputs may be any that keep to these rules, and one draw needn't show every extreme that they name: `doc_ids`: document ids never fall along the packed tokens.
All inputs are finite; a program needn't handle non-finite values.
Results may differ from the reference program's by a relative error of at most 0.008.
Values may be sent and summed in bfloat16 or wider, within the bound.
No kernel may reach another device: no remote copies, remote signals or barrier semaphores. Data moves between devices by JAX's collectives and lax.ppermute only.
A program may use at most 64 MiB of HBM per device.

```python
import math
import jax
import jax.numpy as jnp
import numpy as np
from jax import lax

H = 32
DT = 160
DS = 48
TOK_DEV = 128
TOKENS = 16384
SPAN = 384


def shaped_rows(key, width, strength):
    keys = jax.random.split(key, 5)
    base = jax.random.normal(keys[0], (TOKENS, width), jnp.float32) * 0.5
    place = jnp.arange(TOKENS) % 64
    amp = strength * (1.2 + jax.random.uniform(keys[2], (TOKENS, 1), jnp.float32))
    unit = jax.random.normal(keys[3], (TOKENS, width), jnp.float32)
    noise = jax.random.normal(keys[4], (TOKENS, width), jnp.float32)
    first = amp * unit
    second = jnp.roll(amp, 1, axis=0) * (jnp.roll(unit, 1, axis=0) + 0.08 * noise)
    spiked = jnp.where((place == 5)[:, None], first, jnp.where((place == 6)[:, None], second, base))
    chosen = jnp.where(strength > 0, spiked, base)
    return jnp.clip(chosen, -24.0, 24.0)


def draw_teacher_q(key, part):
    key = jax.random.fold_in(key, 11)
    return shaped_rows(key, H * DT, 0.0).astype(jnp.bfloat16)


def draw_teacher_k(key, part):
    key = jax.random.fold_in(key, 12)
    return shaped_rows(key, H * DT, 0.0).astype(jnp.bfloat16)


def draw_teacher_v(key, part):
    key = jax.random.fold_in(key, 13)
    return shaped_rows(key, H * DT, 0.0).astype(jnp.bfloat16)


def draw_student_q(key, part):
    key = jax.random.fold_in(key, 14)
    return shaped_rows(key, H * DS, 0.0).astype(jnp.bfloat16)


def draw_student_k(key, part):
    key = jax.random.fold_in(key, 15)
    return shaped_rows(key, H * DS, 0.0).astype(jnp.bfloat16)


def draw_student_v(key, part):
    key = jax.random.fold_in(key, 16)
    return shaped_rows(key, H * DS, 0.0).astype(jnp.bfloat16)


def profile(number_of, total, bound, lean):
    weights = [(1 << 20) // math.isqrt(standing ** lean) + 1 for standing in range(2, number_of + 1)]
    rest, holding = total - bound - (number_of - 1), [1] * (number_of - 1)
    while rest > 0:
        free = [i for i in range(number_of - 1) if holding[i] < bound]
        whole, left = sum([weights[i] for i in free]), rest
        for i in free:
            more = min(bound - holding[i], max(1, left * weights[i] // whole), rest)
            holding[i] = holding[i] + more
            rest = rest - more
    return np.array([bound] + holding)


def uneven(own_key, amount, total, bound, lean):
    if amount == 2:
        one = jax.random.randint(own_key, (), max(1, total - bound), min(bound, total - 1) + 1)
        return jnp.stack([one, total - one])
    lengths = jnp.asarray(profile(amount, total, bound, lean), jnp.int32)
    twos = (amount - 1) // 2
    source_of, taker = lengths[1:1 + 2 * twos:2], lengths[2:2 + 2 * twos:2]
    margin = jnp.minimum(source_of - 1, bound - taker)
    moved = jax.random.randint(jax.random.fold_in(own_key, 1), (twos,), 0, 1 << 20) % (margin + 1)
    lengths = lengths.at[1:1 + 2 * twos:2].set(source_of - moved).at[2:2 + 2 * twos:2].set(taker + moved)
    return lengths[jax.random.permutation(jax.random.fold_in(own_key, 2), amount)]


def setup_inputs(seed: int = 0) -> dict:
    splits = jax.random.split(jax.random.key(seed), 9)
    return {
        "teacher_q": draw_teacher_q(jax.random.fold_in(splits[8], 71), 0),
        "teacher_k": draw_teacher_k(jax.random.fold_in(splits[8], 71), 0),
        "teacher_v": draw_teacher_v(jax.random.fold_in(splits[8], 71), 0),
        "student_q": draw_student_q(jax.random.fold_in(splits[8], 71), 0),
        "student_k": draw_student_k(jax.random.fold_in(splits[8], 71), 0),
        "student_v": draw_student_v(jax.random.fold_in(splits[8], 71), 0),
        "doc_ids": jnp.searchsorted(jnp.cumsum(uneven(splits[6], TOKENS // TOK_DEV, TOKENS, SPAN, 2)), jnp.arange(TOKENS), side="right").astype(jnp.int32),
        "row_weight": jnp.clip(jnp.exp(jax.random.uniform(splits[7], (TOKENS,), jnp.float32, math.log(4.0), math.log(64.0))), 4.0, 64.0),
    }


def masked_lse(score, allowed):
    top = jnp.max(jnp.where(allowed, score, -1e30), axis=-1)
    total = jnp.sum(jnp.where(allowed, jnp.exp(score - top[..., None]), 0.0), axis=-1)
    return jnp.log(total) + top


def heads_terms(t_rows, t_keys, s_rows, s_keys, allowed, weight):
    zt = jnp.einsum("qhd,khd->hqk", t_rows.astype(jnp.float32), t_keys.astype(jnp.float32)) * (DT ** -0.5)
    zs = jnp.einsum("qhd,khd->hqk", s_rows.astype(jnp.float32), s_keys.astype(jnp.float32)) * (DS ** -0.5)
    mask = allowed[None, :, :]
    lt = masked_lse(zt, mask)
    ls = masked_lse(zs, mask)
    pt = jnp.where(mask, jnp.exp(zt - lt[..., None]), 0.0)
    ps = jnp.where(mask, jnp.exp(zs - ls[..., None]), 0.0)
    kl_rows = jnp.sum(jnp.where(mask, pt * (zt - zs), 0.0), axis=-1) - lt + ls
    total = jnp.sum(kl_rows * weight[None, :])
    scaled = (weight * (DS ** -0.5))[None, :, None]
    grads = (scaled * (ps - pt)).astype(jnp.bfloat16).astype(jnp.float32)
    row_part = jnp.einsum("hqk,khd->qhd", grads, s_keys.astype(jnp.float32))
    key_part = jnp.einsum("hqk,qhd->khd", grads, s_rows.astype(jnp.float32))
    return total, row_part, key_part


def reference(teacher_q, teacher_k, teacher_v, student_q, student_k, student_v, doc_ids, row_weight):
    lead = 3 * TOK_DEV
    window = 4 * TOK_DEV
    docs = jnp.concatenate([jnp.full((lead,), -1, jnp.int32), doc_ids.astype(jnp.int32)])

    def padded(array):
        return jnp.concatenate([jnp.zeros((lead, array.shape[1]), array.dtype), array])

    teachers = [padded(a) for a in (teacher_q, teacher_k, teacher_v)]
    students = [padded(a) for a in (student_q, student_k, student_v)]
    blocks = TOKENS // TOK_DEV
    start_grads = tuple(jnp.zeros((TOKENS + lead, H * DS), jnp.float32) for _ in range(3))

    def step(carry, block):
        grads, total = carry
        start = (block * TOK_DEV).astype(jnp.int32)
        key_docs = lax.dynamic_slice_in_dim(docs, start, window)
        query_docs = key_docs[lead:]
        key_pos = start - lead + jnp.arange(window, dtype=jnp.int32)
        query_pos = start + jnp.arange(TOK_DEV, dtype=jnp.int32)
        allowed = (key_pos[None, :] <= query_pos[:, None]) & (key_pos[None, :] >= 0) & (key_docs[None, :] == query_docs[:, None])
        weight = lax.dynamic_slice_in_dim(row_weight, start, TOK_DEV)
        updated = []
        for rel in range(3):
            t_keys = lax.dynamic_slice_in_dim(teachers[rel], start, window).reshape(window, H, DT)
            s_keys = lax.dynamic_slice_in_dim(students[rel], start, window).reshape(window, H, DS)
            part, row_part, key_part = heads_terms(t_keys[lead:], t_keys, s_keys[lead:], s_keys, allowed, weight)
            total = total + part
            grad = grads[rel]
            old_keys = lax.dynamic_slice_in_dim(grad, start, window)
            grad = lax.dynamic_update_slice_in_dim(grad, old_keys + key_part.reshape(window, H * DS), start, 0)
            old_rows = lax.dynamic_slice_in_dim(grad, start + lead, TOK_DEV)
            grad = lax.dynamic_update_slice_in_dim(grad, old_rows + row_part.reshape(TOK_DEV, H * DS), start + lead, 0)
            updated.append(grad)
        return (tuple(updated), total), None

    (grads, total), _ = lax.scan(step, (start_grads, jnp.zeros((), jnp.float32)), jnp.arange(blocks, dtype=jnp.int32))
    loss = total / (3 * H * TOKENS)
    return grads[0][lead:], grads[1][lead:], grads[2][lead:], loss
```

```python
import functools
import math

import jax
import jax.numpy as jnp
from jax import lax
from jax.experimental import pallas as pl
from jax.experimental.pallas import tpu as pltpu
from jax.sharding import Mesh
from jax.sharding import PartitionSpec as P

H = 32
DT = 160
DS = 48
SPAN = 384

BLOCK = 128
OWN = 2 * BLOCK
HALO = 192
WINDOW = OWN + 2 * HALO
FIRST_QUERY = WINDOW - OWN
HEADS = 4
TW = HEADS * DT
SW = HEADS * DS
SP = 256
REL = TW + SP
CT = DT ** (-0.5) * math.log2(math.e)
CS = DS ** (-0.5) * math.log2(math.e)
NT = (((1,), (1,)), ((), ()))
VMEM = pl.BlockSpec(memory_space=pltpu.VMEM)
SMEM = pl.BlockSpec(memory_space=pltpu.SMEM)
F32 = jnp.float32
BF16 = jnp.bfloat16


def call(kernel, out_shape, n_smem, n_vmem, scratch=(), flops=0, moved=0, exps=0):
    return pl.pallas_call(
        kernel,
        out_shape=out_shape,
        in_specs=[SMEM] * n_smem + [VMEM] * n_vmem,
        out_specs=jax.tree.map(lambda _: VMEM, out_shape),
        scratch_shapes=list(scratch),
        compiler_params=pltpu.CompilerParams(vmem_limit_bytes=40 * 1024 * 1024),
        cost_estimate=pl.CostEstimate(flops=flops, bytes_accessed=moved, transcendentals=exps),
    )


def split_kernel(core, tq, tk, tv, sq, sk, sv, send_first, send_rest, keep):
    me = core[0]
    lane = lax.broadcasted_iota(jnp.int32, (BLOCK, SP), 1)
    for rel, (teacher, student) in enumerate(((tq, sq), (tk, sk), (tv, sv))):
        send, at = (send_first, 0) if rel == 0 else (send_rest, (rel - 1) * REL)
        mine = pl.ds(pl.multiple_of(me * TW, 128), TW)
        other = pl.ds(pl.multiple_of((1 - me) * TW, 128), TW)
        keep[:, rel * REL : rel * REL + TW] = teacher[:, mine]
        send[:, at : at + TW] = teacher[:, other]
        low = jnp.where(lane < SW, student[:, :SP].astype(F32), 0.0)
        high = pltpu.roll(student[:, 128:].astype(F32), SP - (SW - 128), 1)
        high = jnp.where(lane < SW, high, 0.0)
        keep[:, rel * REL + TW : (rel + 1) * REL] = jnp.where(me == 0, low, high).astype(BF16)
        send[:, at + TW : at + REL] = jnp.where(me == 0, high, low).astype(BF16)


def edges_kernel(rels, keep_at, core, keep, recv, *outs):
    half = HALO - BLOCK
    for slot in range(rels):
        after, before = outs[2 * slot], outs[2 * slot + 1]
        ours = slice(keep_at + slot * REL, keep_at + (slot + 1) * REL)
        theirs = slice(slot * REL, (slot + 1) * REL)

        def write(first, first_at, second, second_at):
            after[:half, :] = first[BLOCK - half :, first_at]
            after[half:, :] = second[:, second_at]
            before[:BLOCK, :] = first[:, first_at]
            before[BLOCK:, :] = second[:half, second_at]

        @pl.when(core[0] == 0)
        def _():
            write(keep, ours, recv, theirs)

        @pl.when(core[0] != 0)
        def _():
            write(recv, theirs, keep, ours)


def fold(value, op):
    rows, lanes = value.shape
    return op(value.reshape(rows // 8, 8, lanes), axis=0)


def relation_kernel(
    keep_at,
    recv_at,
    core,
    starts,
    weights,
    loss_in,
    left,
    keep,
    recv,
    right,
    grad_left,
    grad_own,
    grad_right,
    loss_out,
    win,
    bias,
    rt,
    rs,
    gt,
    qs,
    bt,
):
    me = core[0]
    win[:HALO, :] = left[...]
    win[pl.ds(pl.multiple_of(HALO + me * BLOCK, 64), BLOCK), :] = keep[:, keep_at : keep_at + REL]
    win[pl.ds(pl.multiple_of(HALO + (1 - me) * BLOCK, 64), BLOCK), :] = recv[
        :, recv_at : recv_at + REL
    ]
    win[HALO + OWN :, :] = right[...]

    key = lax.broadcasted_iota(jnp.int32, (WINDOW, OWN), 0)
    query = lax.broadcasted_iota(jnp.int32, (WINDOW, OWN), 1) + FIRST_QUERY
    bias[...] = jnp.where((key >= starts[...]) & (key <= query), 0.0, -1e30)

    lane = lax.broadcasted_iota(jnp.int32, (OWN, SP), 1)
    student = slice(TW, REL)
    row = lax.broadcasted_iota(jnp.int32, (SP, SP), 0)
    col = lax.broadcasted_iota(jnp.int32, (SP, SP), 1)
    unit = jnp.where(row == col, 1.0, 0.0).astype(BF16)
    bt[...] = lax.dot_general(unit, win[:, student], NT, preferred_element_type=F32).astype(BF16)

    gt[:BLOCK, :] = jnp.zeros((BLOCK, HEADS * OWN), BF16)
    gt[WINDOW - BLOCK :, :] = jnp.zeros((BLOCK, HEADS * OWN), BF16)
    total = jnp.zeros((1, BLOCK), F32)
    step = 64
    for head in range(HEADS):
        start = head * DT // 128 * 128
        inside = (lane >= head * DT - start) & (lane < (head + 1) * DT - start)
        t_cols = slice(start, start + 256)
        t_query = win[FIRST_QUERY:, t_cols] * jnp.where(inside, 1.0, 0.0).astype(BF16)
        inside = (lane >= head * DS) & (lane < (head + 1) * DS)
        s_query = win[FIRST_QUERY:, student] * jnp.where(inside, 1.0, 0.0).astype(BF16)
        qs[head * OWN : (head + 1) * OWN, :] = s_query
        rt[...] = (
            lax.dot_general(win[:, t_cols], t_query, NT, preferred_element_type=F32) + bias[...]
        )
        rs[...] = (
            lax.dot_general(win[:, student], s_query, NT, preferred_element_type=F32) + bias[...]
        )
        for tile in range(2):
            first = tile * BLOCK
            lanes = slice(tile * BLOCK, (tile + 1) * BLOCK)
            parts = [slice(first + at, first + at + step) for at in range(0, SPAN + BLOCK, step)]
            top_t = fold(rt[parts[0], lanes], jnp.max)
            top_s = fold(rs[parts[0], lanes], jnp.max)
            for part in parts[1:]:
                top_t = jnp.maximum(top_t, fold(rt[part, lanes], jnp.max))
                top_s = jnp.maximum(top_s, fold(rs[part, lanes], jnp.max))
            top_t = jnp.max(top_t, axis=0, keepdims=True) * CT
            top_s = jnp.max(top_s, axis=0, keepdims=True) * CS
            sum_t = jnp.zeros((8, BLOCK), F32)
            sum_s = jnp.zeros((8, BLOCK), F32)
            cross = jnp.zeros((8, BLOCK), F32)
            for part in parts:
                ut = rt[part, lanes] * CT - top_t
                us = rs[part, lanes] * CS - top_s
                et = jnp.exp2(ut)
                es = jnp.exp2(us)
                sum_t = sum_t + fold(et, jnp.sum)
                sum_s = sum_s + fold(es, jnp.sum)
                cross = cross + fold(et * (ut - us), jnp.sum)
                rt[part, lanes] = et
                rs[part, lanes] = es
            sum_t = jnp.sum(sum_t, axis=0, keepdims=True)
            sum_s = jnp.sum(sum_s, axis=0, keepdims=True)
            cross = jnp.sum(cross, axis=0, keepdims=True)
            weight = weights[:, lanes]
            total = total + weight * (cross / sum_t - jnp.log2(sum_t) + jnp.log2(sum_s))
            scale_t = weight * DS ** (-0.5) / sum_t
            scale_s = weight * DS ** (-0.5) / sum_s
            g_cols = slice(head * OWN + tile * BLOCK, head * OWN + (tile + 1) * BLOCK)
            for part in parts:
                gt[part, g_cols] = (rs[part, lanes] * scale_s - rt[part, lanes] * scale_t).astype(
                    BF16
                )

    loss_out[...] = loss_in[...] + total * math.log(2.0)
    key_grad = jnp.dot(gt[...], qs[...], preferred_element_type=F32)
    row_grads = [
        jnp.dot(
            bt[head * DS : (head + 1) * DS, :],
            gt[:, head * OWN : (head + 1) * OWN],
            preferred_element_type=F32,
        )
        for head in range(HEADS)
    ]
    row_grads.append(jnp.zeros((SP - SW, OWN), F32))
    row_grad = jnp.concatenate(row_grads, axis=0).T
    late = HALO + OWN - FIRST_QUERY
    grad_left[...] = key_grad[:HALO].astype(BF16)
    grad_own[: OWN - late, :] = key_grad[HALO:FIRST_QUERY]
    grad_own[OWN - late :, :] = key_grad[FIRST_QUERY : HALO + OWN] + row_grad[:late]
    grad_right[...] = (key_grad[HALO + OWN :] + row_grad[late:]).astype(BF16)


def join_kernel(loss, l0, l1, l2, r0, r1, r2, to_before, to_after, copies):
    copies[...] = jnp.broadcast_to(loss[...], copies.shape)
    for rel, (left, right) in enumerate(((l0, r0), (l1, r1), (l2, r2))):
        to_before[:, rel * SP : (rel + 1) * SP] = left[...]
        to_after[:, rel * SP : (rel + 1) * SP] = right[...]


def merge_kernel(core, losses, o0, o1, o2, from_after, from_before, keep, send, copies, acc):
    me = core[0]
    copies[...] = jnp.broadcast_to(jnp.sum(losses[...], axis=0, keepdims=True), copies.shape)
    for rel, own in enumerate((o0, o1, o2)):
        acc[:, rel * SP : (rel + 1) * SP] = own[...]
    acc[OWN - HALO :, :] = acc[OWN - HALO :, :] + from_after[...].astype(F32)
    acc[:HALO, :] = acc[:HALO, :] + from_before[...].astype(F32)
    keep[...] = acc[pl.ds(pl.multiple_of(me * BLOCK, 128), BLOCK), :]
    send[...] = acc[pl.ds(pl.multiple_of((1 - me) * BLOCK, 128), BLOCK), :]


def place_kernel(tokens, core, losses, keep, recv, oq, ok, ov, loss):
    me = core[0]
    total = jnp.sum(jnp.sum(losses[...], axis=0, keepdims=True), axis=1, keepdims=True)
    loss[...] = total * (1.0 / (3 * H * tokens))
    empty = jnp.zeros((BLOCK, 2 * SW - SP), F32)
    for rel, out in enumerate((oq, ok, ov)):
        ours = jnp.concatenate([keep[:, rel * SP : (rel + 1) * SP], empty], axis=1)
        theirs = jnp.concatenate([recv[:, rel * SP : (rel + 1) * SP], empty], axis=1)
        low = jnp.where(me == 0, ours, theirs)
        high = jnp.where(me == 0, theirs, ours)
        out[...] = low + pltpu.roll(high, SW, 1)


def shape(rows, cols, dtype):
    return jax.ShapeDtypeStruct((rows, cols), dtype)


def body(teacher_q, teacher_k, teacher_v, student_q, student_k, student_v, doc_ids, row_weight):
    tok = ("y", "z", "core")
    count = lax.axis_size("y") * lax.axis_size("z") * 2
    core = lax.axis_index("core").astype(jnp.int32).reshape(1)
    chip = lax.axis_index("y") * lax.axis_size("z") + lax.axis_index("z")

    def other_core(value):
        return lax.ppermute(value, "core", [(0, 1), (1, 0)])

    def next_chip(value, chips):
        step = 2 * chips
        return lax.ppermute(value, tok, [(i, (i + step) % count) for i in range(count)])

    packed = [shape(BLOCK, n * REL, BF16) for n in (1, 2, 3)]
    send_first, send_rest, keep = call(split_kernel, packed, 1, 6, moved=4 << 20)(
        core, teacher_q, teacher_k, teacher_v, student_q, student_k, student_v
    )
    recv_first = other_core(send_first)
    recv_rest = other_core(send_rest)
    edge = shape(HALO, REL, BF16)
    edges = list(
        call(functools.partial(edges_kernel, 1, 0), [edge] * 2, 1, 2, moved=1 << 20)(
            core, keep, recv_first
        )
    )
    edges += call(functools.partial(edges_kernel, 2, REL), [edge] * 4, 1, 2, moved=2 << 20)(
        core, keep, recv_rest
    )
    lefts = [next_chip(edges[2 * rel], 1) for rel in range(3)]
    rights = [next_chip(edges[2 * rel + 1], -1) for rel in range(3)]

    doc_ids, row_weight, _ = lax.optimization_barrier((doc_ids, row_weight, edges[0]))
    far = 1 << 20
    docs = jnp.concatenate([doc_ids[-HALO:] - far, doc_ids, doc_ids[:HALO] + far])
    docs = lax.dynamic_slice_in_dim(docs, chip * OWN, WINDOW)
    weight = jnp.concatenate([row_weight, row_weight[:HALO]])
    weight = lax.dynamic_slice_in_dim(weight, chip * OWN + HALO, OWN)[None, :]
    starts = jnp.sum(docs[:, None] < docs[None, FIRST_QUERY:], axis=0, dtype=jnp.int32)[None, :]

    loss = jnp.zeros((1, BLOCK), F32)
    grads = []
    for rel in range(3):
        recv, recv_at = (recv_first, 0) if rel == 0 else (recv_rest, (rel - 1) * REL)
        out = call(
            functools.partial(relation_kernel, rel * REL, recv_at),
            [
                shape(HALO, SP, BF16),
                shape(OWN, SP, F32),
                shape(HALO, SP, BF16),
                shape(1, BLOCK, F32),
            ],
            1,
            7,
            scratch=[
                pltpu.VMEM((WINDOW, REL), BF16),
                pltpu.VMEM((WINDOW, OWN), F32),
                pltpu.VMEM((WINDOW, OWN), F32),
                pltpu.VMEM((WINDOW, OWN), F32),
                pltpu.VMEM((WINDOW, HEADS * OWN), BF16),
                pltpu.VMEM((HEADS * OWN, SP), BF16),
                pltpu.VMEM((SP, WINDOW), BF16),
            ],
            flops=2 * 16 * WINDOW * OWN * 256,
            moved=2 << 20,
            exps=2 * HEADS * WINDOW * OWN,
        )(core, starts, weight, loss, lefts[rel], keep, recv, rights[rel])
        grads.append(out[:3])
        loss = out[3]

    stages = (("z", "core"), ("y", "head"))
    copies = [shape(lax.axis_size(axes), BLOCK, F32) for axes in stages]

    def exchange(value, axes):
        return lax.all_to_all(value, axes, 0, 0, tiled=True)

    returned = shape(HALO, 3 * SP, BF16)
    to_before, to_after, partial = call(
        join_kernel, [returned] * 2 + [copies[0]], 0, 7, moved=1 << 20
    )(loss, *(g[0] for g in grads), *(g[2] for g in grads))
    from_after = next_chip(to_before, -1)
    from_before = next_chip(to_after, 1)
    partial = exchange(partial, stages[0])

    third = shape(BLOCK, 3 * SP, F32)
    kept, sent, partial = call(
        merge_kernel,
        [third] * 2 + [copies[1]],
        1,
        6,
        scratch=[pltpu.VMEM((OWN, 3 * SP), F32)],
        moved=2 << 20,
    )(core, partial, *(g[1] for g in grads), from_after, from_before)
    received = other_core(sent)
    partial = exchange(partial, stages[1])
    out = shape(BLOCK, 2 * SW, F32)
    grad_q, grad_k, grad_v, loss = call(
        functools.partial(place_kernel, doc_ids.shape[0]),
        [out] * 3 + [shape(1, 1, F32)],
        1,
        3,
        moved=1 << 20,
    )(core, partial, kept, received)
    return grad_q, grad_k, grad_v, loss[0, 0]


def solution(mesh):
    tok, head = mesh.devices.shape
    y = 8 if tok == 128 else 2
    fine = Mesh(mesh.devices.reshape(y, tok // (2 * y), 2, head), ("y", "z", "core", "head"))
    rows = ("y", "z", "core")
    placed = (P(rows, "head"),) * 6 + (P(), P())
    return jax.shard_map(
        body,
        mesh=fine,
        in_specs=placed,
        out_specs=(P(rows, "head"),) * 3 + (P(),),
        check_vma=False,
    )
```

```python
import functools
import math

import jax
import jax.numpy as jnp
from jax import lax
from jax.experimental import pallas as pl
from jax.experimental.pallas import tpu as pltpu
from jax.sharding import Mesh
from jax.sharding import PartitionSpec as P

H = 32
DT = 160
DS = 48
SPAN = 384

BLOCK = 128
OWN = 2 * BLOCK
HALO = 192
WINDOW = OWN + 2 * HALO
FIRST_QUERY = WINDOW - OWN
HEADS = 4
TW = HEADS * DT
SW = HEADS * DS
SP = 256
REL = TW + SP
WIDTH_A = 2 * TW + 2 * SW
T_AT = (0, TW, 0)
S_AT = (2 * TW, 2 * TW + 128, TW)
S_OFF = (0, SW - 128, 0)
EXTRA = 16
CT = DT ** (-0.5) * math.log2(math.e)
CS = DS ** (-0.5) * math.log2(math.e)
NT = (((1,), (1,)), ((), ()))
VMEM = pl.BlockSpec(memory_space=pltpu.VMEM)
SMEM = pl.BlockSpec(memory_space=pltpu.SMEM)
HBM = pl.BlockSpec(memory_space=pltpu.HBM)
F32 = jnp.float32
BF16 = jnp.bfloat16


def call(kernel, out_shape, in_specs, scratch=(), flops=0, moved=0, exps=0, limit=40):
    return pl.pallas_call(
        kernel,
        out_shape=out_shape,
        in_specs=in_specs,
        out_specs=jax.tree.map(lambda _: VMEM, out_shape),
        scratch_shapes=list(scratch),
        compiler_params=pltpu.CompilerParams(vmem_limit_bytes=limit << 20),
        cost_estimate=pl.CostEstimate(flops=flops, bytes_accessed=moved, transcendentals=exps),
    )


def split_kernel(core, *refs):
    arrays, (send_a, keep_a, send_b, keep_b), buffers, sems = (
        refs[:6],
        refs[6:10],
        refs[10:16],
        refs[16],
    )
    me = core[0]
    copies = [
        pltpu.make_async_copy(array, buffer, sems.at[i])
        for i, (array, buffer) in enumerate(zip(arrays, buffers))
    ]
    for copy in copies:
        copy.start()
    for copy in copies:
        copy.wait()
    lane = lax.broadcasted_iota(jnp.int32, (BLOCK, SP), 1)
    mine = pl.ds(pl.multiple_of(me * TW, 128), TW)
    other = pl.ds(pl.multiple_of((1 - me) * TW, 128), TW)
    ours, theirs = [], []
    for rel in range(3):
        teacher, student = buffers[rel], buffers[3 + rel]
        keep, send, at = (keep_b, send_b, 0) if rel == 2 else (keep_a, send_a, rel * TW)
        keep[:, at : at + TW] = teacher[:, mine]
        send[:, at : at + TW] = teacher[:, other]
        low = jnp.where(lane < SW, student[:, :SP].astype(F32), 0.0)
        high = pltpu.roll(student[:, 128:].astype(F32), SP - (SW - 128), 1)
        high = jnp.where(lane < SW, high, 0.0)
        ours.append(jnp.where(me == 0, low, high))
        theirs.append(jnp.where(me == 0, high, low))
    for halves, out_a, out_b in ((ours, keep_a, keep_b), (theirs, send_a, send_b)):
        second = pltpu.roll(halves[1], S_OFF[1], 1)
        at = 2 * TW
        out_a[:, at : at + 128] = halves[0][:, :128].astype(BF16)
        out_a[:, at + 128 : at + 256] = (halves[0][:, 128:] + second[:, :128]).astype(BF16)
        out_a[:, at + 256 : at + 384] = second[:, 128:].astype(BF16)
        out_b[:, TW:] = halves[2].astype(BF16)


def edges_kernel(core, keep, recv, one, two):
    half = HALO - BLOCK

    def write(first, second, after, before):
        after[:half, :] = first[BLOCK - half :, :]
        after[half:, :] = second[...]
        before[:BLOCK, :] = first[...]
        before[BLOCK:, :] = second[:half, :]

    @pl.when(core[0] == 0)
    def _():
        write(keep, recv, one, two)

    @pl.when(core[0] != 0)
    def _():
        write(recv, keep, two, one)


def fold(value, op):
    rows, lanes = value.shape
    return op(value.reshape(rows // 8, 8, lanes), axis=0)


def relation_kernel(
    t_at,
    s_at,
    s_off,
    core,
    starts,
    weights,
    loss_in,
    keep,
    recv,
    one,
    two,
    grad_left,
    grad_own,
    grad_right,
    loss_out,
    win,
    bias,
    rt,
    rs,
    gt,
    qs,
    bt,
):
    me = core[0]
    def gather(at, rows, source):
        win[at : at + rows, :TW] = source[:, t_at : t_at + TW]
        win[at : at + rows, TW:] = source[:, s_at : s_at + SP]

    @pl.when(me == 0)
    def _():
        gather(0, HALO, one)
        gather(HALO, BLOCK, keep)
        gather(HALO + BLOCK, BLOCK, recv)
        gather(HALO + OWN, HALO, two)

    @pl.when(me != 0)
    def _():
        gather(0, HALO, two)
        gather(HALO, BLOCK, recv)
        gather(HALO + BLOCK, BLOCK, keep)
        gather(HALO + OWN, HALO, one)

    key = lax.broadcasted_iota(jnp.int32, (WINDOW, OWN), 0)
    query = lax.broadcasted_iota(jnp.int32, (WINDOW, OWN), 1) + FIRST_QUERY
    bias[...] = jnp.where((key >= starts[...]) & (key <= query), 0.0, -1e30)

    lane = lax.broadcasted_iota(jnp.int32, (OWN, SP), 1)
    student = slice(TW, REL)
    row = lax.broadcasted_iota(jnp.int32, (SP, SP), 0)
    col = lax.broadcasted_iota(jnp.int32, (SP, SP), 1)
    unit = jnp.where(row == col, 1.0, 0.0).astype(BF16)
    bt[...] = lax.dot_general(unit, win[:, student], NT, preferred_element_type=F32).astype(BF16)

    gt[:BLOCK, :] = jnp.zeros((BLOCK, HEADS * OWN), BF16)
    gt[WINDOW - BLOCK :, :] = jnp.zeros((BLOCK, HEADS * OWN), BF16)
    total = jnp.zeros((1, BLOCK), F32)
    step = 64
    for head in range(HEADS):
        start = head * DT // 128 * 128
        inside = (lane >= head * DT - start) & (lane < (head + 1) * DT - start)
        t_cols = slice(start, start + 256)
        t_query = win[FIRST_QUERY:, t_cols] * jnp.where(inside, 1.0, 0.0).astype(BF16)
        s_start = s_off + head * DS
        inside = (lane >= s_start) & (lane < s_start + DS)
        s_query = win[FIRST_QUERY:, student] * jnp.where(inside, 1.0, 0.0).astype(BF16)
        qs[head * OWN : (head + 1) * OWN, :] = s_query
        rt[...] = (
            lax.dot_general(win[:, t_cols], t_query, NT, preferred_element_type=F32) + bias[...]
        )
        rs[...] = (
            lax.dot_general(win[:, student], s_query, NT, preferred_element_type=F32) + bias[...]
        )
        for tile in range(2):
            first = tile * BLOCK
            lanes = slice(tile * BLOCK, (tile + 1) * BLOCK)
            parts = [slice(first + at, first + at + step) for at in range(0, SPAN + BLOCK, step)]
            top_t = fold(rt[parts[0], lanes], jnp.max)
            top_s = fold(rs[parts[0], lanes], jnp.max)
            for part in parts[1:]:
                top_t = jnp.maximum(top_t, fold(rt[part, lanes], jnp.max))
                top_s = jnp.maximum(top_s, fold(rs[part, lanes], jnp.max))
            top_t = jnp.max(top_t, axis=0, keepdims=True) * CT
            top_s = jnp.max(top_s, axis=0, keepdims=True) * CS
            sum_t = jnp.zeros((8, BLOCK), F32)
            sum_s = jnp.zeros((8, BLOCK), F32)
            cross = jnp.zeros((8, BLOCK), F32)
            for part in parts:
                ut = rt[part, lanes] * CT - top_t
                us = rs[part, lanes] * CS - top_s
                et = jnp.exp2(ut)
                es = jnp.exp2(us)
                sum_t = sum_t + fold(et, jnp.sum)
                sum_s = sum_s + fold(es, jnp.sum)
                cross = cross + fold(et * (ut - us), jnp.sum)
                rt[part, lanes] = et
                rs[part, lanes] = es
            sum_t = jnp.sum(sum_t, axis=0, keepdims=True)
            sum_s = jnp.sum(sum_s, axis=0, keepdims=True)
            cross = jnp.sum(cross, axis=0, keepdims=True)
            weight = weights[:, lanes]
            total = total + weight * (cross / sum_t - jnp.log2(sum_t) + jnp.log2(sum_s))
            scale_t = weight * DS ** (-0.5) / sum_t
            scale_s = weight * DS ** (-0.5) / sum_s
            g_cols = slice(head * OWN + tile * BLOCK, head * OWN + (tile + 1) * BLOCK)
            for part in parts:
                gt[part, g_cols] = (rs[part, lanes] * scale_s - rt[part, lanes] * scale_t).astype(
                    BF16
                )

    loss_out[...] = loss_in[...] + total * math.log(2.0)
    key_grad = jnp.dot(gt[...], qs[...], preferred_element_type=F32)
    row_grads = [
        jnp.dot(
            bt[s_off + head * DS : s_off + (head + 1) * DS, :],
            gt[:, head * OWN : (head + 1) * OWN],
            preferred_element_type=F32,
        )
        for head in range(HEADS)
    ]
    row_grads.insert(HEADS if s_off == 0 else 0, jnp.zeros((SP - SW, OWN), F32))
    row_grad = jnp.concatenate(row_grads, axis=0).T
    late = HALO + OWN - FIRST_QUERY
    grad_left[...] = key_grad[:HALO].astype(BF16)
    grad_own[: OWN - late, :] = key_grad[HALO:FIRST_QUERY]
    grad_own[OWN - late :, :] = key_grad[FIRST_QUERY : HALO + OWN] + row_grad[:late]
    grad_right[...] = (key_grad[HALO + OWN :] + row_grad[late:]).astype(BF16)


def join_kernel(core, loss, l0, l1, l2, r0, r1, r2, one, two):
    def write(after, before):
        for rel, (left, right) in enumerate(((l0, r0), (l1, r1), (l2, r2))):
            before[:HALO, rel * SP : (rel + 1) * SP] = left[...]
            after[:HALO, rel * SP : (rel + 1) * SP] = right[...]

    @pl.when(core[0] == 0)
    def _():
        write(one, two)

    @pl.when(core[0] != 0)
    def _():
        write(two, one)

    row = lax.broadcasted_iota(jnp.int32, (EXTRA, BLOCK), 0)
    high = loss[...].astype(BF16).astype(F32)
    middle = (loss[...] - high).astype(BF16).astype(F32)
    low = loss[...] - high - middle
    pieces = jnp.where(row == 0, high, jnp.where(row == 1, middle, jnp.where(row == 2, low, 0.0)))
    for out in (one, two):
        out[HALO:, :BLOCK] = pieces.astype(BF16)
        out[HALO:, BLOCK:] = jnp.zeros((EXTRA, 3 * SP - BLOCK), BF16)


def merge_kernel(core, loss, o0, o1, o2, one, two, keep, send, acc):
    me = core[0]
    for rel, own in enumerate((o0, o1, o2)):
        acc[:, rel * SP : (rel + 1) * SP] = own[...]

    def add(from_before, from_after):
        acc[:HALO, :] = acc[:HALO, :] + from_before[:HALO, :].astype(F32)
        acc[OWN - HALO :, :] = acc[OWN - HALO :, :] + from_after[:HALO, :].astype(F32)
        pieces = from_after[HALO:, :BLOCK].astype(F32)
        pair = loss[...] + jnp.sum(pieces, axis=0, keepdims=True)
        for out in (keep, send):
            out[BLOCK:, :BLOCK] = jnp.broadcast_to(pair, (8, BLOCK))
            out[BLOCK:, BLOCK:] = jnp.zeros((8, 3 * SP - BLOCK), F32)

    @pl.when(me == 0)
    def _():
        add(one, two)

    @pl.when(me != 0)
    def _():
        add(two, one)

    keep[:BLOCK, :] = acc[pl.ds(pl.multiple_of(me * BLOCK, 128), BLOCK), :]
    send[:BLOCK, :] = acc[pl.ds(pl.multiple_of((1 - me) * BLOCK, 128), BLOCK), :]


def place_kernel(core, keep, recv, oq, ok, ov, copies):
    me = core[0]
    pair = keep[BLOCK : BLOCK + 1, :BLOCK] + recv[BLOCK : BLOCK + 1, :BLOCK]
    copies[...] = jnp.broadcast_to(pair, copies.shape)
    empty = jnp.zeros((BLOCK, 2 * SW - SP), F32)
    for rel, out in enumerate((oq, ok, ov)):
        ours = jnp.concatenate([keep[:BLOCK, rel * SP : (rel + 1) * SP], empty], axis=1)
        theirs = jnp.concatenate([recv[:BLOCK, rel * SP : (rel + 1) * SP], empty], axis=1)
        low = jnp.where(me == 0, ours, theirs)
        high = jnp.where(me == 0, theirs, ours)
        off = S_OFF[rel]
        if off:
            low = pltpu.roll(low, 2 * SW - off, 1)
        out[...] = low + pltpu.roll(high, SW - off, 1)


def loss_kernel(tokens, parts, loss):
    total = jnp.sum(jnp.sum(parts[...], axis=0, keepdims=True), axis=1, keepdims=True)
    loss[...] = total * (1.0 / (3 * H * tokens))


def shape(rows, cols, dtype):
    return jax.ShapeDtypeStruct((rows, cols), dtype)


def body(teacher_q, teacher_k, teacher_v, student_q, student_k, student_v, doc_ids, row_weight):
    tok = ("y", "z", "parity", "core")
    count = lax.axis_size(tok)
    core = lax.axis_index("core").astype(jnp.int32).reshape(1)
    chip = lax.axis_index(("y", "z", "parity"))

    def other_core(value):
        return lax.ppermute(value, "core", [(0, 1), (1, 0)])

    def neighbours(value, way):
        step = (2 * way, -2 * way)
        pairs = [(i, (i + step[i % 2]) % count) for i in range(count)]
        return lax.ppermute(value, tok, pairs)

    arrays = (teacher_q, teacher_k, teacher_v, student_q, student_k, student_v)
    send_a, keep_a, send_b, keep_b = call(
        split_kernel,
        [shape(BLOCK, WIDTH_A, BF16)] * 2 + [shape(BLOCK, REL, BF16)] * 2,
        [SMEM] + [HBM] * 6,
        scratch=[pltpu.VMEM(a.shape, BF16) for a in arrays] + [pltpu.SemaphoreType.DMA((6,))],
        moved=4 << 20,
        limit=56,
    )(core, *arrays)
    recv_a = other_core(send_a)
    recv_b = other_core(send_b)
    edges_a = call(edges_kernel, [shape(HALO, WIDTH_A, BF16)] * 2, [SMEM] + [VMEM] * 2, moved=2 << 20)(
        core, keep_a, recv_a
    )
    halo_a = [neighbours(edges_a[0], 1), neighbours(edges_a[1], -1)]
    edges_b = call(edges_kernel, [shape(HALO, REL, BF16)] * 2, [SMEM] + [VMEM] * 2, moved=1 << 20)(
        core, keep_b, recv_b
    )
    halo_b = [neighbours(edges_b[0], 1), neighbours(edges_b[1], -1)]

    doc_ids, row_weight, _ = lax.optimization_barrier((doc_ids, row_weight, edges_b[0]))
    far = 1 << 20
    docs = jnp.concatenate([doc_ids[-HALO:] - far, doc_ids, doc_ids[:HALO] + far])
    docs = lax.dynamic_slice_in_dim(docs, chip * OWN, WINDOW)
    weight = jnp.concatenate([row_weight, row_weight[:HALO]])
    weight = lax.dynamic_slice_in_dim(weight, chip * OWN + HALO, OWN)[None, :]
    starts = jnp.sum(docs[:, None] < docs[None, FIRST_QUERY:], axis=0, dtype=jnp.int32)[None, :]

    loss = jnp.zeros((1, BLOCK), F32)
    grads = []
    for rel in range(3):
        chunk = (keep_b, recv_b, *halo_b) if rel == 2 else (keep_a, recv_a, *halo_a)
        *grad, loss = call(
            functools.partial(relation_kernel, T_AT[rel], S_AT[rel], S_OFF[rel]),
            [
                shape(HALO, SP, BF16),
                shape(OWN, SP, F32),
                shape(HALO, SP, BF16),
                shape(1, BLOCK, F32),
            ],
            [SMEM] + [VMEM] * 7,
            scratch=[
                pltpu.VMEM((WINDOW, REL), BF16),
                pltpu.VMEM((WINDOW, OWN), F32),
                pltpu.VMEM((WINDOW, OWN), F32),
                pltpu.VMEM((WINDOW, OWN), F32),
                pltpu.VMEM((WINDOW, HEADS * OWN), BF16),
                pltpu.VMEM((HEADS * OWN, SP), BF16),
                pltpu.VMEM((SP, WINDOW), BF16),
            ],
            flops=2 * 16 * WINDOW * OWN * 256,
            moved=2 << 20,
            exps=2 * HEADS * WINDOW * OWN,
        )(core, starts, weight, loss, *chunk)
        grads.append(grad)

    one, two = call(
        join_kernel, [shape(HALO + EXTRA, 3 * SP, BF16)] * 2, [SMEM] + [VMEM] * 7, moved=1 << 20
    )(core, loss, *(g[0] for g in grads), *(g[2] for g in grads))
    one = neighbours(one, 1)
    two = neighbours(two, -1)
    kept, sent = call(
        merge_kernel,
        [shape(BLOCK + 8, 3 * SP, F32)] * 2,
        [SMEM] + [VMEM] * 6,
        scratch=[pltpu.VMEM((OWN, 3 * SP), F32)],
        moved=2 << 20,
    )(core, loss, *(g[1] for g in grads), one, two)
    received = other_core(sent)
    group = ("y", "z", "head")
    grad_q, grad_k, grad_v, parts = call(
        place_kernel,
        [shape(BLOCK, 2 * SW, F32)] * 3 + [shape(lax.axis_size(group), BLOCK, F32)],
        [SMEM] + [VMEM] * 2,
        moved=1 << 20,
    )(core, kept, received)
    parts = lax.all_to_all(parts, group, 0, 0, tiled=True)
    loss = call(
        functools.partial(loss_kernel, doc_ids.shape[0]), shape(1, 1, F32), [VMEM], moved=1 << 16
    )(parts)
    return grad_q, grad_k, grad_v, loss[0, 0]


def solution(mesh):
    tok, head = mesh.devices.shape
    z = 4 if tok == 128 else 1
    axes = ("y", "z", "parity", "core", "head")
    fine = Mesh(mesh.devices.reshape(tok // (4 * z), z, 2, 2, head), axes)
    rows = axes[:4]
    placed = (P(rows, "head"),) * 6 + (P(), P())
    return jax.shard_map(
        body,
        mesh=fine,
        in_specs=placed,
        out_specs=(P(rows, "head"),) * 3 + (P(),),
        check_vma=False,
    )
```

```python
import functools
import math

import jax
import jax.numpy as jnp
from jax import lax
from jax.experimental import pallas as pl
from jax.experimental.pallas import tpu as pltpu
from jax.sharding import Mesh
from jax.sharding import PartitionSpec as P

H = 32
DT = 160
DS = 48
SPAN = 384

BLOCK = 128
OWN = 2 * BLOCK
HALO = 192
WINDOW = OWN + 2 * HALO
FIRST_QUERY = WINDOW - OWN
HEADS = 4
TW = HEADS * DT
SW = HEADS * DS
SP = 256
REL = TW + SP
WIDTH_A = 2 * TW + 2 * SW
T_AT = (0, TW, 0)
S_AT = (2 * TW, 2 * TW + 128, TW)
S_OFF = (0, SW - 128, 0)
CT = DT ** (-0.5) * math.log2(math.e)
CS = DS ** (-0.5) * math.log2(math.e)
NT = (((1,), (1,)), ((), ()))
FAR = 4096
VMEM = pl.BlockSpec(memory_space=pltpu.VMEM)
SMEM = pl.BlockSpec(memory_space=pltpu.SMEM)
F32 = jnp.float32
BF16 = jnp.bfloat16


def call(kernel, out_shape, in_specs, scratch=(), flops=0, moved=0, exps=0, limit=8):
    return pl.pallas_call(
        kernel,
        out_shape=out_shape,
        in_specs=in_specs,
        out_specs=jax.tree.map(lambda _: VMEM, out_shape),
        scratch_shapes=list(scratch),
        compiler_params=pltpu.CompilerParams(vmem_limit_bytes=limit << 20),
        cost_estimate=pl.CostEstimate(flops=flops, bytes_accessed=moved, transcendentals=exps),
    )


def zero_kernel(loss):
    loss[...] = jnp.zeros_like(loss)


def split_kernel(core, _, tq, tk, tv, sq, sk, sv, send_a, keep_a, send_b, keep_b):
    me = core[0]
    buffers = (tq, tk, tv, sq, sk, sv)
    lane = lax.broadcasted_iota(jnp.int32, (BLOCK, SP), 1)
    mine = pl.ds(pl.multiple_of(me * TW, 128), TW)
    other = pl.ds(pl.multiple_of((1 - me) * TW, 128), TW)
    ours, theirs = [], []
    for rel in range(3):
        teacher, student = buffers[rel], buffers[3 + rel]
        keep, send, at = (keep_b, send_b, 0) if rel == 2 else (keep_a, send_a, rel * TW)
        keep[:, at : at + TW] = teacher[:, mine]
        send[:, at : at + TW] = teacher[:, other]
        low = jnp.where(lane < SW, student[:, :SP].astype(F32), 0.0)
        high = pltpu.roll(student[:, 128:].astype(F32), SP - (SW - 128), 1)
        high = jnp.where(lane < SW, high, 0.0)
        ours.append(jnp.where(me == 0, low, high))
        theirs.append(jnp.where(me == 0, high, low))
    for halves, out_a, out_b in ((ours, keep_a, keep_b), (theirs, send_a, send_b)):
        second = pltpu.roll(halves[1], S_OFF[1], 1)
        at = 2 * TW
        out_a[:, at : at + 128] = halves[0][:, :128].astype(BF16)
        out_a[:, at + 128 : at + 256] = (halves[0][:, 128:] + second[:, :128]).astype(BF16)
        out_a[:, at + 256 : at + 384] = second[:, 128:].astype(BF16)
        out_b[:, TW:] = halves[2].astype(BF16)


def mask_kernel(chip, docs, rows, starts, weights):
    count = docs.shape[0]
    first = 2 * chip[0] - 2

    def row_of(ref, r):
        at = first + r
        return ref[pl.ds(lax.rem(at + count, count), 1), :]

    lines = []
    for r in range(6):
        at = first + r
        shift = jnp.where(at < 0, -FAR, jnp.where(at >= count, FAR, 0))
        lines.append((row_of(docs, r) + shift).astype(F32))

    def queries(parts):
        joined = jnp.broadcast_to(jnp.concatenate(parts, axis=1), (8, 3 * BLOCK))
        return pltpu.roll(joined, 2 * BLOCK + 64, 1)[:1, :OWN]

    query = queries(lines[3:])
    before = jnp.zeros((1, OWN), F32)
    for line in lines:
        keys = jnp.broadcast_to(line, (BLOCK, BLOCK)).T
        keys = jnp.concatenate([keys, keys], axis=1)
        before = before + jnp.sum(jnp.where(keys < query, 1.0, 0.0), axis=0, keepdims=True)
    starts[...] = before.astype(jnp.int32) - 64
    weights[...] = queries([row_of(rows, r) for r in range(3, 6)])


def edges_kernel(core, keep, recv, one, two):
    half = HALO - BLOCK

    def write(first, second, after, before):
        after[:half, :] = first[BLOCK - half :, :]
        after[half:, :] = second[...]
        before[:BLOCK, :] = first[...]
        before[BLOCK:, :] = second[:half, :]

    @pl.when(core[0] == 0)
    def _():
        write(keep, recv, one, two)

    @pl.when(core[0] != 0)
    def _():
        write(recv, keep, two, one)


def fold(value, op):
    rows, lanes = value.shape
    return op(value.reshape(rows // 8, 8, lanes), axis=0)


def relation_kernel(
    t_at,
    s_at,
    s_off,
    core,
    starts,
    weights,
    loss_in,
    keep,
    recv,
    one,
    two,
    grad_left,
    grad_own,
    grad_right,
    loss_out,
    win,
    bias,
    rt,
    rs,
    gt,
    qs,
    bt,
    kg,
):
    me = core[0]
    def gather(at, rows, source):
        win[at : at + rows, :TW] = source[:, t_at : t_at + TW]
        win[at : at + rows, TW:] = source[:, s_at : s_at + SP]

    @pl.when(me == 0)
    def _():
        gather(0, HALO, one)
        gather(HALO, BLOCK, keep)
        gather(HALO + BLOCK, BLOCK, recv)
        gather(HALO + OWN, HALO, two)

    @pl.when(me != 0)
    def _():
        gather(0, HALO, two)
        gather(HALO, BLOCK, recv)
        gather(HALO + BLOCK, BLOCK, keep)
        gather(HALO + OWN, HALO, one)

    key = lax.broadcasted_iota(jnp.int32, (WINDOW, OWN), 0)
    query = lax.broadcasted_iota(jnp.int32, (WINDOW, OWN), 1) + FIRST_QUERY
    bias[...] = jnp.where((key >= starts[...]) & (key <= query), 0.0, -1e30)

    lane = lax.broadcasted_iota(jnp.int32, (OWN, SP), 1)
    student = slice(TW, REL)
    row = lax.broadcasted_iota(jnp.int32, (SP, SP), 0)
    col = lax.broadcasted_iota(jnp.int32, (SP, SP), 1)
    unit = jnp.where(row == col, 1.0, 0.0).astype(BF16)
    bt[...] = lax.dot_general(unit, win[:, student], NT, preferred_element_type=F32).astype(BF16)

    gt[:BLOCK, :] = jnp.zeros((BLOCK, HEADS * OWN), BF16)
    gt[WINDOW - BLOCK :, :] = jnp.zeros((BLOCK, HEADS * OWN), BF16)
    step = 64
    tiles = [
        (
            slice(tile * BLOCK, (tile + 1) * BLOCK),
            [slice(at, at + step) for at in range(tile * BLOCK, SPAN + (tile + 1) * BLOCK, step)],
        )
        for tile in range(2)
    ]
    tops, sums = {}, {}
    totals = []

    def scores(head):
        start = head * DT // 128 * 128
        inside = (lane >= head * DT - start) & (lane < (head + 1) * DT - start)
        t_cols = slice(start, start + 256)
        t_query = win[FIRST_QUERY:, t_cols] * jnp.where(inside, 1.0, 0.0).astype(BF16)
        s_start = s_off + head * DS
        inside = (lane >= s_start) & (lane < s_start + DS)
        s_query = win[FIRST_QUERY:, student] * jnp.where(inside, 1.0, 0.0).astype(BF16)
        qs[head * OWN : (head + 1) * OWN, :] = s_query
        rt[head] = (
            lax.dot_general(win[:, t_cols], t_query, NT, preferred_element_type=F32) + bias[...]
        )
        rs[head] = (
            lax.dot_general(win[:, student], s_query, NT, preferred_element_type=F32) + bias[...]
        )

    def maxima(head):
        for tile, (lanes, parts) in enumerate(tiles):
            for z, r, scale in ((0, rt, CT), (1, rs, CS)):
                top = fold(r[head, parts[0], lanes], jnp.max)
                for part in parts[1:]:
                    top = jnp.maximum(top, fold(r[head, part, lanes], jnp.max))
                tops[head, tile, z] = jnp.max(top, axis=0, keepdims=True) * scale

    def exponentials(head):
        for tile, (lanes, parts) in enumerate(tiles):
            top_t, top_s = tops[head, tile, 0], tops[head, tile, 1]
            sum_t = jnp.zeros((8, BLOCK), F32)
            sum_s = jnp.zeros((8, BLOCK), F32)
            cross = jnp.zeros((8, BLOCK), F32)
            for part in parts:
                ut = rt[head, part, lanes] * CT - top_t
                us = rs[head, part, lanes] * CS - top_s
                et = jnp.exp2(ut)
                es = jnp.exp2(us)
                sum_t = sum_t + fold(et, jnp.sum)
                sum_s = sum_s + fold(es, jnp.sum)
                cross = cross + fold(et * (ut - us), jnp.sum)
                rt[head, part, lanes] = et
                rs[head, part, lanes] = es
            sum_t = jnp.sum(sum_t, axis=0, keepdims=True)
            sum_s = jnp.sum(sum_s, axis=0, keepdims=True)
            cross = jnp.sum(cross, axis=0, keepdims=True)
            weight = weights[:, lanes]
            totals.append(weight * (cross / sum_t - jnp.log2(sum_t) + jnp.log2(sum_s)))
            sums[head, tile] = weight * DS ** (-0.5) / sum_t, weight * DS ** (-0.5) / sum_s

    def gradients(head):
        for tile, (lanes, parts) in enumerate(tiles):
            scale_t, scale_s = sums[head, tile]
            g_cols = slice(head * OWN + tile * BLOCK, head * OWN + (tile + 1) * BLOCK)
            for part in parts:
                gt[part, g_cols] = (
                    rs[head, part, lanes] * scale_s - rt[head, part, lanes] * scale_t
                ).astype(BF16)

    row_grads = []

    def products(head):
        row_grads.append(
            jnp.dot(
                bt[s_off + head * DS : s_off + (head + 1) * DS, :],
                gt[:, head * OWN : (head + 1) * OWN],
                preferred_element_type=F32,
            )
        )

    def key_product(first, last):
        return jnp.dot(
            gt[:, first * OWN : last * OWN],
            qs[first * OWN : last * OWN, :],
            preferred_element_type=F32,
        )

    scores(0)
    scores(1)
    maxima(0)
    exponentials(0)
    scores(2)
    maxima(1)
    gradients(0)
    exponentials(1)
    products(0)
    scores(3)
    maxima(2)
    gradients(1)
    exponentials(2)
    products(1)
    kg[...] = key_product(0, 2)
    maxima(3)
    gradients(2)
    exponentials(3)
    products(2)
    gradients(3)
    products(3)
    key_grad = kg[...] + key_product(2, 4)
    loss_out[...] = loss_in[...] + functools.reduce(jnp.add, totals) * math.log(2.0)
    row_grads.insert(HEADS if s_off == 0 else 0, jnp.zeros((SP - SW, OWN), F32))
    row_grad = jnp.concatenate(row_grads, axis=0).T
    late = HALO + OWN - FIRST_QUERY
    grad_left[...] = key_grad[:HALO].astype(BF16)
    grad_own[: OWN - late, :] = key_grad[HALO:FIRST_QUERY]
    grad_own[OWN - late :, :] = key_grad[FIRST_QUERY : HALO + OWN] + row_grad[:late]
    grad_right[...] = (key_grad[HALO + OWN :] + row_grad[late:]).astype(BF16)


def join_kernel(core, loss, l0, l1, l2, r0, r1, r2, one, two, copies):
    copies[...] = jnp.broadcast_to(loss[...], copies.shape)

    def write(after, before):
        for rel, (left, right) in enumerate(((l0, r0), (l1, r1), (l2, r2))):
            before[:, rel * SP : (rel + 1) * SP] = left[...]
            after[:, rel * SP : (rel + 1) * SP] = right[...]

    @pl.when(core[0] == 0)
    def _():
        write(one, two)

    @pl.when(core[0] != 0)
    def _():
        write(two, one)


def merge_kernel(core, parts, o0, o1, o2, one, two, keep, send, copies, acc):
    me = core[0]
    copies[...] = jnp.broadcast_to(jnp.sum(parts[...], axis=0, keepdims=True), copies.shape)
    for rel, own in enumerate((o0, o1, o2)):
        acc[:, rel * SP : (rel + 1) * SP] = own[...]

    def add(from_before, from_after):
        acc[:HALO, :] = acc[:HALO, :] + from_before[...].astype(F32)
        acc[OWN - HALO :, :] = acc[OWN - HALO :, :] + from_after[...].astype(F32)

    @pl.when(me == 0)
    def _():
        add(one, two)

    @pl.when(me != 0)
    def _():
        add(two, one)

    keep[...] = acc[pl.ds(pl.multiple_of(me * BLOCK, 128), BLOCK), :]
    send[...] = acc[pl.ds(pl.multiple_of((1 - me) * BLOCK, 128), BLOCK), :]


def place_kernel(tokens, core, parts, keep, recv, oq, ok, ov, loss):
    me = core[0]
    total = jnp.sum(jnp.sum(parts[...], axis=0, keepdims=True), axis=1, keepdims=True)
    loss[...] = total * (1.0 / (3 * H * tokens))
    empty = jnp.zeros((BLOCK, 2 * SW - SP), F32)
    for rel, out in enumerate((oq, ok, ov)):
        ours = jnp.concatenate([keep[:, rel * SP : (rel + 1) * SP], empty], axis=1)
        theirs = jnp.concatenate([recv[:, rel * SP : (rel + 1) * SP], empty], axis=1)
        low = jnp.where(me == 0, ours, theirs)
        high = jnp.where(me == 0, theirs, ours)
        off = S_OFF[rel]
        if off:
            low = pltpu.roll(low, 2 * SW - off, 1)
        out[...] = low + pltpu.roll(high, SW - off, 1)


def shape(rows, cols, dtype):
    return jax.ShapeDtypeStruct((rows, cols), dtype)


def call_relation(rel, core, starts, weight, loss, chunk):
    return call(
        functools.partial(relation_kernel, T_AT[rel], S_AT[rel], S_OFF[rel]),
        [
            shape(HALO, SP, BF16),
            shape(OWN, SP, F32),
            shape(HALO, SP, BF16),
            shape(1, BLOCK, F32),
        ],
        [SMEM] + [VMEM] * 7,
        scratch=[
            pltpu.VMEM((WINDOW, REL), BF16),
            pltpu.VMEM((WINDOW, OWN), F32),
            pltpu.VMEM((HEADS, WINDOW, OWN), F32),
            pltpu.VMEM((HEADS, WINDOW, OWN), F32),
            pltpu.VMEM((WINDOW, HEADS * OWN), BF16),
            pltpu.VMEM((HEADS * OWN, SP), BF16),
            pltpu.VMEM((SP, WINDOW), BF16),
            pltpu.VMEM((WINDOW, SP), F32),
        ],
        flops=2 * 16 * WINDOW * OWN * 256,
        moved=2 << 20,
        exps=2 * HEADS * WINDOW * OWN,
        limit=20,
    )(core, starts, weight, loss, *chunk)


def body(teacher_q, teacher_k, teacher_v, student_q, student_k, student_v, doc_ids, row_weight):
    tok = ("y", "z", "parity", "core")
    count = lax.axis_size(tok)
    core = lax.axis_index("core").astype(jnp.int32).reshape(1)
    chip = lax.axis_index(("y", "z", "parity"))

    def other_core(value):
        return lax.ppermute(value, "core", [(0, 1), (1, 0)])

    def neighbours(value, way):
        step = (2 * way, -2 * way)
        pairs = [(i, (i + step[i % 2]) % count) for i in range(count)]
        return lax.ppermute(value, tok, pairs)

    loss = call(zero_kernel, shape(1, BLOCK, F32), [], moved=32 << 20)()
    send_a, keep_a, send_b, keep_b = call(
        split_kernel,
        [shape(BLOCK, WIDTH_A, BF16)] * 2 + [shape(BLOCK, REL, BF16)] * 2,
        [SMEM] + [VMEM] * 7,
        moved=4 << 20,
    )(core, loss, teacher_q, teacher_k, teacher_v, student_q, student_k, student_v)
    recv_a = other_core(send_a)
    recv_b = other_core(send_b)
    edges_a = call(edges_kernel, [shape(HALO, WIDTH_A, BF16)] * 2, [SMEM] + [VMEM] * 2, moved=2 << 20)(
        core, keep_a, recv_a
    )
    halo_a = [neighbours(edges_a[0], 1), neighbours(edges_a[1], -1)]
    keep_b, recv_b, _ = lax.optimization_barrier((keep_b, recv_b, halo_a[0]))
    edges_b = call(edges_kernel, [shape(HALO, REL, BF16)] * 2, [SMEM] + [VMEM] * 2, moved=1 << 20)(
        core, keep_b, recv_b
    )
    halo_b = [neighbours(edges_b[0], 1), neighbours(edges_b[1], -1)]

    doc_ids, row_weight, _ = lax.optimization_barrier((doc_ids, row_weight, edges_a[0]))
    starts, weight = call(
        mask_kernel,
        [shape(1, OWN, jnp.int32), shape(1, OWN, F32)],
        [SMEM] + [VMEM] * 2,
        moved=1 << 17,
    )(
        chip.astype(jnp.int32).reshape(1),
        doc_ids.reshape(-1, BLOCK),
        row_weight.reshape(-1, BLOCK),
    )
    grads = []
    for rel in range(3):
        chunk = (keep_b, recv_b, *halo_b) if rel == 2 else (keep_a, recv_a, *halo_a)
        *grad, loss = call_relation(rel, core, starts, weight, loss, chunk)
        grads.append(grad)

    stages = (("z", "parity", "core"), ("y", "head"))
    copies = [shape(lax.axis_size(axes), BLOCK, F32) for axes in stages]

    def exchange(value, axes):
        return lax.all_to_all(value, axes, 0, 0, tiled=True)

    one, two, parts = call(
        join_kernel,
        [shape(HALO, 3 * SP, BF16)] * 2 + [copies[0]],
        [SMEM] + [VMEM] * 7,
        moved=1 << 20,
    )(core, loss, *(g[0] for g in grads), *(g[2] for g in grads))
    one = neighbours(one, 1)
    two = neighbours(two, -1)
    parts = exchange(parts, stages[0])
    kept, sent, parts = call(
        merge_kernel,
        [shape(BLOCK, 3 * SP, F32)] * 2 + [copies[1]],
        [SMEM] + [VMEM] * 6,
        scratch=[pltpu.VMEM((OWN, 3 * SP), F32)],
        moved=2 << 20,
    )(core, parts, *(g[1] for g in grads), one, two)
    received = other_core(sent)
    parts = exchange(parts, stages[1])
    grad_q, grad_k, grad_v, loss = call(
        functools.partial(place_kernel, doc_ids.shape[0]),
        [shape(BLOCK, 2 * SW, F32)] * 3 + [shape(1, 1, F32)],
        [SMEM] + [VMEM] * 3,
        moved=1 << 20,
    )(core, parts, kept, received)
    return grad_q, grad_k, grad_v, loss[0, 0]


def solution(mesh):
    tok, head = mesh.devices.shape
    z = 4 if tok == 128 else 1
    axes = ("y", "z", "parity", "core", "head")
    fine = Mesh(mesh.devices.reshape(tok // (4 * z), z, 2, 2, head), axes)
    rows = axes[:4]
    placed = (P(rows, "head"),) * 6 + (P(), P())
    return jax.shard_map(
        body,
        mesh=fine,
        in_specs=placed,
        out_specs=(P(rows, "head"),) * 3 + (P(),),
        check_vma=False,
    )
```

```python
import functools
import math

import jax
import jax.numpy as jnp
from jax import lax
from jax.experimental import pallas as pl
from jax.experimental.pallas import tpu as pltpu
from jax.sharding import Mesh
from jax.sharding import PartitionSpec as P

H = 32
DT = 160
DS = 48
SPAN = 384

BLOCK = 128
OWN = 2 * BLOCK
HALO = 192
WINDOW = OWN + 2 * HALO
FIRST_QUERY = WINDOW - OWN
HEADS = 4
TW = HEADS * DT
SW = HEADS * DS
SP = 256
REL = TW + SP
WIDTH_A = 2 * TW + 2 * SW
T_AT = (0, TW, 0)
S_AT = (2 * TW, 2 * TW + 128, TW)
S_OFF = (0, SW - 128, 0)
CT = DT ** (-0.5) * math.log2(math.e)
CS = DS ** (-0.5) * math.log2(math.e)
NT = (((1,), (1,)), ((), ()))
FAR = 4096
VMEM = pl.BlockSpec(memory_space=pltpu.VMEM)
SMEM = pl.BlockSpec(memory_space=pltpu.SMEM)
HBM = pl.BlockSpec(memory_space=pltpu.HBM)
F32 = jnp.float32
BF16 = jnp.bfloat16


def call(kernel, out_shape, in_specs, scratch=(), flops=0, moved=0, exps=0, limit=8):
    return pl.pallas_call(
        kernel,
        out_shape=out_shape,
        in_specs=in_specs,
        out_specs=jax.tree.map(lambda _: VMEM, out_shape),
        scratch_shapes=list(scratch),
        compiler_params=pltpu.CompilerParams(vmem_limit_bytes=limit << 20),
        cost_estimate=pl.CostEstimate(flops=flops, bytes_accessed=moved, transcendentals=exps),
    )


def split_kernel(core, *refs):
    arrays, (send_a, keep_a, send_b, keep_b), buffers, sems = (
        refs[:6],
        refs[6:10],
        refs[10:16],
        refs[16],
    )
    me = core[0]
    copies = [
        pltpu.make_async_copy(array, buffer, sems.at[i])
        for i, (array, buffer) in enumerate(zip(arrays, buffers))
    ]
    for copy in copies:
        copy.start()
    for copy in copies:
        copy.wait()
    lane = lax.broadcasted_iota(jnp.int32, (BLOCK, SP), 1)
    mine = pl.ds(pl.multiple_of(me * TW, 128), TW)
    other = pl.ds(pl.multiple_of((1 - me) * TW, 128), TW)
    ours, theirs = [], []
    for rel in range(3):
        teacher, student = buffers[rel], buffers[3 + rel]
        keep, send, at = (keep_b, send_b, 0) if rel == 2 else (keep_a, send_a, rel * TW)
        keep[:, at : at + TW] = teacher[:, mine]
        send[:, at : at + TW] = teacher[:, other]
        low = jnp.where(lane < SW, student[:, :SP].astype(F32), 0.0)
        high = pltpu.roll(student[:, 128:].astype(F32), SP - (SW - 128), 1)
        high = jnp.where(lane < SW, high, 0.0)
        ours.append(jnp.where(me == 0, low, high))
        theirs.append(jnp.where(me == 0, high, low))
    for halves, out_a, out_b in ((ours, keep_a, keep_b), (theirs, send_a, send_b)):
        second = pltpu.roll(halves[1], S_OFF[1], 1)
        at = 2 * TW
        out_a[:, at : at + 128] = halves[0][:, :128].astype(BF16)
        out_a[:, at + 128 : at + 256] = (halves[0][:, 128:] + second[:, :128]).astype(BF16)
        out_a[:, at + 256 : at + 384] = second[:, 128:].astype(BF16)
        out_b[:, TW:] = halves[2].astype(BF16)


def mask_kernel(chip, docs, rows, starts, weights):
    count = docs.shape[0]
    first = 2 * chip[0] - 2

    def row_of(ref, r):
        at = first + r
        return ref[pl.ds(lax.rem(at + count, count), 1), :]

    lines = []
    for r in range(6):
        at = first + r
        shift = jnp.where(at < 0, -FAR, jnp.where(at >= count, FAR, 0))
        lines.append((row_of(docs, r) + shift).astype(F32))

    def queries(parts):
        joined = jnp.broadcast_to(jnp.concatenate(parts, axis=1), (8, 3 * BLOCK))
        return pltpu.roll(joined, 2 * BLOCK + 64, 1)[:1, :OWN]

    query = queries(lines[3:])
    before = jnp.zeros((1, OWN), F32)
    for line in lines:
        keys = jnp.broadcast_to(line, (BLOCK, BLOCK)).T
        keys = jnp.concatenate([keys, keys], axis=1)
        before = before + jnp.sum(jnp.where(keys < query, 1.0, 0.0), axis=0, keepdims=True)
    starts[...] = before.astype(jnp.int32) - 64
    weights[...] = queries([row_of(rows, r) for r in range(3, 6)])


def edges_kernel(core, keep, recv, one, two):
    half = HALO - BLOCK

    def write(first, second, after, before):
        after[:half, :] = first[BLOCK - half :, :]
        after[half:, :] = second[...]
        before[:BLOCK, :] = first[...]
        before[BLOCK:, :] = second[:half, :]

    @pl.when(core[0] == 0)
    def _():
        write(keep, recv, one, two)

    @pl.when(core[0] != 0)
    def _():
        write(recv, keep, two, one)


def rest_kernel(core, keep, recv, one, two):
    half = HALO - BLOCK

    @pl.when(core[0] == 0)
    def _():
        one[:half, :] = keep[BLOCK - half :, :]
        one[half:, :] = recv[...]
        two[...] = recv[:half, :]

    @pl.when(core[0] != 0)
    def _():
        one[:BLOCK, :] = recv[...]
        one[BLOCK:, :] = keep[:half, :]
        two[...] = recv[BLOCK - half :, :]


def fold(value, op):
    rows, lanes = value.shape
    return op(value.reshape(rows // 8, 8, lanes), axis=0)


def relation_kernel(
    t_at,
    s_at,
    s_off,
    core,
    starts,
    weights,
    loss_in,
    *refs,
):
    keep, recv, *halo = refs[:-12]
    grad_left, grad_own, grad_right, loss_out, win, bias, rt, rs, gt, qs, bt, kg = refs[-12:]
    me = core[0]
    def gather(at, rows, source):
        win[at : at + rows, :TW] = source[:, t_at : t_at + TW]
        win[at : at + rows, TW:] = source[:, s_at : s_at + SP]

    def gather_all(*sources):
        at = 0
        for source in sources:
            gather(at, source.shape[0], source)
            at += source.shape[0]

    if len(halo) == 2:
        one, two = halo
        order = (one, keep, recv, two), (two, recv, keep, one)
    else:
        own, one, two = halo
        order = (one, keep, recv, own, two), (two, own, recv, keep, one)

    @pl.when(me == 0)
    def _():
        gather_all(*order[0])

    @pl.when(me != 0)
    def _():
        gather_all(*order[1])

    key = lax.broadcasted_iota(jnp.int32, (WINDOW, OWN), 0)
    query = lax.broadcasted_iota(jnp.int32, (WINDOW, OWN), 1) + FIRST_QUERY
    bias[...] = jnp.where((key >= starts[...]) & (key <= query), 0.0, -1e30)

    lane = lax.broadcasted_iota(jnp.int32, (OWN, SP), 1)
    student = slice(TW, REL)
    row = lax.broadcasted_iota(jnp.int32, (SP, SP), 0)
    col = lax.broadcasted_iota(jnp.int32, (SP, SP), 1)
    unit = jnp.where(row == col, 1.0, 0.0).astype(BF16)
    bt[...] = lax.dot_general(unit, win[:, student], NT, preferred_element_type=F32).astype(BF16)

    gt[:BLOCK, :] = jnp.zeros((BLOCK, HEADS * OWN), BF16)
    gt[WINDOW - BLOCK :, :] = jnp.zeros((BLOCK, HEADS * OWN), BF16)
    step = 64
    tiles = [
        (
            slice(tile * BLOCK, (tile + 1) * BLOCK),
            [slice(at, at + step) for at in range(tile * BLOCK, SPAN + (tile + 1) * BLOCK, step)],
        )
        for tile in range(2)
    ]
    tops, sums = {}, {}
    totals = []

    def scores(head):
        start = head * DT // 128 * 128
        inside = (lane >= head * DT - start) & (lane < (head + 1) * DT - start)
        t_cols = slice(start, start + 256)
        t_query = win[FIRST_QUERY:, t_cols] * jnp.where(inside, 1.0, 0.0).astype(BF16)
        s_start = s_off + head * DS
        inside = (lane >= s_start) & (lane < s_start + DS)
        s_query = win[FIRST_QUERY:, student] * jnp.where(inside, 1.0, 0.0).astype(BF16)
        qs[head * OWN : (head + 1) * OWN, :] = s_query
        rt[head] = (
            lax.dot_general(win[:, t_cols], t_query, NT, preferred_element_type=F32) + bias[...]
        )
        rs[head] = (
            lax.dot_general(win[:, student], s_query, NT, preferred_element_type=F32) + bias[...]
        )

    def maxima(head):
        for tile, (lanes, parts) in enumerate(tiles):
            for z, r, scale in ((0, rt, CT), (1, rs, CS)):
                top = fold(r[head, parts[0], lanes], jnp.max)
                for part in parts[1:]:
                    top = jnp.maximum(top, fold(r[head, part, lanes], jnp.max))
                tops[head, tile, z] = jnp.max(top, axis=0, keepdims=True) * scale

    def exponentials(head):
        for tile, (lanes, parts) in enumerate(tiles):
            top_t, top_s = tops[head, tile, 0], tops[head, tile, 1]
            sum_t = jnp.zeros((8, BLOCK), F32)
            sum_s = jnp.zeros((8, BLOCK), F32)
            cross = jnp.zeros((8, BLOCK), F32)
            for part in parts:
                ut = rt[head, part, lanes] * CT - top_t
                us = rs[head, part, lanes] * CS - top_s
                et = jnp.exp2(ut)
                es = jnp.exp2(us)
                sum_t = sum_t + fold(et, jnp.sum)
                sum_s = sum_s + fold(es, jnp.sum)
                cross = cross + fold(et * (ut - us), jnp.sum)
                rt[head, part, lanes] = et
                rs[head, part, lanes] = es
            sum_t = jnp.sum(sum_t, axis=0, keepdims=True)
            sum_s = jnp.sum(sum_s, axis=0, keepdims=True)
            cross = jnp.sum(cross, axis=0, keepdims=True)
            weight = weights[:, lanes]
            totals.append(weight * (cross / sum_t - jnp.log2(sum_t) + jnp.log2(sum_s)))
            sums[head, tile] = weight * DS ** (-0.5) / sum_t, weight * DS ** (-0.5) / sum_s

    def gradients(head):
        for tile, (lanes, parts) in enumerate(tiles):
            scale_t, scale_s = sums[head, tile]
            g_cols = slice(head * OWN + tile * BLOCK, head * OWN + (tile + 1) * BLOCK)
            for part in parts:
                gt[part, g_cols] = (
                    rs[head, part, lanes] * scale_s - rt[head, part, lanes] * scale_t
                ).astype(BF16)

    row_grads = []

    def products(head):
        row_grads.append(
            jnp.dot(
                bt[s_off + head * DS : s_off + (head + 1) * DS, :],
                gt[:, head * OWN : (head + 1) * OWN],
                preferred_element_type=F32,
            )
        )

    def key_product(first, last):
        return jnp.dot(
            gt[:, first * OWN : last * OWN],
            qs[first * OWN : last * OWN, :],
            preferred_element_type=F32,
        )

    scores(0)
    scores(1)
    maxima(0)
    exponentials(0)
    scores(2)
    maxima(1)
    gradients(0)
    exponentials(1)
    products(0)
    scores(3)
    maxima(2)
    gradients(1)
    exponentials(2)
    products(1)
    kg[...] = key_product(0, 2)
    maxima(3)
    gradients(2)
    exponentials(3)
    products(2)
    gradients(3)
    products(3)
    key_grad = kg[...] + key_product(2, 4)
    loss_out[...] = loss_in[...] + functools.reduce(jnp.add, totals) * math.log(2.0)
    row_grads.insert(HEADS if s_off == 0 else 0, jnp.zeros((SP - SW, OWN), F32))
    row_grad = jnp.concatenate(row_grads, axis=0).T
    late = HALO + OWN - FIRST_QUERY
    grad_left[...] = key_grad[:HALO].astype(BF16)
    grad_own[: OWN - late, :] = key_grad[HALO:FIRST_QUERY]
    grad_own[OWN - late :, :] = key_grad[FIRST_QUERY : HALO + OWN] + row_grad[:late]
    grad_right[...] = (key_grad[HALO + OWN :] + row_grad[late:]).astype(BF16)


def join_kernel(core, loss, l0, l1, l2, r0, r1, r2, one, two, copies):
    copies[...] = jnp.broadcast_to(loss[...], copies.shape)

    def write(after, before):
        for rel, (left, right) in enumerate(((l0, r0), (l1, r1), (l2, r2))):
            before[:, rel * SP : (rel + 1) * SP] = left[...]
            after[:, rel * SP : (rel + 1) * SP] = right[...]

    @pl.when(core[0] == 0)
    def _():
        write(one, two)

    @pl.when(core[0] != 0)
    def _():
        write(two, one)


def merge_kernel(core, parts, o0, o1, o2, one, two, keep, send, copies, acc):
    me = core[0]
    copies[...] = jnp.broadcast_to(jnp.sum(parts[...], axis=0, keepdims=True), copies.shape)
    for rel, own in enumerate((o0, o1, o2)):
        acc[:, rel * SP : (rel + 1) * SP] = own[...]

    def add(from_before, from_after):
        acc[:HALO, :] = acc[:HALO, :] + from_before[...].astype(F32)
        acc[OWN - HALO :, :] = acc[OWN - HALO :, :] + from_after[...].astype(F32)

    @pl.when(me == 0)
    def _():
        add(one, two)

    @pl.when(me != 0)
    def _():
        add(two, one)

    keep[...] = acc[pl.ds(pl.multiple_of(me * BLOCK, 128), BLOCK), :]
    send[...] = acc[pl.ds(pl.multiple_of((1 - me) * BLOCK, 128), BLOCK), :]


def place_kernel(tokens, core, parts, keep, recv, oq, ok, ov, loss):
    me = core[0]
    total = jnp.sum(jnp.sum(parts[...], axis=0, keepdims=True), axis=1, keepdims=True)
    loss[...] = total * (1.0 / (3 * H * tokens))
    empty = jnp.zeros((BLOCK, 2 * SW - SP), F32)
    for rel, out in enumerate((oq, ok, ov)):
        ours = jnp.concatenate([keep[:, rel * SP : (rel + 1) * SP], empty], axis=1)
        theirs = jnp.concatenate([recv[:, rel * SP : (rel + 1) * SP], empty], axis=1)
        low = jnp.where(me == 0, ours, theirs)
        high = jnp.where(me == 0, theirs, ours)
        off = S_OFF[rel]
        if off:
            low = pltpu.roll(low, 2 * SW - off, 1)
        out[...] = low + pltpu.roll(high, SW - off, 1)


def shape(rows, cols, dtype):
    return jax.ShapeDtypeStruct((rows, cols), dtype)


def call_relation(rel, core, starts, weight, loss, chunk):
    return call(
        functools.partial(relation_kernel, T_AT[rel], S_AT[rel], S_OFF[rel]),
        [
            shape(HALO, SP, BF16),
            shape(OWN, SP, F32),
            shape(HALO, SP, BF16),
            shape(1, BLOCK, F32),
        ],
        [SMEM] + [VMEM] * (3 + len(chunk)),
        scratch=[
            pltpu.VMEM((WINDOW, REL), BF16),
            pltpu.VMEM((WINDOW, OWN), F32),
            pltpu.VMEM((HEADS, WINDOW, OWN), F32),
            pltpu.VMEM((HEADS, WINDOW, OWN), F32),
            pltpu.VMEM((WINDOW, HEADS * OWN), BF16),
            pltpu.VMEM((HEADS * OWN, SP), BF16),
            pltpu.VMEM((SP, WINDOW), BF16),
            pltpu.VMEM((WINDOW, SP), F32),
        ],
        flops=2 * 16 * WINDOW * OWN * 256,
        moved=2 << 20,
        exps=2 * HEADS * WINDOW * OWN,
        limit=20,
    )(core, starts, weight, loss, *chunk)


def body(teacher_q, teacher_k, teacher_v, student_q, student_k, student_v, doc_ids, row_weight):
    tok = ("y", "z", "parity", "core")
    count = lax.axis_size(tok)
    core = lax.axis_index("core").astype(jnp.int32).reshape(1)
    chip = lax.axis_index(("y", "z", "parity"))

    def other_core(value):
        return lax.ppermute(value, "core", [(0, 1), (1, 0)])

    def neighbours(value, way):
        step = (2 * way, -2 * way)
        pairs = [(i, (i + step[i % 2]) % count) for i in range(count)]
        return lax.ppermute(value, tok, pairs)

    arrays = (teacher_q, teacher_k, teacher_v, student_q, student_k, student_v)
    send_a, keep_a, send_b, keep_b = call(
        split_kernel,
        [shape(BLOCK, WIDTH_A, BF16)] * 2 + [shape(BLOCK, REL, BF16)] * 2,
        [SMEM] + [HBM] * 6,
        scratch=[pltpu.VMEM(a.shape, BF16) for a in arrays] + [pltpu.SemaphoreType.DMA((6,))],
        moved=4 << 20,
        limit=56,
    )(core, *arrays)
    recv_a = other_core(send_a)
    recv_b = other_core(send_b)
    own_a = neighbours(keep_a, -1)
    recv_a, recv_b, own_a = lax.optimization_barrier((recv_a, recv_b, own_a))
    halo_a = [own_a]
    rest_a = call(
        rest_kernel,
        [shape(HALO, WIDTH_A, BF16), shape(HALO - BLOCK, WIDTH_A, BF16)],
        [SMEM] + [VMEM] * 2,
        moved=2 << 20,
    )(core, keep_a, recv_a)
    halo_a += [neighbours(rest_a[0], 1), neighbours(rest_a[1], -1)]
    edges_b = call(edges_kernel, [shape(HALO, REL, BF16)] * 2, [SMEM] + [VMEM] * 2, moved=1 << 20)(
        core, keep_b, recv_b
    )
    halo_b = [neighbours(edges_b[0], 1), neighbours(edges_b[1], -1)]

    doc_ids, row_weight, _ = lax.optimization_barrier((doc_ids, row_weight, rest_a[0]))
    starts, weight = call(
        mask_kernel,
        [shape(1, OWN, jnp.int32), shape(1, OWN, F32)],
        [SMEM] + [VMEM] * 2,
        moved=1 << 17,
    )(
        chip.astype(jnp.int32).reshape(1),
        doc_ids.reshape(-1, BLOCK),
        row_weight.reshape(-1, BLOCK),
    )
    loss = jnp.zeros((1, BLOCK), F32)
    grads = []
    for rel in range(3):
        chunk = (keep_b, recv_b, *halo_b) if rel == 2 else (keep_a, recv_a, *halo_a)
        *grad, loss = call_relation(rel, core, starts, weight, loss, chunk)
        grads.append(grad)

    stages = (("z", "parity", "core"), ("y", "head"))
    copies = [shape(lax.axis_size(axes), BLOCK, F32) for axes in stages]

    def exchange(value, axes):
        return lax.all_to_all(value, axes, 0, 0, tiled=True)

    one, two, parts = call(
        join_kernel,
        [shape(HALO, 3 * SP, BF16)] * 2 + [copies[0]],
        [SMEM] + [VMEM] * 7,
        moved=1 << 20,
    )(core, loss, *(g[0] for g in grads), *(g[2] for g in grads))
    one = neighbours(one, 1)
    two = neighbours(two, -1)
    parts = exchange(parts, stages[0])
    kept, sent, parts = call(
        merge_kernel,
        [shape(BLOCK, 3 * SP, F32)] * 2 + [copies[1]],
        [SMEM] + [VMEM] * 6,
        scratch=[pltpu.VMEM((OWN, 3 * SP), F32)],
        moved=2 << 20,
    )(core, parts, *(g[1] for g in grads), one, two)
    received = other_core(sent)
    parts = exchange(parts, stages[1])
    grad_q, grad_k, grad_v, loss = call(
        functools.partial(place_kernel, doc_ids.shape[0]),
        [shape(BLOCK, 2 * SW, F32)] * 3 + [shape(1, 1, F32)],
        [SMEM] + [VMEM] * 3,
        moved=1 << 20,
    )(core, parts, kept, received)
    return grad_q, grad_k, grad_v, loss[0, 0]


def solution(mesh):
    tok, head = mesh.devices.shape
    z = 4 if tok == 128 else 1
    axes = ("y", "z", "parity", "core", "head")
    fine = Mesh(mesh.devices.reshape(tok // (4 * z), z, 2, 2, head), axes)
    rows = axes[:4]
    placed = (P(rows, "head"),) * 6 + (P(), P())
    return jax.shard_map(
        body,
        mesh=fine,
        in_specs=placed,
        out_specs=(P(rows, "head"),) * 3 + (P(),),
        check_vma=False,
    )
```

```python
import functools
import math

import jax
import jax.numpy as jnp
from jax import lax
from jax.experimental import pallas as pl
from jax.experimental.pallas import tpu as pltpu
from jax.sharding import Mesh
from jax.sharding import PartitionSpec as P

H = 32
DT = 160
DS = 48
SPAN = 384

BLOCK = 128
OWN = 2 * BLOCK
HALO = 192
WINDOW = OWN + 2 * HALO
FIRST_QUERY = WINDOW - OWN
HEADS = 4
TW = HEADS * DT
SW = HEADS * DS
SP = 256
REL = TW + SP
WIDTH_A = 2 * TW + 2 * SW
T_AT = (0, TW, 0)
S_AT = (2 * TW, 2 * TW + 128, TW)
S_OFF = (0, SW - 128, 0)
CT = DT ** (-0.5) * math.log2(math.e)
CS = DS ** (-0.5) * math.log2(math.e)
NT = (((1,), (1,)), ((), ()))
FAR = 4096
VMEM = pl.BlockSpec(memory_space=pltpu.VMEM)
SMEM = pl.BlockSpec(memory_space=pltpu.SMEM)
HBM = pl.BlockSpec(memory_space=pltpu.HBM)
F32 = jnp.float32
BF16 = jnp.bfloat16


def call(kernel, out_shape, in_specs, scratch=(), flops=0, moved=0, exps=0, limit=8):
    return pl.pallas_call(
        kernel,
        out_shape=out_shape,
        in_specs=in_specs,
        out_specs=jax.tree.map(lambda _: VMEM, out_shape),
        scratch_shapes=list(scratch),
        compiler_params=pltpu.CompilerParams(vmem_limit_bytes=limit << 20),
        cost_estimate=pl.CostEstimate(flops=flops, bytes_accessed=moved, transcendentals=exps),
    )


def split_kernel(core, *refs):
    arrays, (send_a, keep_a, send_b, keep_b), buffers, sems = (
        refs[:6],
        refs[6:10],
        refs[10:16],
        refs[16],
    )
    me = core[0]
    copies = [
        pltpu.make_async_copy(array, buffer, sems.at[i])
        for i, (array, buffer) in enumerate(zip(arrays, buffers))
    ]
    for copy in copies:
        copy.start()
    for copy in copies:
        copy.wait()
    lane = lax.broadcasted_iota(jnp.int32, (BLOCK, SP), 1)
    mine = pl.ds(pl.multiple_of(me * TW, 128), TW)
    other = pl.ds(pl.multiple_of((1 - me) * TW, 128), TW)
    ours, theirs = [], []
    for rel in range(3):
        teacher, student = buffers[rel], buffers[3 + rel]
        keep, send, at = (keep_b, send_b, 0) if rel == 2 else (keep_a, send_a, rel * TW)
        keep[:, at : at + TW] = teacher[:, mine]
        send[:, at : at + TW] = teacher[:, other]
        low = jnp.where(lane < SW, student[:, :SP].astype(F32), 0.0)
        high = pltpu.roll(student[:, 128:].astype(F32), SP - (SW - 128), 1)
        high = jnp.where(lane < SW, high, 0.0)
        ours.append(jnp.where(me == 0, low, high))
        theirs.append(jnp.where(me == 0, high, low))
    for halves, out_a, out_b in ((ours, keep_a, keep_b), (theirs, send_a, send_b)):
        second = pltpu.roll(halves[1], S_OFF[1], 1)
        at = 2 * TW
        out_a[:, at : at + 128] = halves[0][:, :128].astype(BF16)
        out_a[:, at + 128 : at + 256] = (halves[0][:, 128:] + second[:, :128]).astype(BF16)
        out_a[:, at + 256 : at + 384] = second[:, 128:].astype(BF16)
        out_b[:, TW:] = halves[2].astype(BF16)


def mask_kernel(chip, docs, rows, starts, weights):
    count = docs.shape[0]
    first = 2 * chip[0] - 2

    def row_of(ref, r):
        at = first + r
        return ref[pl.ds(lax.rem(at + count, count), 1), :]

    lines = []
    for r in range(6):
        at = first + r
        shift = jnp.where(at < 0, -FAR, jnp.where(at >= count, FAR, 0))
        lines.append((row_of(docs, r) + shift).astype(F32))

    def queries(parts):
        joined = jnp.broadcast_to(jnp.concatenate(parts, axis=1), (8, 3 * BLOCK))
        return pltpu.roll(joined, 2 * BLOCK + 64, 1)[:1, :OWN]

    query = queries(lines[3:])
    before = jnp.zeros((1, OWN), F32)
    for line in lines:
        keys = jnp.broadcast_to(line, (BLOCK, BLOCK)).T
        keys = jnp.concatenate([keys, keys], axis=1)
        before = before + jnp.sum(jnp.where(keys < query, 1.0, 0.0), axis=0, keepdims=True)
    starts[...] = before.astype(jnp.int32) - 64
    weights[...] = queries([row_of(rows, r) for r in range(3, 6)])


def edges_kernel(core, keep, recv, one, two):
    half = HALO - BLOCK

    def write(first, second, after, before):
        after[:half, :] = first[BLOCK - half :, :]
        after[half:, :] = second[...]
        before[:BLOCK, :] = first[...]
        before[BLOCK:, :] = second[:half, :]

    @pl.when(core[0] == 0)
    def _():
        write(keep, recv, one, two)

    @pl.when(core[0] != 0)
    def _():
        write(recv, keep, two, one)


def edges(core, keep, recv):
    out = [shape(HALO, keep.shape[1], BF16)] * 2
    return call(edges_kernel, out, [SMEM] + [VMEM] * 2, moved=2 << 20)(core, keep, recv)


def fold(value, op):
    rows, lanes = value.shape
    return op(value.reshape(rows // 8, 8, lanes), axis=0)


def relation_kernel(
    t_at,
    s_at,
    s_off,
    flipped,
    core,
    starts,
    weights,
    loss_in,
    *refs,
):
    keep, recv, one, two = refs[:-12]
    if flipped:
        one, two = two, one
    grad_left, grad_own, grad_right, loss_out, win, bias, rt, rs, gt, qs, bt, kg = refs[-12:]
    me = core[0]
    def gather(at, rows, source):
        win[at : at + rows, :TW] = source[:, t_at : t_at + TW]
        win[at : at + rows, TW:] = source[:, s_at : s_at + SP]

    def gather_all(*sources):
        at = 0
        for source in sources:
            gather(at, source.shape[0], source)
            at += source.shape[0]

    @pl.when(me == 0)
    def _():
        gather_all(one, keep, recv, two)

    @pl.when(me != 0)
    def _():
        gather_all(two, recv, keep, one)

    key = lax.broadcasted_iota(jnp.int32, (WINDOW, OWN), 0)
    query = lax.broadcasted_iota(jnp.int32, (WINDOW, OWN), 1) + FIRST_QUERY
    bias[...] = jnp.where((key >= starts[...]) & (key <= query), 0.0, -1e30)

    lane = lax.broadcasted_iota(jnp.int32, (OWN, SP), 1)
    student = slice(TW, REL)
    row = lax.broadcasted_iota(jnp.int32, (SP, SP), 0)
    col = lax.broadcasted_iota(jnp.int32, (SP, SP), 1)
    unit = jnp.where(row == col, 1.0, 0.0).astype(BF16)
    bt[...] = lax.dot_general(unit, win[:, student], NT, preferred_element_type=F32).astype(BF16)

    gt[:BLOCK, :] = jnp.zeros((BLOCK, HEADS * OWN), BF16)
    gt[WINDOW - BLOCK :, :] = jnp.zeros((BLOCK, HEADS * OWN), BF16)
    step = 64
    tiles = [
        (
            slice(tile * BLOCK, (tile + 1) * BLOCK),
            [slice(at, at + step) for at in range(tile * BLOCK, SPAN + (tile + 1) * BLOCK, step)],
        )
        for tile in range(2)
    ]
    tops, sums = {}, {}
    totals = []

    def scores(head):
        start = head * DT // 128 * 128
        inside = (lane >= head * DT - start) & (lane < (head + 1) * DT - start)
        t_cols = slice(start, start + 256)
        t_query = win[FIRST_QUERY:, t_cols] * jnp.where(inside, 1.0, 0.0).astype(BF16)
        s_start = s_off + head * DS
        inside = (lane >= s_start) & (lane < s_start + DS)
        s_query = win[FIRST_QUERY:, student] * jnp.where(inside, 1.0, 0.0).astype(BF16)
        qs[head * OWN : (head + 1) * OWN, :] = s_query
        rt[head] = (
            lax.dot_general(win[:, t_cols], t_query, NT, preferred_element_type=F32) + bias[...]
        )
        rs[head] = (
            lax.dot_general(win[:, student], s_query, NT, preferred_element_type=F32) + bias[...]
        )

    def maxima(head):
        for tile, (lanes, parts) in enumerate(tiles):
            for z, r, scale in ((0, rt, CT), (1, rs, CS)):
                top = fold(r[head, parts[0], lanes], jnp.max)
                for part in parts[1:]:
                    top = jnp.maximum(top, fold(r[head, part, lanes], jnp.max))
                tops[head, tile, z] = jnp.max(top, axis=0, keepdims=True) * scale

    def exponentials(head):
        for tile, (lanes, parts) in enumerate(tiles):
            top_t, top_s = tops[head, tile, 0], tops[head, tile, 1]
            sum_t = jnp.zeros((8, BLOCK), F32)
            sum_s = jnp.zeros((8, BLOCK), F32)
            cross = jnp.zeros((8, BLOCK), F32)
            for part in parts:
                ut = rt[head, part, lanes] * CT - top_t
                us = rs[head, part, lanes] * CS - top_s
                et = jnp.exp2(ut)
                es = jnp.exp2(us)
                sum_t = sum_t + fold(et, jnp.sum)
                sum_s = sum_s + fold(es, jnp.sum)
                cross = cross + fold(et * (ut - us), jnp.sum)
                rt[head, part, lanes] = et
                rs[head, part, lanes] = es
            sum_t = jnp.sum(sum_t, axis=0, keepdims=True)
            sum_s = jnp.sum(sum_s, axis=0, keepdims=True)
            cross = jnp.sum(cross, axis=0, keepdims=True)
            weight = weights[:, lanes]
            totals.append(weight * (cross / sum_t - jnp.log2(sum_t) + jnp.log2(sum_s)))
            sums[head, tile] = weight * DS ** (-0.5) / sum_t, weight * DS ** (-0.5) / sum_s

    def gradients(head):
        for tile, (lanes, parts) in enumerate(tiles):
            scale_t, scale_s = sums[head, tile]
            g_cols = slice(head * OWN + tile * BLOCK, head * OWN + (tile + 1) * BLOCK)
            for part in parts:
                gt[part, g_cols] = (
                    rs[head, part, lanes] * scale_s - rt[head, part, lanes] * scale_t
                ).astype(BF16)

    row_grads = []

    def products(head):
        row_grads.append(
            jnp.dot(
                bt[s_off + head * DS : s_off + (head + 1) * DS, :],
                gt[:, head * OWN : (head + 1) * OWN],
                preferred_element_type=F32,
            )
        )

    def key_product(first, last):
        return jnp.dot(
            gt[:, first * OWN : last * OWN],
            qs[first * OWN : last * OWN, :],
            preferred_element_type=F32,
        )

    scores(0)
    scores(1)
    maxima(0)
    exponentials(0)
    scores(2)
    maxima(1)
    gradients(0)
    exponentials(1)
    products(0)
    scores(3)
    maxima(2)
    gradients(1)
    exponentials(2)
    products(1)
    kg[...] = key_product(0, 2)
    maxima(3)
    gradients(2)
    exponentials(3)
    products(2)
    gradients(3)
    products(3)
    key_grad = kg[...] + key_product(2, 4)
    loss_out[...] = loss_in[...] + functools.reduce(jnp.add, totals) * math.log(2.0)
    row_grads.insert(HEADS if s_off == 0 else 0, jnp.zeros((SP - SW, OWN), F32))
    row_grad = jnp.concatenate(row_grads, axis=0).T
    late = HALO + OWN - FIRST_QUERY
    grad_left[...] = key_grad[:HALO].astype(BF16)
    grad_own[: OWN - late, :] = key_grad[HALO:FIRST_QUERY]
    grad_own[OWN - late :, :] = key_grad[FIRST_QUERY : HALO + OWN] + row_grad[:late]
    grad_right[...] = (key_grad[HALO + OWN :] + row_grad[late:]).astype(BF16)


def join_kernel(core, loss, l0, l1, l2, r0, r1, r2, one, two, copies):
    copies[...] = jnp.broadcast_to(loss[...], copies.shape)

    def write(after, before):
        for rel, (left, right) in enumerate(((l0, r0), (l1, r1), (l2, r2))):
            before[:, rel * SP : (rel + 1) * SP] = left[...]
            after[:, rel * SP : (rel + 1) * SP] = right[...]

    @pl.when(core[0] == 0)
    def _():
        write(one, two)

    @pl.when(core[0] != 0)
    def _():
        write(two, one)


def merge_kernel(core, parts, o0, o1, o2, one, two, keep, send, copies, acc):
    me = core[0]
    copies[...] = jnp.broadcast_to(jnp.sum(parts[...], axis=0, keepdims=True), copies.shape)
    for rel, own in enumerate((o0, o1, o2)):
        acc[:, rel * SP : (rel + 1) * SP] = own[...]

    def add(from_before, from_after):
        acc[:HALO, :] = acc[:HALO, :] + from_before[...].astype(F32)
        acc[OWN - HALO :, :] = acc[OWN - HALO :, :] + from_after[...].astype(F32)

    @pl.when(me == 0)
    def _():
        add(one, two)

    @pl.when(me != 0)
    def _():
        add(two, one)

    keep[...] = acc[pl.ds(pl.multiple_of(me * BLOCK, 128), BLOCK), :]
    send[...] = acc[pl.ds(pl.multiple_of((1 - me) * BLOCK, 128), BLOCK), :]


def place_kernel(tokens, core, parts, keep, recv, oq, ok, ov, loss):
    me = core[0]
    total = jnp.sum(jnp.sum(parts[...], axis=0, keepdims=True), axis=1, keepdims=True)
    loss[...] = total * (1.0 / (3 * H * tokens))
    empty = jnp.zeros((BLOCK, 2 * SW - SP), F32)
    for rel, out in enumerate((oq, ok, ov)):
        ours = jnp.concatenate([keep[:, rel * SP : (rel + 1) * SP], empty], axis=1)
        theirs = jnp.concatenate([recv[:, rel * SP : (rel + 1) * SP], empty], axis=1)
        low = jnp.where(me == 0, ours, theirs)
        high = jnp.where(me == 0, theirs, ours)
        off = S_OFF[rel]
        if off:
            low = pltpu.roll(low, 2 * SW - off, 1)
        out[...] = low + pltpu.roll(high, SW - off, 1)


def shape(rows, cols, dtype):
    return jax.ShapeDtypeStruct((rows, cols), dtype)


def call_relation(rel, core, starts, weight, loss, chunk):
    return call(
        functools.partial(relation_kernel, T_AT[rel], S_AT[rel], S_OFF[rel], rel == 2),
        [
            shape(HALO, SP, BF16),
            shape(OWN, SP, F32),
            shape(HALO, SP, BF16),
            shape(1, BLOCK, F32),
        ],
        [SMEM] + [VMEM] * (3 + len(chunk)),
        scratch=[
            pltpu.VMEM((WINDOW, REL), BF16),
            pltpu.VMEM((WINDOW, OWN), F32),
            pltpu.VMEM((HEADS, WINDOW, OWN), F32),
            pltpu.VMEM((HEADS, WINDOW, OWN), F32),
            pltpu.VMEM((WINDOW, HEADS * OWN), BF16),
            pltpu.VMEM((HEADS * OWN, SP), BF16),
            pltpu.VMEM((SP, WINDOW), BF16),
            pltpu.VMEM((WINDOW, SP), F32),
        ],
        flops=2 * 16 * WINDOW * OWN * 256,
        moved=2 << 20,
        exps=2 * HEADS * WINDOW * OWN,
        limit=20,
    )(core, starts, weight, loss, *chunk)


def body(teacher_q, teacher_k, teacher_v, student_q, student_k, student_v, doc_ids, row_weight):
    tok = ("y", "z", "parity", "core")
    count = lax.axis_size(tok)
    core = lax.axis_index("core").astype(jnp.int32).reshape(1)
    chip = lax.axis_index(("y", "z", "parity"))

    def other_core(value):
        return lax.ppermute(value, "core", [(0, 1), (1, 0)])

    def neighbours(value, way):
        step = (2 * way, -2 * way)
        pairs = [(i, (i + step[i % 2]) % count) for i in range(count)]
        return lax.ppermute(value, tok, pairs)

    arrays = (teacher_q, teacher_k, teacher_v, student_q, student_k, student_v)
    send_a, keep_a, send_b, keep_b = call(
        split_kernel,
        [shape(BLOCK, WIDTH_A, BF16)] * 2 + [shape(BLOCK, REL, BF16)] * 2,
        [SMEM] + [HBM] * 6,
        scratch=[pltpu.VMEM(a.shape, BF16) for a in arrays] + [pltpu.SemaphoreType.DMA((6,))],
        moved=4 << 20,
        limit=56,
    )(core, *arrays)
    recv_a = other_core(send_a)
    recv_b = other_core(send_b)
    edges_a = edges(core, keep_a, recv_a)
    halo_a = [neighbours(edges_a[0], 1), neighbours(edges_a[1], -1)]
    edges_b = edges(core, keep_b, recv_b)
    halo_b = [neighbours(edges_b[1], -1), neighbours(edges_b[0], 1)]

    doc_ids, row_weight, _ = lax.optimization_barrier((doc_ids, row_weight, edges_a[0]))
    starts, weight = call(
        mask_kernel,
        [shape(1, OWN, jnp.int32), shape(1, OWN, F32)],
        [SMEM] + [VMEM] * 2,
        moved=1 << 17,
    )(
        chip.astype(jnp.int32).reshape(1),
        doc_ids.reshape(-1, BLOCK),
        row_weight.reshape(-1, BLOCK),
    )
    loss = jnp.zeros((1, BLOCK), F32)
    grads = []
    for rel in range(3):
        chunk = (keep_b, recv_b, *halo_b) if rel == 2 else (keep_a, recv_a, *halo_a)
        *grad, loss = call_relation(rel, core, starts, weight, loss, chunk)
        grads.append(grad)

    stages = (("z", "parity", "core"), ("y", "head"))
    copies = [shape(lax.axis_size(axes), BLOCK, F32) for axes in stages]

    def exchange(value, axes):
        return lax.all_to_all(value, axes, 0, 0, tiled=True)

    one, two, parts = call(
        join_kernel,
        [shape(HALO, 3 * SP, BF16)] * 2 + [copies[0]],
        [SMEM] + [VMEM] * 7,
        moved=1 << 20,
    )(core, loss, *(g[0] for g in grads), *(g[2] for g in grads))
    one = neighbours(one, 1)
    two = neighbours(two, -1)
    parts = exchange(parts, stages[0])
    kept, sent, parts = call(
        merge_kernel,
        [shape(BLOCK, 3 * SP, F32)] * 2 + [copies[1]],
        [SMEM] + [VMEM] * 6,
        scratch=[pltpu.VMEM((OWN, 3 * SP), F32)],
        moved=2 << 20,
    )(core, parts, *(g[1] for g in grads), one, two)
    received = other_core(sent)
    parts = exchange(parts, stages[1])
    grad_q, grad_k, grad_v, loss = call(
        functools.partial(place_kernel, doc_ids.shape[0]),
        [shape(BLOCK, 2 * SW, F32)] * 3 + [shape(1, 1, F32)],
        [SMEM] + [VMEM] * 3,
        moved=1 << 20,
    )(core, parts, kept, received)
    return grad_q, grad_k, grad_v, loss[0, 0]


def solution(mesh):
    tok, head = mesh.devices.shape
    z = 4 if tok == 128 else 1
    axes = ("y", "z", "parity", "core", "head")
    fine = Mesh(mesh.devices.reshape(tok // (4 * z), z, 2, 2, head), axes)
    rows = axes[:4]
    placed = (P(rows, "head"),) * 6 + (P(), P())
    return jax.shard_map(
        body,
        mesh=fine,
        in_specs=placed,
        out_specs=(P(rows, "head"),) * 3 + (P(),),
        check_vma=False,
    )
```

```python
import functools
import math

import jax
import jax.numpy as jnp
from jax import lax
from jax.experimental import pallas as pl
from jax.experimental.pallas import tpu as pltpu
from jax.sharding import Mesh
from jax.sharding import PartitionSpec as P

H = 32
DT = 160
DS = 48
SPAN = 384

BLOCK = 128
OWN = 2 * BLOCK
HALO = 192
WINDOW = OWN + 2 * HALO
FIRST_QUERY = WINDOW - OWN
HEADS = 4
TW = HEADS * DT
SW = HEADS * DS
SP = 256
REL = TW + SP
WIDTH_A = 2 * TW + 2 * SW
WIDTH = WIDTH_A + REL
T_AT = (0, TW, 0)
S_AT = (2 * TW, 2 * TW + 128, TW)
CHUNK_AT = (0, 0, WIDTH_A)
S_OFF = (0, SW - 128, 0)
CT = DT ** (-0.5) * math.log2(math.e)
CS = DS ** (-0.5) * math.log2(math.e)
NT = (((1,), (1,)), ((), ()))
FAR = 4096
VMEM = pl.BlockSpec(memory_space=pltpu.VMEM)
SMEM = pl.BlockSpec(memory_space=pltpu.SMEM)
HBM = pl.BlockSpec(memory_space=pltpu.HBM)
F32 = jnp.float32
BF16 = jnp.bfloat16


def call(kernel, out_shape, in_specs, scratch=(), flops=0, moved=0, exps=0, limit=8):
    return pl.pallas_call(
        kernel,
        out_shape=out_shape,
        in_specs=in_specs,
        out_specs=jax.tree.map(lambda _: VMEM, out_shape),
        scratch_shapes=list(scratch),
        compiler_params=pltpu.CompilerParams(vmem_limit_bytes=limit << 20),
        cost_estimate=pl.CostEstimate(flops=flops, bytes_accessed=moved, transcendentals=exps),
    )


def split_kernel(core, *refs):
    arrays, (send, keep), buffers, sems = refs[:6], refs[6:8], refs[8:14], refs[14]
    me = core[0]
    copies = [
        pltpu.make_async_copy(array, buffer, sems.at[i])
        for i, (array, buffer) in enumerate(zip(arrays, buffers))
    ]
    for copy in copies:
        copy.start()
    for copy in copies:
        copy.wait()
    lane = lax.broadcasted_iota(jnp.int32, (BLOCK, SP), 1)
    mine = pl.ds(pl.multiple_of(me * TW, 128), TW)
    other = pl.ds(pl.multiple_of((1 - me) * TW, 128), TW)
    ours, theirs = [], []
    for rel in range(3):
        teacher, student = buffers[rel], buffers[3 + rel]
        at = CHUNK_AT[rel] + T_AT[rel]
        keep[:, at : at + TW] = teacher[:, mine]
        send[:, at : at + TW] = teacher[:, other]
        low = jnp.where(lane < SW, student[:, :SP].astype(F32), 0.0)
        high = pltpu.roll(student[:, 128:].astype(F32), SP - (SW - 128), 1)
        high = jnp.where(lane < SW, high, 0.0)
        ours.append(jnp.where(me == 0, low, high))
        theirs.append(jnp.where(me == 0, high, low))
    for halves, out in ((ours, keep), (theirs, send)):
        second = pltpu.roll(halves[1], S_OFF[1], 1)
        at = 2 * TW
        out[:, at : at + 128] = halves[0][:, :128].astype(BF16)
        out[:, at + 128 : at + 256] = (halves[0][:, 128:] + second[:, :128]).astype(BF16)
        out[:, at + 256 : at + 384] = second[:, 128:].astype(BF16)
        out[:, WIDTH_A + TW :] = halves[2].astype(BF16)


def mask_kernel(chip, docs, rows, starts, weights):
    count = docs.shape[0]
    first = 2 * chip[0] - 2

    def row_of(ref, r):
        at = first + r
        return ref[pl.ds(lax.rem(at + count, count), 1), :]

    lines = []
    for r in range(6):
        at = first + r
        shift = jnp.where(at < 0, -FAR, jnp.where(at >= count, FAR, 0))
        lines.append((row_of(docs, r) + shift).astype(F32))

    def queries(parts):
        joined = jnp.broadcast_to(jnp.concatenate(parts, axis=1), (8, 3 * BLOCK))
        return pltpu.roll(joined, 2 * BLOCK + 64, 1)[:1, :OWN]

    query = queries(lines[3:])
    before = jnp.zeros((1, OWN), F32)
    for line in lines:
        keys = jnp.broadcast_to(line, (BLOCK, BLOCK)).T
        keys = jnp.concatenate([keys, keys], axis=1)
        before = before + jnp.sum(jnp.where(keys < query, 1.0, 0.0), axis=0, keepdims=True)
    starts[...] = before.astype(jnp.int32) - 64
    weights[...] = queries([row_of(rows, r) for r in range(3, 6)])


def edges_kernel(core, keep, recv, *outs):
    half = HALO - BLOCK
    for chunk, cols in enumerate((slice(0, WIDTH_A), slice(WIDTH_A, WIDTH))):
        one, two = outs[2 * chunk : 2 * chunk + 2]

        def write(first, second, after, before):
            after[:half, :] = first[BLOCK - half :, cols]
            after[half:, :] = second[:, cols]
            before[:BLOCK, :] = first[:, cols]
            before[BLOCK:, :] = second[:half, cols]

        @pl.when(core[0] == 0)
        def _():
            write(keep, recv, one, two)

        @pl.when(core[0] != 0)
        def _():
            write(recv, keep, two, one)


def fold(value, op):
    rows, lanes = value.shape
    return op(value.reshape(rows // 8, 8, lanes), axis=0)


def relation_kernel(
    rel,
    core,
    starts,
    weights,
    loss_in,
    *refs,
):
    keep, recv, one, two = refs[:-12]
    t_at, s_at, s_off = T_AT[rel], S_AT[rel], S_OFF[rel]
    grad_left, grad_own, grad_right, loss_out, win, bias, rt, rs, gt, qs, bt, kg = refs[-12:]
    me = core[0]
    def gather(at, rows, source):
        base = CHUNK_AT[rel] if source.shape[1] == WIDTH else 0
        win[at : at + rows, :TW] = source[:, base + t_at : base + t_at + TW]
        win[at : at + rows, TW:] = source[:, base + s_at : base + s_at + SP]

    def gather_all(*sources):
        at = 0
        for source in sources:
            gather(at, source.shape[0], source)
            at += source.shape[0]

    @pl.when(me == 0)
    def _():
        gather_all(one, keep, recv, two)

    @pl.when(me != 0)
    def _():
        gather_all(two, recv, keep, one)

    key = lax.broadcasted_iota(jnp.int32, (WINDOW, OWN), 0)
    query = lax.broadcasted_iota(jnp.int32, (WINDOW, OWN), 1) + FIRST_QUERY
    bias[...] = jnp.where((key >= starts[...]) & (key <= query), 0.0, -1e30)

    lane = lax.broadcasted_iota(jnp.int32, (OWN, SP), 1)
    student = slice(TW, REL)
    row = lax.broadcasted_iota(jnp.int32, (SP, SP), 0)
    col = lax.broadcasted_iota(jnp.int32, (SP, SP), 1)
    unit = jnp.where(row == col, 1.0, 0.0).astype(BF16)
    bt[...] = lax.dot_general(unit, win[:, student], NT, preferred_element_type=F32).astype(BF16)

    gt[:BLOCK, :] = jnp.zeros((BLOCK, HEADS * OWN), BF16)
    gt[WINDOW - BLOCK :, :] = jnp.zeros((BLOCK, HEADS * OWN), BF16)
    step = 64
    tiles = [
        (
            slice(tile * BLOCK, (tile + 1) * BLOCK),
            [slice(at, at + step) for at in range(tile * BLOCK, SPAN + (tile + 1) * BLOCK, step)],
        )
        for tile in range(2)
    ]
    tops, sums = {}, {}
    totals = []

    def scores(head):
        start = head * DT // 128 * 128
        inside = (lane >= head * DT - start) & (lane < (head + 1) * DT - start)
        t_cols = slice(start, start + 256)
        t_query = win[FIRST_QUERY:, t_cols] * jnp.where(inside, 1.0, 0.0).astype(BF16)
        s_start = s_off + head * DS
        inside = (lane >= s_start) & (lane < s_start + DS)
        s_query = win[FIRST_QUERY:, student] * jnp.where(inside, 1.0, 0.0).astype(BF16)
        qs[head * OWN : (head + 1) * OWN, :] = s_query
        rt[head] = (
            lax.dot_general(win[:, t_cols], t_query, NT, preferred_element_type=F32) + bias[...]
        )
        rs[head] = (
            lax.dot_general(win[:, student], s_query, NT, preferred_element_type=F32) + bias[...]
        )

    def maxima(head):
        for tile, (lanes, parts) in enumerate(tiles):
            for z, r, scale in ((0, rt, CT), (1, rs, CS)):
                top = fold(r[head, parts[0], lanes], jnp.max)
                for part in parts[1:]:
                    top = jnp.maximum(top, fold(r[head, part, lanes], jnp.max))
                tops[head, tile, z] = jnp.max(top, axis=0, keepdims=True) * scale

    def exponentials(head):
        for tile, (lanes, parts) in enumerate(tiles):
            top_t, top_s = tops[head, tile, 0], tops[head, tile, 1]
            sum_t = jnp.zeros((8, BLOCK), F32)
            sum_s = jnp.zeros((8, BLOCK), F32)
            cross = jnp.zeros((8, BLOCK), F32)
            for part in parts:
                ut = rt[head, part, lanes] * CT - top_t
                us = rs[head, part, lanes] * CS - top_s
                et = jnp.exp2(ut)
                es = jnp.exp2(us)
                sum_t = sum_t + fold(et, jnp.sum)
                sum_s = sum_s + fold(es, jnp.sum)
                cross = cross + fold(et * (ut - us), jnp.sum)
                rt[head, part, lanes] = et
                rs[head, part, lanes] = es
            sum_t = jnp.sum(sum_t, axis=0, keepdims=True)
            sum_s = jnp.sum(sum_s, axis=0, keepdims=True)
            cross = jnp.sum(cross, axis=0, keepdims=True)
            weight = weights[:, lanes]
            totals.append(weight * (cross / sum_t - jnp.log2(sum_t) + jnp.log2(sum_s)))
            sums[head, tile] = weight * DS ** (-0.5) / sum_t, weight * DS ** (-0.5) / sum_s

    def gradients(head):
        for tile, (lanes, parts) in enumerate(tiles):
            scale_t, scale_s = sums[head, tile]
            g_cols = slice(head * OWN + tile * BLOCK, head * OWN + (tile + 1) * BLOCK)
            for part in parts:
                gt[part, g_cols] = (
                    rs[head, part, lanes] * scale_s - rt[head, part, lanes] * scale_t
                ).astype(BF16)

    row_grads = []

    def products(head):
        row_grads.append(
            jnp.dot(
                bt[s_off + head * DS : s_off + (head + 1) * DS, :],
                gt[:, head * OWN : (head + 1) * OWN],
                preferred_element_type=F32,
            )
        )

    def key_product(first, last):
        return jnp.dot(
            gt[:, first * OWN : last * OWN],
            qs[first * OWN : last * OWN, :],
            preferred_element_type=F32,
        )

    scores(0)
    scores(1)
    maxima(0)
    exponentials(0)
    scores(2)
    maxima(1)
    gradients(0)
    exponentials(1)
    products(0)
    scores(3)
    maxima(2)
    gradients(1)
    exponentials(2)
    products(1)
    kg[...] = key_product(0, 2)
    maxima(3)
    gradients(2)
    exponentials(3)
    products(2)
    gradients(3)
    products(3)
    key_grad = kg[...] + key_product(2, 4)
    loss_out[...] = loss_in[...] + functools.reduce(jnp.add, totals) * math.log(2.0)
    row_grads.insert(HEADS if s_off == 0 else 0, jnp.zeros((SP - SW, OWN), F32))
    row_grad = jnp.concatenate(row_grads, axis=0).T
    late = HALO + OWN - FIRST_QUERY
    grad_left[...] = key_grad[:HALO].astype(BF16)
    grad_own[: OWN - late, :] = key_grad[HALO:FIRST_QUERY]
    grad_own[OWN - late :, :] = key_grad[FIRST_QUERY : HALO + OWN] + row_grad[:late]
    grad_right[...] = (key_grad[HALO + OWN :] + row_grad[late:]).astype(BF16)


def join_kernel(core, loss, l0, l1, l2, r0, r1, r2, one, two, copies):
    copies[...] = jnp.broadcast_to(loss[...], copies.shape)

    def write(after, before):
        for rel, (left, right) in enumerate(((l0, r0), (l1, r1), (l2, r2))):
            before[:, rel * SP : (rel + 1) * SP] = left[...]
            after[:, rel * SP : (rel + 1) * SP] = right[...]

    @pl.when(core[0] == 0)
    def _():
        write(one, two)

    @pl.when(core[0] != 0)
    def _():
        write(two, one)


def merge_kernel(core, parts, o0, o1, o2, mine, other, keep, send, copies):
    copies[...] = jnp.broadcast_to(jnp.sum(parts[...], axis=0, keepdims=True), copies.shape)
    half = HALO - BLOCK
    for rel, own in enumerate((o0, o1, o2)):
        cols = slice(rel * SP, (rel + 1) * SP)

        @pl.when(core[0] == 0)
        def _():
            keep[:BLOCK, cols] = own[:BLOCK, :] + mine[:BLOCK, cols].astype(F32)
            keep[BLOCK:, cols] = other[:BLOCK, cols].astype(F32)
            send[:half, cols] = own[BLOCK : BLOCK + half, :] + mine[BLOCK:, cols].astype(F32)
            send[half:BLOCK, cols] = own[BLOCK + half :, :]
            send[BLOCK:, cols] = other[BLOCK:, cols].astype(F32)

        @pl.when(core[0] != 0)
        def _():
            keep[:BLOCK, cols] = own[BLOCK:, :] + mine[half:, cols].astype(F32)
            keep[BLOCK:, cols] = other[half:, cols].astype(F32)
            send[: BLOCK - half, cols] = own[: BLOCK - half, :]
            send[BLOCK - half : BLOCK, cols] = own[BLOCK - half : BLOCK, :] + mine[
                :half, cols
            ].astype(F32)
            send[BLOCK:, cols] = other[:half, cols].astype(F32)


def place_kernel(tokens, core, parts, keep, recv, oq, ok, ov, loss):
    me = core[0]
    total = jnp.sum(jnp.sum(parts[...], axis=0, keepdims=True), axis=1, keepdims=True)
    loss[...] = total * (1.0 / (3 * H * tokens))
    half = HALO - BLOCK
    empty = jnp.zeros((BLOCK, 2 * SW - SP), F32)
    gap = jnp.zeros((BLOCK - half, SP), F32)
    for rel, out in enumerate((oq, ok, ov)):
        cols = slice(rel * SP, (rel + 1) * SP)
        late = recv[BLOCK:, cols]
        first = jnp.concatenate([late, gap], axis=0)
        last = jnp.concatenate([gap, late], axis=0)
        ours = keep[:BLOCK, cols] + jnp.where(me == 0, last, first)
        theirs = keep[BLOCK:, cols] + recv[:BLOCK, cols]
        ours = jnp.concatenate([ours, empty], axis=1)
        theirs = jnp.concatenate([theirs, empty], axis=1)
        low = jnp.where(me == 0, ours, theirs)
        high = jnp.where(me == 0, theirs, ours)
        off = S_OFF[rel]
        if off:
            low = pltpu.roll(low, 2 * SW - off, 1)
        out[...] = low + pltpu.roll(high, SW - off, 1)


def shape(rows, cols, dtype):
    return jax.ShapeDtypeStruct((rows, cols), dtype)


def call_relation(rel, core, starts, weight, loss, chunk):
    return call(
        functools.partial(relation_kernel, rel),
        [
            shape(HALO, SP, BF16),
            shape(OWN, SP, F32),
            shape(HALO, SP, BF16),
            shape(1, BLOCK, F32),
        ],
        [SMEM] + [VMEM] * (3 + len(chunk)),
        scratch=[
            pltpu.VMEM((WINDOW, REL), BF16),
            pltpu.VMEM((WINDOW, OWN), F32),
            pltpu.VMEM((HEADS, WINDOW, OWN), F32),
            pltpu.VMEM((HEADS, WINDOW, OWN), F32),
            pltpu.VMEM((WINDOW, HEADS * OWN), BF16),
            pltpu.VMEM((HEADS * OWN, SP), BF16),
            pltpu.VMEM((SP, WINDOW), BF16),
            pltpu.VMEM((WINDOW, SP), F32),
        ],
        flops=2 * 16 * WINDOW * OWN * 256,
        moved=2 << 20,
        exps=2 * HEADS * WINDOW * OWN,
        limit=20,
    )(core, starts, weight, loss, *chunk)


def body(teacher_q, teacher_k, teacher_v, student_q, student_k, student_v, doc_ids, row_weight):
    tok = ("y", "z", "parity", "core")
    count = lax.axis_size(tok)
    core = lax.axis_index("core").astype(jnp.int32).reshape(1)
    chip = lax.axis_index(("y", "z", "parity"))

    def other_core(value):
        return lax.ppermute(value, "core", [(0, 1), (1, 0)])

    def neighbours(value, way, cross=0):
        step = (2 * way, -2 * way)
        pairs = [(i, ((i + step[i % 2]) % count) ^ cross) for i in range(count)]
        return lax.ppermute(value, tok, pairs)

    arrays = (teacher_q, teacher_k, teacher_v, student_q, student_k, student_v)
    send, keep = call(
        split_kernel,
        [shape(BLOCK, WIDTH, BF16)] * 2,
        [SMEM] + [HBM] * 6,
        scratch=[pltpu.VMEM(a.shape, BF16) for a in arrays] + [pltpu.SemaphoreType.DMA((6,))],
        moved=4 << 20,
        limit=56,
    )(core, *arrays)
    recv = other_core(send)
    edges = call(
        edges_kernel,
        [shape(HALO, WIDTH_A, BF16)] * 2 + [shape(HALO, REL, BF16)] * 2,
        [SMEM] + [VMEM] * 2,
        moved=2 << 20,
    )(core, keep, recv)
    halo_a = [neighbours(edges[0], 1), neighbours(edges[1], -1)]
    halo_b = [neighbours(edges[2], 1), neighbours(edges[3], -1)]

    doc_ids, row_weight, _ = lax.optimization_barrier((doc_ids, row_weight, edges[0]))
    starts, weight = call(
        mask_kernel,
        [shape(1, OWN, jnp.int32), shape(1, OWN, F32)],
        [SMEM] + [VMEM] * 2,
        moved=1 << 17,
    )(
        chip.astype(jnp.int32).reshape(1),
        doc_ids.reshape(-1, BLOCK),
        row_weight.reshape(-1, BLOCK),
    )
    loss = jnp.zeros((1, BLOCK), F32)
    grads = []
    for rel in range(3):
        chunk = (keep, recv, *(halo_b if rel == 2 else halo_a))
        *grad, loss = call_relation(rel, core, starts, weight, loss, chunk)
        grads.append(grad)

    stages = (("z", "parity", "core"), ("y", "head"))
    copies = [shape(lax.axis_size(axes), BLOCK, F32) for axes in stages]

    def exchange(value, axes):
        return lax.all_to_all(value, axes, 0, 0, tiled=True)

    one, two, parts = call(
        join_kernel,
        [shape(HALO, 3 * SP, BF16)] * 2 + [copies[0]],
        [SMEM] + [VMEM] * 7,
        moved=1 << 20,
    )(core, loss, *(g[0] for g in grads), *(g[2] for g in grads))
    one = neighbours(one, 1)
    two = neighbours(two, -1, 1)
    parts = exchange(parts, stages[0])
    kept, sent, parts = call(
        merge_kernel,
        [shape(OWN, 3 * SP, F32), shape(HALO, 3 * SP, F32), copies[1]],
        [SMEM] + [VMEM] * 6,
        moved=2 << 20,
    )(core, parts, *(g[1] for g in grads), one, two)
    received = other_core(sent)
    parts = exchange(parts, stages[1])
    grad_q, grad_k, grad_v, loss = call(
        functools.partial(place_kernel, doc_ids.shape[0]),
        [shape(BLOCK, 2 * SW, F32)] * 3 + [shape(1, 1, F32)],
        [SMEM] + [VMEM] * 3,
        moved=1 << 20,
    )(core, parts, kept, received)
    return grad_q, grad_k, grad_v, loss[0, 0]


def solution(mesh):
    tok, head = mesh.devices.shape
    z = 4 if tok == 128 else 1
    axes = ("y", "z", "parity", "core", "head")
    fine = Mesh(mesh.devices.reshape(tok // (4 * z), z, 2, 2, head), axes)
    rows = axes[:4]
    placed = (P(rows, "head"),) * 6 + (P(), P())
    return jax.shard_map(
        body,
        mesh=fine,
        in_specs=placed,
        out_specs=(P(rows, "head"),) * 3 + (P(),),
        check_vma=False,
    )
```

```python
import functools
import math

import jax
import jax.numpy as jnp
from jax import lax
from jax.experimental import pallas as pl
from jax.experimental.pallas import tpu as pltpu
from jax.sharding import Mesh
from jax.sharding import PartitionSpec as P

H = 32
DT = 160
DS = 48
SPAN = 384

BLOCK = 128
OWN = 2 * BLOCK
HALO = 192
WINDOW = OWN + 2 * HALO
FIRST_QUERY = WINDOW - OWN
HEADS = 4
TW = HEADS * DT
SW = HEADS * DS
SP = 256
REL = TW + SP
PART = 2 * TW
WIDTH = 2 * PART
T_AT = (0, PART, PART + TW)
S_AT = (TW, TW + SP, TW + SP + 128)
S_OFF = (0, 0, SW - 128)
CT = DT ** (-0.5) * math.log2(math.e)
CS = DS ** (-0.5) * math.log2(math.e)
NT = (((1,), (1,)), ((), ()))
FAR = 4096
VMEM = pl.BlockSpec(memory_space=pltpu.VMEM)
SMEM = pl.BlockSpec(memory_space=pltpu.SMEM)
HBM = pl.BlockSpec(memory_space=pltpu.HBM)
F32 = jnp.float32
BF16 = jnp.bfloat16


def call(kernel, out_shape, in_specs, scratch=(), flops=0, moved=0, exps=0, limit=8):
    return pl.pallas_call(
        kernel,
        out_shape=out_shape,
        in_specs=in_specs,
        out_specs=jax.tree.map(lambda _: VMEM, out_shape),
        scratch_shapes=list(scratch),
        compiler_params=pltpu.CompilerParams(vmem_limit_bytes=limit << 20),
        cost_estimate=pl.CostEstimate(flops=flops, bytes_accessed=moved, transcendentals=exps),
    )


def split_kernel(core, *refs):
    arrays, (send, keep), buffers, sems = refs[:6], refs[6:8], refs[8:14], refs[14]
    me = core[0]
    copies = [
        pltpu.make_async_copy(array, buffer, sems.at[i])
        for i, (array, buffer) in enumerate(zip(arrays, buffers))
    ]
    for copy in copies:
        copy.start()
    for copy in copies:
        copy.wait()
    lane = lax.broadcasted_iota(jnp.int32, (BLOCK, SP), 1)
    mine = pl.ds(pl.multiple_of(me * TW, 128), TW)
    other = pl.ds(pl.multiple_of((1 - me) * TW, 128), TW)
    ours, theirs = [], []
    for rel in range(3):
        teacher, student = buffers[rel], buffers[3 + rel]
        at = T_AT[rel]
        keep[:, at : at + TW] = teacher[:, mine]
        send[:, at : at + TW] = teacher[:, other]
        low = jnp.where(lane < SW, student[:, :SP].astype(F32), 0.0)
        high = pltpu.roll(student[:, 128:].astype(F32), SP - (SW - 128), 1)
        high = jnp.where(lane < SW, high, 0.0)
        ours.append(jnp.where(me == 0, low, high))
        theirs.append(jnp.where(me == 0, high, low))
    for halves, out in ((ours, keep), (theirs, send)):
        out[:, TW : TW + SP] = halves[0].astype(BF16)
        second = pltpu.roll(halves[2], S_OFF[2], 1)
        at = S_AT[1]
        out[:, at : at + 128] = halves[1][:, :128].astype(BF16)
        out[:, at + 128 : at + 256] = (halves[1][:, 128:] + second[:, :128]).astype(BF16)
        out[:, at + 256 : at + 384] = second[:, 128:].astype(BF16)


def mask_kernel(chip, docs, rows, starts, weights):
    count = docs.shape[0]
    first = 2 * chip[0] - 2

    def row_of(ref, r):
        at = first + r
        return ref[pl.ds(lax.rem(at + count, count), 1), :]

    lines = []
    for r in range(6):
        at = first + r
        shift = jnp.where(at < 0, -FAR, jnp.where(at >= count, FAR, 0))
        lines.append((row_of(docs, r) + shift).astype(F32))

    def queries(parts):
        joined = jnp.broadcast_to(jnp.concatenate(parts, axis=1), (8, 3 * BLOCK))
        return pltpu.roll(joined, 2 * BLOCK + 64, 1)[:1, :OWN]

    query = queries(lines[3:])
    before = jnp.zeros((1, OWN), F32)
    for line in lines:
        keys = jnp.broadcast_to(line, (BLOCK, BLOCK)).T
        keys = jnp.concatenate([keys, keys], axis=1)
        before = before + jnp.sum(jnp.where(keys < query, 1.0, 0.0), axis=0, keepdims=True)
    starts[...] = before.astype(jnp.int32) - 64
    weights[...] = queries([row_of(rows, r) for r in range(3, 6)])


def edges_kernel(cols, core, keep, recv, *refs):
    one, two = refs[-2:]
    half = HALO - BLOCK

    def write(first, second, after, before):
        after[:half, :] = first[BLOCK - half :, cols]
        after[half:, :] = second[:, cols]
        before[:BLOCK, :] = first[:, cols]
        before[BLOCK:, :] = second[:half, cols]

    @pl.when(core[0] == 0)
    def _():
        write(keep, recv, one, two)

    @pl.when(core[0] != 0)
    def _():
        write(recv, keep, two, one)


def call_edges(cols, core, keep, recv, *after):
    return call(
        functools.partial(edges_kernel, cols),
        [shape(HALO, cols.stop - cols.start, BF16)] * 2,
        [SMEM] + [VMEM] * (2 + len(after)),
        moved=2 << 20,
    )(core, keep, recv, *after)


def fold(value, op):
    rows, lanes = value.shape
    return op(value.reshape(rows // 8, 8, lanes), axis=0)


def relation_kernel(
    rel,
    core,
    starts,
    weights,
    loss_in,
    *refs,
):
    keep, recv, *halo = refs[:-12]
    grad_left, grad_own, grad_right, loss_out, win, bias, rt, rs, gt, qs, bt, kg = refs[-12:]
    t_at, s_at, s_off = T_AT[rel], S_AT[rel], S_OFF[rel]
    me = core[0]

    def gather_all(*sources):
        at = 0
        for source in sources:
            t_source, s_source = source if isinstance(source, tuple) else (source, source)
            rows, width = t_source.shape
            win[at : at + rows, :TW] = t_source[:, t_at % width : t_at % width + TW]
            win[at : at + rows, TW:] = s_source[:, s_at : s_at + SP]
            at += rows

    one, two = (halo[-2], halo[0]), (halo[-1], halo[1])

    @pl.when(me == 0)
    def _():
        gather_all(one, keep, recv, two)

    @pl.when(me != 0)
    def _():
        gather_all(two, recv, keep, one)

    key = lax.broadcasted_iota(jnp.int32, (WINDOW, OWN), 0)
    query = lax.broadcasted_iota(jnp.int32, (WINDOW, OWN), 1) + FIRST_QUERY
    bias[...] = jnp.where((key >= starts[...]) & (key <= query), 0.0, -1e30)

    lane = lax.broadcasted_iota(jnp.int32, (OWN, SP), 1)
    student = slice(TW, REL)
    row = lax.broadcasted_iota(jnp.int32, (SP, SP), 0)
    col = lax.broadcasted_iota(jnp.int32, (SP, SP), 1)
    unit = jnp.where(row == col, 1.0, 0.0).astype(BF16)
    bt[...] = lax.dot_general(unit, win[:, student], NT, preferred_element_type=F32).astype(BF16)

    gt[:BLOCK, :] = jnp.zeros((BLOCK, HEADS * OWN), BF16)
    gt[WINDOW - BLOCK :, :] = jnp.zeros((BLOCK, HEADS * OWN), BF16)
    step = 64
    tiles = [
        (
            slice(tile * BLOCK, (tile + 1) * BLOCK),
            [slice(at, at + step) for at in range(tile * BLOCK, SPAN + (tile + 1) * BLOCK, step)],
        )
        for tile in range(2)
    ]
    tops, sums = {}, {}
    totals = []

    def scores(head):
        start = head * DT // 128 * 128
        inside = (lane >= head * DT - start) & (lane < (head + 1) * DT - start)
        t_cols = slice(start, start + 256)
        t_query = win[FIRST_QUERY:, t_cols] * jnp.where(inside, 1.0, 0.0).astype(BF16)
        s_start = s_off + head * DS
        inside = (lane >= s_start) & (lane < s_start + DS)
        s_query = win[FIRST_QUERY:, student] * jnp.where(inside, 1.0, 0.0).astype(BF16)
        qs[head * OWN : (head + 1) * OWN, :] = s_query
        rt[head] = (
            lax.dot_general(win[:, t_cols], t_query, NT, preferred_element_type=F32) + bias[...]
        )
        rs[head] = (
            lax.dot_general(win[:, student], s_query, NT, preferred_element_type=F32) + bias[...]
        )

    def maxima(head):
        for tile, (lanes, parts) in enumerate(tiles):
            for z, r, scale in ((0, rt, CT), (1, rs, CS)):
                top = fold(r[head, parts[0], lanes], jnp.max)
                for part in parts[1:]:
                    top = jnp.maximum(top, fold(r[head, part, lanes], jnp.max))
                tops[head, tile, z] = jnp.max(top, axis=0, keepdims=True) * scale

    def exponentials(head):
        for tile, (lanes, parts) in enumerate(tiles):
            top_t, top_s = tops[head, tile, 0], tops[head, tile, 1]
            sum_t = jnp.zeros((8, BLOCK), F32)
            sum_s = jnp.zeros((8, BLOCK), F32)
            cross = jnp.zeros((8, BLOCK), F32)
            for part in parts:
                ut = rt[head, part, lanes] * CT - top_t
                us = rs[head, part, lanes] * CS - top_s
                et = jnp.exp2(ut)
                es = jnp.exp2(us)
                sum_t = sum_t + fold(et, jnp.sum)
                sum_s = sum_s + fold(es, jnp.sum)
                cross = cross + fold(et * (ut - us), jnp.sum)
                rt[head, part, lanes] = et
                rs[head, part, lanes] = es
            sum_t = jnp.sum(sum_t, axis=0, keepdims=True)
            sum_s = jnp.sum(sum_s, axis=0, keepdims=True)
            cross = jnp.sum(cross, axis=0, keepdims=True)
            weight = weights[:, lanes]
            totals.append(weight * (cross / sum_t - jnp.log2(sum_t) + jnp.log2(sum_s)))
            sums[head, tile] = weight * DS ** (-0.5) / sum_t, weight * DS ** (-0.5) / sum_s

    def gradients(head):
        for tile, (lanes, parts) in enumerate(tiles):
            scale_t, scale_s = sums[head, tile]
            g_cols = slice(head * OWN + tile * BLOCK, head * OWN + (tile + 1) * BLOCK)
            for part in parts:
                gt[part, g_cols] = (
                    rs[head, part, lanes] * scale_s - rt[head, part, lanes] * scale_t
                ).astype(BF16)

    row_grads = []

    def products(head):
        row_grads.append(
            jnp.dot(
                bt[s_off + head * DS : s_off + (head + 1) * DS, :],
                gt[:, head * OWN : (head + 1) * OWN],
                preferred_element_type=F32,
            )
        )

    def key_product(first, last):
        return jnp.dot(
            gt[:, first * OWN : last * OWN],
            qs[first * OWN : last * OWN, :],
            preferred_element_type=F32,
        )

    scores(0)
    scores(1)
    maxima(0)
    exponentials(0)
    scores(2)
    maxima(1)
    gradients(0)
    exponentials(1)
    products(0)
    scores(3)
    maxima(2)
    gradients(1)
    exponentials(2)
    products(1)
    kg[...] = key_product(0, 2)
    maxima(3)
    gradients(2)
    exponentials(3)
    products(2)
    gradients(3)
    products(3)
    key_grad = kg[...] + key_product(2, 4)
    loss_out[...] = loss_in[...] + functools.reduce(jnp.add, totals) * math.log(2.0)
    row_grads.insert(HEADS if s_off == 0 else 0, jnp.zeros((SP - SW, OWN), F32))
    row_grad = jnp.concatenate(row_grads, axis=0).T
    late = HALO + OWN - FIRST_QUERY
    grad_left[...] = key_grad[:HALO].astype(BF16)
    grad_own[: OWN - late, :] = key_grad[HALO:FIRST_QUERY]
    grad_own[OWN - late :, :] = key_grad[FIRST_QUERY : HALO + OWN] + row_grad[:late]
    grad_right[...] = (key_grad[HALO + OWN :] + row_grad[late:]).astype(BF16)


def join_kernel(core, loss, l0, l1, l2, r0, r1, r2, one, two, copies):
    copies[...] = jnp.broadcast_to(loss[...], copies.shape)

    def write(after, before):
        for rel, (left, right) in enumerate(((l0, r0), (l1, r1), (l2, r2))):
            before[:, rel * SP : (rel + 1) * SP] = left[...]
            after[:, rel * SP : (rel + 1) * SP] = right[...]

    @pl.when(core[0] == 0)
    def _():
        write(one, two)

    @pl.when(core[0] != 0)
    def _():
        write(two, one)


def merge_kernel(core, parts, o0, o1, o2, mine, other, keep, send, copies):
    copies[...] = jnp.broadcast_to(jnp.sum(parts[...], axis=0, keepdims=True), copies.shape)
    half = HALO - BLOCK
    for rel, own in enumerate((o0, o1, o2)):
        cols = slice(rel * SP, (rel + 1) * SP)

        @pl.when(core[0] == 0)
        def _():
            keep[:BLOCK, cols] = own[:BLOCK, :] + mine[:BLOCK, cols].astype(F32)
            keep[BLOCK:, cols] = other[:BLOCK, cols].astype(F32)
            send[:half, cols] = own[BLOCK : BLOCK + half, :] + mine[BLOCK:, cols].astype(F32)
            send[half:BLOCK, cols] = own[BLOCK + half :, :]
            send[BLOCK:, cols] = other[BLOCK:, cols].astype(F32)

        @pl.when(core[0] != 0)
        def _():
            keep[:BLOCK, cols] = own[BLOCK:, :] + mine[half:, cols].astype(F32)
            keep[BLOCK:, cols] = other[half:, cols].astype(F32)
            send[: BLOCK - half, cols] = own[: BLOCK - half, :]
            send[BLOCK - half : BLOCK, cols] = own[BLOCK - half : BLOCK, :] + mine[
                :half, cols
            ].astype(F32)
            send[BLOCK:, cols] = other[:half, cols].astype(F32)


def place_kernel(tokens, core, parts, keep, recv, oq, ok, ov, loss):
    me = core[0]
    total = jnp.sum(jnp.sum(parts[...], axis=0, keepdims=True), axis=1, keepdims=True)
    loss[...] = total * (1.0 / (3 * H * tokens))
    half = HALO - BLOCK
    empty = jnp.zeros((BLOCK, 2 * SW - SP), F32)
    gap = jnp.zeros((BLOCK - half, SP), F32)
    for rel, out in enumerate((oq, ok, ov)):
        cols = slice(rel * SP, (rel + 1) * SP)
        late = recv[BLOCK:, cols]
        first = jnp.concatenate([late, gap], axis=0)
        last = jnp.concatenate([gap, late], axis=0)
        ours = keep[:BLOCK, cols] + jnp.where(me == 0, last, first)
        theirs = keep[BLOCK:, cols] + recv[:BLOCK, cols]
        ours = jnp.concatenate([ours, empty], axis=1)
        theirs = jnp.concatenate([theirs, empty], axis=1)
        low = jnp.where(me == 0, ours, theirs)
        high = jnp.where(me == 0, theirs, ours)
        off = S_OFF[rel]
        if off:
            low = pltpu.roll(low, 2 * SW - off, 1)
        out[...] = low + pltpu.roll(high, SW - off, 1)


def shape(rows, cols, dtype):
    return jax.ShapeDtypeStruct((rows, cols), dtype)


def call_relation(rel, core, starts, weight, loss, chunk):
    return call(
        functools.partial(relation_kernel, rel),
        [
            shape(HALO, SP, BF16),
            shape(OWN, SP, F32),
            shape(HALO, SP, BF16),
            shape(1, BLOCK, F32),
        ],
        [SMEM] + [VMEM] * (3 + len(chunk)),
        scratch=[
            pltpu.VMEM((WINDOW, REL), BF16),
            pltpu.VMEM((WINDOW, OWN), F32),
            pltpu.VMEM((HEADS, WINDOW, OWN), F32),
            pltpu.VMEM((HEADS, WINDOW, OWN), F32),
            pltpu.VMEM((WINDOW, HEADS * OWN), BF16),
            pltpu.VMEM((HEADS * OWN, SP), BF16),
            pltpu.VMEM((SP, WINDOW), BF16),
            pltpu.VMEM((WINDOW, SP), F32),
        ],
        flops=2 * 16 * WINDOW * OWN * 256,
        moved=2 << 20,
        exps=2 * HEADS * WINDOW * OWN,
        limit=20,
    )(core, starts, weight, loss, *chunk)


def body(teacher_q, teacher_k, teacher_v, student_q, student_k, student_v, doc_ids, row_weight):
    tok = ("y", "z", "parity", "core")
    count = lax.axis_size(tok)
    core = lax.axis_index("core").astype(jnp.int32).reshape(1)
    chip = lax.axis_index(("y", "z", "parity"))

    def other_core(value):
        return lax.ppermute(value, "core", [(0, 1), (1, 0)])

    def neighbours(value, way, cross=0):
        step = (2 * way, -2 * way)
        pairs = [(i, ((i + step[i % 2]) % count) ^ cross) for i in range(count)]
        return lax.ppermute(value, tok, pairs)

    arrays = (teacher_q, teacher_k, teacher_v, student_q, student_k, student_v)
    send, keep = call(
        split_kernel,
        [shape(BLOCK, WIDTH, BF16)] * 2,
        [SMEM] + [HBM] * 6,
        scratch=[pltpu.VMEM(a.shape, BF16) for a in arrays] + [pltpu.SemaphoreType.DMA((6,))],
        moved=4 << 20,
        limit=56,
    )(core, *arrays)
    recv = other_core(send)
    edges_a = call_edges(slice(0, PART), core, keep, recv)
    halo_a = [neighbours(edges_a[0], 1), neighbours(edges_a[1], -1)]
    doc_ids, row_weight, _ = lax.optimization_barrier((doc_ids, row_weight, edges_a[0]))
    starts, weight = call(
        mask_kernel,
        [shape(1, OWN, jnp.int32), shape(1, OWN, F32)],
        [SMEM] + [VMEM] * 2,
        moved=1 << 17,
    )(
        chip.astype(jnp.int32).reshape(1),
        doc_ids.reshape(-1, BLOCK),
        row_weight.reshape(-1, BLOCK),
    )
    edges_b = call_edges(slice(PART, WIDTH), core, keep, recv, weight)
    halo_b = [neighbours(edges_b[0], 1), neighbours(edges_b[1], -1)]

    loss = jnp.zeros((1, BLOCK), F32)
    grads = []
    for rel in range(3):
        chunk = (keep, recv, *halo_a, *(halo_b if rel else ()))
        *grad, loss = call_relation(rel, core, starts, weight, loss, chunk)
        grads.append(grad)

    stages = (("z", "parity", "core"), ("y", "head"))
    copies = [shape(lax.axis_size(axes), BLOCK, F32) for axes in stages]

    def exchange(value, axes):
        return lax.all_to_all(value, axes, 0, 0, tiled=True)

    one, two, parts = call(
        join_kernel,
        [shape(HALO, 3 * SP, BF16)] * 2 + [copies[0]],
        [SMEM] + [VMEM] * 7,
        moved=1 << 20,
    )(core, loss, *(g[0] for g in grads), *(g[2] for g in grads))
    one = neighbours(one, 1)
    two = neighbours(two, -1, 1)
    parts = exchange(parts, stages[0])
    kept, sent, parts = call(
        merge_kernel,
        [shape(OWN, 3 * SP, F32), shape(HALO, 3 * SP, F32), copies[1]],
        [SMEM] + [VMEM] * 6,
        moved=2 << 20,
    )(core, parts, *(g[1] for g in grads), one, two)
    received = other_core(sent)
    parts = exchange(parts, stages[1])
    grad_q, grad_k, grad_v, loss = call(
        functools.partial(place_kernel, doc_ids.shape[0]),
        [shape(BLOCK, 2 * SW, F32)] * 3 + [shape(1, 1, F32)],
        [SMEM] + [VMEM] * 3,
        moved=1 << 20,
    )(core, parts, kept, received)
    return grad_q, grad_k, grad_v, loss[0, 0]


def solution(mesh):
    tok, head = mesh.devices.shape
    z = 4 if tok == 128 else 1
    axes = ("y", "z", "parity", "core", "head")
    fine = Mesh(mesh.devices.reshape(tok // (4 * z), z, 2, 2, head), axes)
    rows = axes[:4]
    placed = (P(rows, "head"),) * 6 + (P(), P())
    return jax.shard_map(
        body,
        mesh=fine,
        in_specs=placed,
        out_specs=(P(rows, "head"),) * 3 + (P(),),
        check_vma=False,
    )
```

```python
import functools
import math

import jax
import jax.numpy as jnp
from jax import lax
from jax.experimental import pallas as pl
from jax.experimental.pallas import tpu as pltpu
from jax.sharding import Mesh
from jax.sharding import PartitionSpec as P

H = 32
DT = 160
DS = 48
SPAN = 384

BLOCK = 128
OWN = 2 * BLOCK
HALO = 192
WINDOW = OWN + 2 * HALO
FIRST_QUERY = WINDOW - OWN
HEADS = 4
TW = HEADS * DT
SW = HEADS * DS
SP = 256
REL = TW + SP
PART = 2 * TW
WIDTH = 2 * PART
T_AT = (0, PART, PART + TW)
S_AT = (TW, TW + SP, TW + SP + 128)
S_OFF = (0, 0, SW - 128)
CT = DT ** (-0.5) * math.log2(math.e)
CS = DS ** (-0.5) * math.log2(math.e)
NT = (((1,), (1,)), ((), ()))
FAR = 4096
VMEM = pl.BlockSpec(memory_space=pltpu.VMEM)
SMEM = pl.BlockSpec(memory_space=pltpu.SMEM)
HBM = pl.BlockSpec(memory_space=pltpu.HBM)
F32 = jnp.float32
BF16 = jnp.bfloat16


def call(kernel, out_shape, in_specs, scratch=(), flops=0, moved=0, exps=0, limit=8):
    return pl.pallas_call(
        kernel,
        out_shape=out_shape,
        in_specs=in_specs,
        out_specs=jax.tree.map(lambda _: VMEM, out_shape),
        scratch_shapes=list(scratch),
        compiler_params=pltpu.CompilerParams(vmem_limit_bytes=limit << 20),
        cost_estimate=pl.CostEstimate(flops=flops, bytes_accessed=moved, transcendentals=exps),
    )


def split_kernel(core, *refs):
    arrays, (send, keep), buffers, sems = refs[:6], refs[6:8], refs[8:14], refs[14]
    me = core[0]
    copies = [
        pltpu.make_async_copy(array, buffer, sems.at[i])
        for i, (array, buffer) in enumerate(zip(arrays, buffers))
    ]
    for copy in copies:
        copy.start()
    for copy in copies:
        copy.wait()
    lane = lax.broadcasted_iota(jnp.int32, (BLOCK, SP), 1)
    mine = pl.ds(pl.multiple_of(me * TW, 128), TW)
    other = pl.ds(pl.multiple_of((1 - me) * TW, 128), TW)
    ours, theirs = [], []
    for rel in range(3):
        teacher, student = buffers[rel], buffers[3 + rel]
        at = T_AT[rel]
        keep[:, at : at + TW] = teacher[:, mine]
        send[:, at : at + TW] = teacher[:, other]
        low = jnp.where(lane < SW, student[:, :SP].astype(F32), 0.0)
        high = pltpu.roll(student[:, 128:].astype(F32), SP - (SW - 128), 1)
        high = jnp.where(lane < SW, high, 0.0)
        ours.append(jnp.where(me == 0, low, high))
        theirs.append(jnp.where(me == 0, high, low))
    for halves, out in ((ours, keep), (theirs, send)):
        out[:, TW : TW + SP] = halves[0].astype(BF16)
        second = pltpu.roll(halves[2], S_OFF[2], 1)
        at = S_AT[1]
        out[:, at : at + 128] = halves[1][:, :128].astype(BF16)
        out[:, at + 128 : at + 256] = (halves[1][:, 128:] + second[:, :128]).astype(BF16)
        out[:, at + 256 : at + 384] = second[:, 128:].astype(BF16)


def mask_kernel(chip, docs, rows, starts, weights):
    count = docs.shape[0]
    first = 2 * chip[0] - 2

    def row_of(ref, r):
        at = first + r
        return ref[pl.ds(lax.rem(at + count, count), 1), :]

    lines = []
    for r in range(6):
        at = first + r
        shift = jnp.where(at < 0, -FAR, jnp.where(at >= count, FAR, 0))
        lines.append((row_of(docs, r) + shift).astype(F32))

    def queries(parts):
        joined = jnp.broadcast_to(jnp.concatenate(parts, axis=1), (8, 3 * BLOCK))
        return pltpu.roll(joined, 2 * BLOCK + 64, 1)[:1, :OWN]

    query = queries(lines[3:])
    before = jnp.zeros((1, OWN), F32)
    for line in lines:
        keys = jnp.broadcast_to(line, (BLOCK, BLOCK)).T
        keys = jnp.concatenate([keys, keys], axis=1)
        before = before + jnp.sum(jnp.where(keys < query, 1.0, 0.0), axis=0, keepdims=True)
    starts[...] = before.astype(jnp.int32) - 64
    weights[...] = queries([row_of(rows, r) for r in range(3, 6)])


def edges_kernel(way, core, keep, recv, *refs):
    outs = refs[-2:] if way > 0 else refs[-1:]
    half = HALO - BLOCK

    def write(first, second, late):
        width = WIDTH // len(outs)
        for part, out in enumerate(outs):
            cols = slice(part * width, (part + 1) * width)
            if late:
                out[:half, :] = first[BLOCK - half :, cols]
                out[half:, :] = second[:, cols]
            else:
                out[:BLOCK, :] = first[:, cols]
                out[BLOCK:, :] = second[:half, cols]

    @pl.when(core[0] == 0)
    def _():
        write(keep, recv, way > 0)

    @pl.when(core[0] != 0)
    def _():
        write(recv, keep, way < 0)


def call_edges(way, core, keep, recv, *after):
    return call(
        functools.partial(edges_kernel, way),
        [shape(HALO, PART, BF16)] * 2 if way > 0 else [shape(HALO, WIDTH, BF16)],
        [SMEM] + [VMEM] * (2 + len(after)),
        moved=2 << 20,
    )(core, keep, recv, *after)


def fold(value, op):
    rows, lanes = value.shape
    return op(value.reshape(rows // 8, 8, lanes), axis=0)


def relation_kernel(
    rel,
    core,
    starts,
    weights,
    loss_in,
    *refs,
):
    keep, recv, two, *one = refs[:-12]
    grad_left, grad_own, grad_right, loss_out, win, bias, rt, rs, gt, qs, bt, kg = refs[-12:]
    t_at, s_at, s_off = T_AT[rel], S_AT[rel], S_OFF[rel]
    me = core[0]

    def gather_all(*sources):
        at = 0
        for source in sources:
            t_source, s_source = source if isinstance(source, tuple) else (source, source)
            rows, width = t_source.shape
            win[at : at + rows, :TW] = t_source[:, t_at % width : t_at % width + TW]
            win[at : at + rows, TW:] = s_source[:, s_at : s_at + SP]
            at += rows

    one = (one[-1], one[0])

    @pl.when(me == 0)
    def _():
        gather_all(one, keep, recv, two)

    @pl.when(me != 0)
    def _():
        gather_all(two, recv, keep, one)

    key = lax.broadcasted_iota(jnp.int32, (WINDOW, OWN), 0)
    query = lax.broadcasted_iota(jnp.int32, (WINDOW, OWN), 1) + FIRST_QUERY
    bias[...] = jnp.where((key >= starts[...]) & (key <= query), 0.0, -1e30)

    lane = lax.broadcasted_iota(jnp.int32, (OWN, SP), 1)
    student = slice(TW, REL)
    row = lax.broadcasted_iota(jnp.int32, (SP, SP), 0)
    col = lax.broadcasted_iota(jnp.int32, (SP, SP), 1)
    unit = jnp.where(row == col, 1.0, 0.0).astype(BF16)
    bt[...] = lax.dot_general(unit, win[:, student], NT, preferred_element_type=F32).astype(BF16)

    gt[:BLOCK, :] = jnp.zeros((BLOCK, HEADS * OWN), BF16)
    gt[WINDOW - BLOCK :, :] = jnp.zeros((BLOCK, HEADS * OWN), BF16)
    step = 64
    tiles = [
        (
            slice(tile * BLOCK, (tile + 1) * BLOCK),
            [slice(at, at + step) for at in range(tile * BLOCK, SPAN + (tile + 1) * BLOCK, step)],
        )
        for tile in range(2)
    ]
    tops, sums = {}, {}
    totals = []

    def scores(head):
        start = head * DT // 128 * 128
        inside = (lane >= head * DT - start) & (lane < (head + 1) * DT - start)
        t_cols = slice(start, start + 256)
        t_query = win[FIRST_QUERY:, t_cols] * jnp.where(inside, 1.0, 0.0).astype(BF16)
        s_start = s_off + head * DS
        inside = (lane >= s_start) & (lane < s_start + DS)
        s_query = win[FIRST_QUERY:, student] * jnp.where(inside, 1.0, 0.0).astype(BF16)
        qs[head * OWN : (head + 1) * OWN, :] = s_query
        rt[head] = (
            lax.dot_general(win[:, t_cols], t_query, NT, preferred_element_type=F32) + bias[...]
        )
        rs[head] = (
            lax.dot_general(win[:, student], s_query, NT, preferred_element_type=F32) + bias[...]
        )

    def maxima(head):
        for tile, (lanes, parts) in enumerate(tiles):
            for z, r, scale in ((0, rt, CT), (1, rs, CS)):
                top = fold(r[head, parts[0], lanes], jnp.max)
                for part in parts[1:]:
                    top = jnp.maximum(top, fold(r[head, part, lanes], jnp.max))
                tops[head, tile, z] = jnp.max(top, axis=0, keepdims=True) * scale

    def exponentials(head):
        for tile, (lanes, parts) in enumerate(tiles):
            top_t, top_s = tops[head, tile, 0], tops[head, tile, 1]
            sum_t = jnp.zeros((8, BLOCK), F32)
            sum_s = jnp.zeros((8, BLOCK), F32)
            cross = jnp.zeros((8, BLOCK), F32)
            for part in parts:
                ut = rt[head, part, lanes] * CT - top_t
                us = rs[head, part, lanes] * CS - top_s
                et = jnp.exp2(ut)
                es = jnp.exp2(us)
                sum_t = sum_t + fold(et, jnp.sum)
                sum_s = sum_s + fold(es, jnp.sum)
                cross = cross + fold(et * (ut - us), jnp.sum)
                rt[head, part, lanes] = et
                rs[head, part, lanes] = es
            sum_t = jnp.sum(sum_t, axis=0, keepdims=True)
            sum_s = jnp.sum(sum_s, axis=0, keepdims=True)
            cross = jnp.sum(cross, axis=0, keepdims=True)
            weight = weights[:, lanes]
            totals.append(weight * (cross / sum_t - jnp.log2(sum_t) + jnp.log2(sum_s)))
            sums[head, tile] = weight * DS ** (-0.5) / sum_t, weight * DS ** (-0.5) / sum_s

    def gradients(head):
        for tile, (lanes, parts) in enumerate(tiles):
            scale_t, scale_s = sums[head, tile]
            g_cols = slice(head * OWN + tile * BLOCK, head * OWN + (tile + 1) * BLOCK)
            for part in parts:
                gt[part, g_cols] = (
                    rs[head, part, lanes] * scale_s - rt[head, part, lanes] * scale_t
                ).astype(BF16)

    row_grads = []

    def products(head):
        row_grads.append(
            jnp.dot(
                bt[s_off + head * DS : s_off + (head + 1) * DS, :],
                gt[:, head * OWN : (head + 1) * OWN],
                preferred_element_type=F32,
            )
        )

    def key_product(first, last):
        return jnp.dot(
            gt[:, first * OWN : last * OWN],
            qs[first * OWN : last * OWN, :],
            preferred_element_type=F32,
        )

    scores(0)
    scores(1)
    maxima(0)
    exponentials(0)
    scores(2)
    maxima(1)
    gradients(0)
    exponentials(1)
    products(0)
    scores(3)
    maxima(2)
    gradients(1)
    exponentials(2)
    products(1)
    kg[...] = key_product(0, 2)
    maxima(3)
    gradients(2)
    exponentials(3)
    products(2)
    gradients(3)
    products(3)
    key_grad = kg[...] + key_product(2, 4)
    loss_out[...] = loss_in[...] + functools.reduce(jnp.add, totals) * math.log(2.0)
    row_grads.insert(HEADS if s_off == 0 else 0, jnp.zeros((SP - SW, OWN), F32))
    row_grad = jnp.concatenate(row_grads, axis=0).T
    late = HALO + OWN - FIRST_QUERY
    grad_left[...] = key_grad[:HALO].astype(BF16)
    grad_own[: OWN - late, :] = key_grad[HALO:FIRST_QUERY]
    grad_own[OWN - late :, :] = key_grad[FIRST_QUERY : HALO + OWN] + row_grad[:late]
    grad_right[...] = (key_grad[HALO + OWN :] + row_grad[late:]).astype(BF16)


def join_kernel(core, loss, l0, l1, l2, r0, r1, r2, one, two, copies):
    copies[...] = jnp.broadcast_to(loss[...], copies.shape)

    def write(after, before):
        for rel, (left, right) in enumerate(((l0, r0), (l1, r1), (l2, r2))):
            before[:, rel * SP : (rel + 1) * SP] = left[...]
            after[:, rel * SP : (rel + 1) * SP] = right[...]

    @pl.when(core[0] == 0)
    def _():
        write(one, two)

    @pl.when(core[0] != 0)
    def _():
        write(two, one)


def merge_kernel(core, parts, o0, o1, o2, mine, other, keep, send, copies):
    copies[...] = jnp.broadcast_to(jnp.sum(parts[...], axis=0, keepdims=True), copies.shape)
    half = HALO - BLOCK
    for rel, own in enumerate((o0, o1, o2)):
        cols = slice(rel * SP, (rel + 1) * SP)

        @pl.when(core[0] == 0)
        def _():
            keep[:BLOCK, cols] = own[:BLOCK, :] + mine[:BLOCK, cols].astype(F32)
            keep[BLOCK:, cols] = other[:BLOCK, cols].astype(F32)
            send[:half, cols] = own[BLOCK : BLOCK + half, :] + mine[BLOCK:, cols].astype(F32)
            send[half:BLOCK, cols] = own[BLOCK + half :, :]
            send[BLOCK:, cols] = other[BLOCK:, cols].astype(F32)

        @pl.when(core[0] != 0)
        def _():
            keep[:BLOCK, cols] = own[BLOCK:, :] + mine[half:, cols].astype(F32)
            keep[BLOCK:, cols] = other[half:, cols].astype(F32)
            send[: BLOCK - half, cols] = own[: BLOCK - half, :]
            send[BLOCK - half : BLOCK, cols] = own[BLOCK - half : BLOCK, :] + mine[
                :half, cols
            ].astype(F32)
            send[BLOCK:, cols] = other[:half, cols].astype(F32)


def place_kernel(tokens, core, parts, keep, recv, oq, ok, ov, loss):
    me = core[0]
    total = jnp.sum(jnp.sum(parts[...], axis=0, keepdims=True), axis=1, keepdims=True)
    loss[...] = total * (1.0 / (3 * H * tokens))
    half = HALO - BLOCK
    empty = jnp.zeros((BLOCK, 2 * SW - SP), F32)
    gap = jnp.zeros((BLOCK - half, SP), F32)
    for rel, out in enumerate((oq, ok, ov)):
        cols = slice(rel * SP, (rel + 1) * SP)
        late = recv[BLOCK:, cols]
        first = jnp.concatenate([late, gap], axis=0)
        last = jnp.concatenate([gap, late], axis=0)
        ours = keep[:BLOCK, cols] + jnp.where(me == 0, last, first)
        theirs = keep[BLOCK:, cols] + recv[:BLOCK, cols]
        ours = jnp.concatenate([ours, empty], axis=1)
        theirs = jnp.concatenate([theirs, empty], axis=1)
        low = jnp.where(me == 0, ours, theirs)
        high = jnp.where(me == 0, theirs, ours)
        off = S_OFF[rel]
        if off:
            low = pltpu.roll(low, 2 * SW - off, 1)
        out[...] = low + pltpu.roll(high, SW - off, 1)


def shape(rows, cols, dtype):
    return jax.ShapeDtypeStruct((rows, cols), dtype)


def call_relation(rel, core, starts, weight, loss, chunk):
    return call(
        functools.partial(relation_kernel, rel),
        [
            shape(HALO, SP, BF16),
            shape(OWN, SP, F32),
            shape(HALO, SP, BF16),
            shape(1, BLOCK, F32),
        ],
        [SMEM] + [VMEM] * (3 + len(chunk)),
        scratch=[
            pltpu.VMEM((WINDOW, REL), BF16),
            pltpu.VMEM((WINDOW, OWN), F32),
            pltpu.VMEM((HEADS, WINDOW, OWN), F32),
            pltpu.VMEM((HEADS, WINDOW, OWN), F32),
            pltpu.VMEM((WINDOW, HEADS * OWN), BF16),
            pltpu.VMEM((HEADS * OWN, SP), BF16),
            pltpu.VMEM((SP, WINDOW), BF16),
            pltpu.VMEM((WINDOW, SP), F32),
        ],
        flops=2 * 16 * WINDOW * OWN * 256,
        moved=2 << 20,
        exps=2 * HEADS * WINDOW * OWN,
        limit=20,
    )(core, starts, weight, loss, *chunk)


def body(teacher_q, teacher_k, teacher_v, student_q, student_k, student_v, doc_ids, row_weight):
    tok = ("y", "z", "parity", "core")
    count = lax.axis_size(tok)
    core = lax.axis_index("core").astype(jnp.int32).reshape(1)
    chip = lax.axis_index(("y", "z", "parity"))

    def other_core(value):
        return lax.ppermute(value, "core", [(0, 1), (1, 0)])

    def neighbours(value, way, cross=0):
        step = (2 * way, -2 * way)
        pairs = [(i, ((i + step[i % 2]) % count) ^ cross) for i in range(count)]
        return lax.ppermute(value, tok, pairs)

    arrays = (teacher_q, teacher_k, teacher_v, student_q, student_k, student_v)
    send, keep = call(
        split_kernel,
        [shape(BLOCK, WIDTH, BF16)] * 2,
        [SMEM] + [HBM] * 6,
        scratch=[pltpu.VMEM(a.shape, BF16) for a in arrays] + [pltpu.SemaphoreType.DMA((6,))],
        moved=4 << 20,
        limit=56,
    )(core, *arrays)
    recv = other_core(send)
    (edges,) = call_edges(-1, core, keep, recv)
    two = neighbours(edges, -1)
    doc_ids, row_weight, _ = lax.optimization_barrier((doc_ids, row_weight, edges))
    starts, weight = call(
        mask_kernel,
        [shape(1, OWN, jnp.int32), shape(1, OWN, F32)],
        [SMEM] + [VMEM] * 2,
        moved=1 << 17,
    )(
        chip.astype(jnp.int32).reshape(1),
        doc_ids.reshape(-1, BLOCK),
        row_weight.reshape(-1, BLOCK),
    )
    one = [neighbours(edge, 1) for edge in call_edges(1, core, keep, recv, weight)]
    loss = jnp.zeros((1, BLOCK), F32)
    grads = []
    for rel in range(3):
        chunk = (keep, recv, two, *(one if rel else one[:1]))
        *grad, loss = call_relation(rel, core, starts, weight, loss, chunk)
        grads.append(grad)

    stages = (("z", "parity", "core"), ("y", "head"))
    copies = [shape(lax.axis_size(axes), BLOCK, F32) for axes in stages]

    def exchange(value, axes):
        return lax.all_to_all(value, axes, 0, 0, tiled=True)

    one, two, parts = call(
        join_kernel,
        [shape(HALO, 3 * SP, BF16)] * 2 + [copies[0]],
        [SMEM] + [VMEM] * 7,
        moved=1 << 20,
    )(core, loss, *(g[0] for g in grads), *(g[2] for g in grads))
    one = neighbours(one, 1)
    two = neighbours(two, -1, 1)
    parts = exchange(parts, stages[0])
    kept, sent, parts = call(
        merge_kernel,
        [shape(OWN, 3 * SP, F32), shape(HALO, 3 * SP, F32), copies[1]],
        [SMEM] + [VMEM] * 6,
        moved=2 << 20,
    )(core, parts, *(g[1] for g in grads), one, two)
    received = other_core(sent)
    parts = exchange(parts, stages[1])
    grad_q, grad_k, grad_v, loss = call(
        functools.partial(place_kernel, doc_ids.shape[0]),
        [shape(BLOCK, 2 * SW, F32)] * 3 + [shape(1, 1, F32)],
        [SMEM] + [VMEM] * 3,
        moved=1 << 20,
    )(core, parts, kept, received)
    return grad_q, grad_k, grad_v, loss[0, 0]


def solution(mesh):
    tok, head = mesh.devices.shape
    z = 4 if tok == 128 else 1
    axes = ("y", "z", "parity", "core", "head")
    fine = Mesh(mesh.devices.reshape(tok // (4 * z), z, 2, 2, head), axes)
    rows = axes[:4]
    placed = (P(rows, "head"),) * 6 + (P(), P())
    return jax.shard_map(
        body,
        mesh=fine,
        in_specs=placed,
        out_specs=(P(rows, "head"),) * 3 + (P(),),
        check_vma=False,
    )
```

```python
import functools
import math

import jax
import jax.numpy as jnp
from jax import lax
from jax.experimental import pallas as pl
from jax.experimental.pallas import tpu as pltpu
from jax.sharding import Mesh
from jax.sharding import PartitionSpec as P

H = 32
DT = 160
DS = 48
SPAN = 384

BLOCK = 128
OWN = 2 * BLOCK
HALO = 192
WINDOW = OWN + 2 * HALO
FIRST_QUERY = WINDOW - OWN
HEADS = 4
TW = HEADS * DT
SW = HEADS * DS
SP = 256
REL = TW + SP
PART = 2 * TW
WIDTH = 2 * PART
T_AT = (0, PART, PART + TW)
S_AT = (TW, TW + SP, TW + SP + 128)
S_OFF = (0, 0, SW - 128)
CT = DT ** (-0.5) * math.log2(math.e)
CS = DS ** (-0.5) * math.log2(math.e)
NT = (((1,), (1,)), ((), ()))
FAR = 4096
VMEM = pl.BlockSpec(memory_space=pltpu.VMEM)
SMEM = pl.BlockSpec(memory_space=pltpu.SMEM)
HBM = pl.BlockSpec(memory_space=pltpu.HBM)
F32 = jnp.float32
BF16 = jnp.bfloat16


def call(kernel, out_shape, in_specs, scratch=(), flops=0, moved=0, exps=0, limit=8):
    return pl.pallas_call(
        kernel,
        out_shape=out_shape,
        in_specs=in_specs,
        out_specs=jax.tree.map(lambda _: VMEM, out_shape),
        scratch_shapes=list(scratch),
        compiler_params=pltpu.CompilerParams(vmem_limit_bytes=limit << 20),
        cost_estimate=pl.CostEstimate(flops=flops, bytes_accessed=moved, transcendentals=exps),
    )


def split_kernel(core, *refs):
    arrays, (send, keep), buffers, sems = refs[:6], refs[6:8], refs[8:14], refs[14]
    me = core[0]
    copies = [
        pltpu.make_async_copy(array, buffer, sems.at[i])
        for i, (array, buffer) in enumerate(zip(arrays, buffers))
    ]
    for copy in copies:
        copy.start()
    for copy in copies:
        copy.wait()
    lane = lax.broadcasted_iota(jnp.int32, (BLOCK, SP), 1)
    mine = pl.ds(pl.multiple_of(me * TW, 128), TW)
    other = pl.ds(pl.multiple_of((1 - me) * TW, 128), TW)
    ours, theirs = [], []
    for rel in range(3):
        teacher, student = buffers[rel], buffers[3 + rel]
        at = T_AT[rel]
        keep[:, at : at + TW] = teacher[:, mine]
        send[:, at : at + TW] = teacher[:, other]
        low = jnp.where(lane < SW, student[:, :SP].astype(F32), 0.0)
        high = pltpu.roll(student[:, 128:].astype(F32), SP - (SW - 128), 1)
        high = jnp.where(lane < SW, high, 0.0)
        ours.append(jnp.where(me == 0, low, high))
        theirs.append(jnp.where(me == 0, high, low))
    for halves, out in ((ours, keep), (theirs, send)):
        out[:, TW : TW + SP] = halves[0].astype(BF16)
        second = pltpu.roll(halves[2], S_OFF[2], 1)
        at = S_AT[1]
        out[:, at : at + 128] = halves[1][:, :128].astype(BF16)
        out[:, at + 128 : at + 256] = (halves[1][:, 128:] + second[:, :128]).astype(BF16)
        out[:, at + 256 : at + 384] = second[:, 128:].astype(BF16)


def mask_kernel(chip, docs, rows, starts, weights):
    count = docs.shape[0]
    first = 2 * chip[0] - 2

    def row_of(ref, r):
        at = first + r
        return ref[pl.ds(lax.rem(at + count, count), 1), :]

    lines = []
    for r in range(6):
        at = first + r
        shift = jnp.where(at < 0, -FAR, jnp.where(at >= count, FAR, 0))
        lines.append((row_of(docs, r) + shift).astype(F32))

    def queries(parts):
        joined = jnp.broadcast_to(jnp.concatenate(parts, axis=1), (8, 3 * BLOCK))
        return pltpu.roll(joined, 2 * BLOCK + 64, 1)[:1, :OWN]

    query = queries(lines[3:])
    before = jnp.zeros((1, OWN), F32)
    for line in lines:
        keys = jnp.broadcast_to(line, (BLOCK, BLOCK)).T
        keys = jnp.concatenate([keys, keys], axis=1)
        before = before + jnp.sum(jnp.where(keys < query, 1.0, 0.0), axis=0, keepdims=True)
    starts[...] = before.astype(jnp.int32) - 64
    weights[...] = queries([row_of(rows, r) for r in range(3, 6)])


def edges_kernel(way, core, keep, recv, *refs):
    outs = refs[-2:]
    half = HALO - BLOCK

    def write(first, second, late):
        for part, out in enumerate(outs):
            cols = slice(part * PART, (part + 1) * PART)
            if late:
                out[:half, :] = first[BLOCK - half :, cols]
                out[half:, :] = second[:, cols]
            else:
                out[:BLOCK, :] = first[:, cols]
                out[BLOCK:, :] = second[:half, cols]

    @pl.when(core[0] == 0)
    def _():
        write(keep, recv, way > 0)

    @pl.when(core[0] != 0)
    def _():
        write(recv, keep, way < 0)


def call_edges(way, core, keep, recv, *after):
    return call(
        functools.partial(edges_kernel, way),
        [shape(HALO, PART, BF16)] * 2,
        [SMEM] + [VMEM] * (2 + len(after)),
        moved=2 << 20,
    )(core, keep, recv, *after)


def fold(value, op):
    rows, lanes = value.shape
    return op(value.reshape(rows // 8, 8, lanes), axis=0)


def relation_kernel(
    rel,
    core,
    starts,
    weights,
    loss_in,
    *refs,
):
    keep, recv, *halo = refs[:-12]
    grad_left, grad_own, grad_right, loss_out, win, bias, rt, rs, gt, qs, bt, kg = refs[-12:]
    t_at, s_at, s_off = T_AT[rel], S_AT[rel], S_OFF[rel]
    me = core[0]

    def gather_all(*sources):
        at = 0
        for source in sources:
            t_source, s_source = source if isinstance(source, tuple) else (source, source)
            rows, width = t_source.shape
            win[at : at + rows, :TW] = t_source[:, t_at % width : t_at % width + TW]
            win[at : at + rows, TW:] = s_source[:, s_at : s_at + SP]
            at += rows

    two, one = (halo[1 if rel else 0], halo[0]), (halo[-1], halo[2])

    @pl.when(me == 0)
    def _():
        gather_all(one, keep, recv, two)

    @pl.when(me != 0)
    def _():
        gather_all(two, recv, keep, one)

    key = lax.broadcasted_iota(jnp.int32, (WINDOW, OWN), 0)
    query = lax.broadcasted_iota(jnp.int32, (WINDOW, OWN), 1) + FIRST_QUERY
    bias[...] = jnp.where((key >= starts[...]) & (key <= query), 0.0, -1e30)

    lane = lax.broadcasted_iota(jnp.int32, (OWN, SP), 1)
    student = slice(TW, REL)
    row = lax.broadcasted_iota(jnp.int32, (SP, SP), 0)
    col = lax.broadcasted_iota(jnp.int32, (SP, SP), 1)
    unit = jnp.where(row == col, 1.0, 0.0).astype(BF16)
    bt[...] = lax.dot_general(unit, win[:, student], NT, preferred_element_type=F32).astype(BF16)

    gt[:BLOCK, :] = jnp.zeros((BLOCK, HEADS * OWN), BF16)
    gt[WINDOW - BLOCK :, :] = jnp.zeros((BLOCK, HEADS * OWN), BF16)
    step = 64
    tiles = [
        (
            slice(tile * BLOCK, (tile + 1) * BLOCK),
            [slice(at, at + step) for at in range(tile * BLOCK, SPAN + (tile + 1) * BLOCK, step)],
        )
        for tile in range(2)
    ]
    tops, sums = {}, {}
    totals = []

    def scores(head):
        start = head * DT // 128 * 128
        inside = (lane >= head * DT - start) & (lane < (head + 1) * DT - start)
        t_cols = slice(start, start + 256)
        t_query = win[FIRST_QUERY:, t_cols] * jnp.where(inside, 1.0, 0.0).astype(BF16)
        s_start = s_off + head * DS
        inside = (lane >= s_start) & (lane < s_start + DS)
        s_query = win[FIRST_QUERY:, student] * jnp.where(inside, 1.0, 0.0).astype(BF16)
        qs[head * OWN : (head + 1) * OWN, :] = s_query
        rt[head] = (
            lax.dot_general(win[:, t_cols], t_query, NT, preferred_element_type=F32) + bias[...]
        )
        rs[head] = (
            lax.dot_general(win[:, student], s_query, NT, preferred_element_type=F32) + bias[...]
        )

    def maxima(head):
        for tile, (lanes, parts) in enumerate(tiles):
            for z, r, scale in ((0, rt, CT), (1, rs, CS)):
                top = fold(r[head, parts[0], lanes], jnp.max)
                for part in parts[1:]:
                    top = jnp.maximum(top, fold(r[head, part, lanes], jnp.max))
                tops[head, tile, z] = jnp.max(top, axis=0, keepdims=True) * scale

    def exponentials(head):
        for tile, (lanes, parts) in enumerate(tiles):
            top_t, top_s = tops[head, tile, 0], tops[head, tile, 1]
            sum_t = jnp.zeros((8, BLOCK), F32)
            sum_s = jnp.zeros((8, BLOCK), F32)
            cross = jnp.zeros((8, BLOCK), F32)
            for part in parts:
                ut = rt[head, part, lanes] * CT - top_t
                us = rs[head, part, lanes] * CS - top_s
                et = jnp.exp2(ut)
                es = jnp.exp2(us)
                sum_t = sum_t + fold(et, jnp.sum)
                sum_s = sum_s + fold(es, jnp.sum)
                cross = cross + fold(et * (ut - us), jnp.sum)
                rt[head, part, lanes] = et
                rs[head, part, lanes] = es
            sum_t = jnp.sum(sum_t, axis=0, keepdims=True)
            sum_s = jnp.sum(sum_s, axis=0, keepdims=True)
            cross = jnp.sum(cross, axis=0, keepdims=True)
            weight = weights[:, lanes]
            totals.append(weight * (cross / sum_t - jnp.log2(sum_t) + jnp.log2(sum_s)))
            sums[head, tile] = weight * DS ** (-0.5) / sum_t, weight * DS ** (-0.5) / sum_s

    def gradients(head):
        for tile, (lanes, parts) in enumerate(tiles):
            scale_t, scale_s = sums[head, tile]
            g_cols = slice(head * OWN + tile * BLOCK, head * OWN + (tile + 1) * BLOCK)
            for part in parts:
                gt[part, g_cols] = (
                    rs[head, part, lanes] * scale_s - rt[head, part, lanes] * scale_t
                ).astype(BF16)

    row_grads = []

    def products(head):
        row_grads.append(
            jnp.dot(
                bt[s_off + head * DS : s_off + (head + 1) * DS, :],
                gt[:, head * OWN : (head + 1) * OWN],
                preferred_element_type=F32,
            )
        )

    def key_product(first, last):
        return jnp.dot(
            gt[:, first * OWN : last * OWN],
            qs[first * OWN : last * OWN, :],
            preferred_element_type=F32,
        )

    scores(0)
    scores(1)
    maxima(0)
    exponentials(0)
    scores(2)
    maxima(1)
    gradients(0)
    exponentials(1)
    products(0)
    scores(3)
    maxima(2)
    gradients(1)
    exponentials(2)
    products(1)
    kg[...] = key_product(0, 2)
    maxima(3)
    gradients(2)
    exponentials(3)
    products(2)
    gradients(3)
    products(3)
    key_grad = kg[...] + key_product(2, 4)
    loss_out[...] = loss_in[...] + functools.reduce(jnp.add, totals) * math.log(2.0)
    row_grads.insert(HEADS if s_off == 0 else 0, jnp.zeros((SP - SW, OWN), F32))
    row_grad = jnp.concatenate(row_grads, axis=0).T
    late = HALO + OWN - FIRST_QUERY
    grad_left[...] = key_grad[:HALO].astype(BF16)
    grad_own[: OWN - late, :] = key_grad[HALO:FIRST_QUERY]
    grad_own[OWN - late :, :] = key_grad[FIRST_QUERY : HALO + OWN] + row_grad[:late]
    grad_right[...] = (key_grad[HALO + OWN :] + row_grad[late:]).astype(BF16)


def join_kernel(core, loss, l0, l1, l2, r0, r1, r2, one, two, copies):
    copies[...] = jnp.broadcast_to(loss[...], copies.shape)

    def write(after, before):
        for rel, (left, right) in enumerate(((l0, r0), (l1, r1), (l2, r2))):
            before[:, rel * SP : (rel + 1) * SP] = left[...]
            after[:, rel * SP : (rel + 1) * SP] = right[...]

    @pl.when(core[0] == 0)
    def _():
        write(one, two)

    @pl.when(core[0] != 0)
    def _():
        write(two, one)


def merge_kernel(core, parts, o0, o1, o2, mine, other, keep, send, copies):
    copies[...] = jnp.broadcast_to(jnp.sum(parts[...], axis=0, keepdims=True), copies.shape)
    half = HALO - BLOCK
    for rel, own in enumerate((o0, o1, o2)):
        cols = slice(rel * SP, (rel + 1) * SP)

        @pl.when(core[0] == 0)
        def _():
            keep[:BLOCK, cols] = own[:BLOCK, :] + mine[:BLOCK, cols].astype(F32)
            keep[BLOCK:, cols] = other[:BLOCK, cols].astype(F32)
            send[:half, cols] = own[BLOCK : BLOCK + half, :] + mine[BLOCK:, cols].astype(F32)
            send[half:BLOCK, cols] = own[BLOCK + half :, :]
            send[BLOCK:, cols] = other[BLOCK:, cols].astype(F32)

        @pl.when(core[0] != 0)
        def _():
            keep[:BLOCK, cols] = own[BLOCK:, :] + mine[half:, cols].astype(F32)
            keep[BLOCK:, cols] = other[half:, cols].astype(F32)
            send[: BLOCK - half, cols] = own[: BLOCK - half, :]
            send[BLOCK - half : BLOCK, cols] = own[BLOCK - half : BLOCK, :] + mine[
                :half, cols
            ].astype(F32)
            send[BLOCK:, cols] = other[:half, cols].astype(F32)


def place_kernel(tokens, core, parts, keep, recv, oq, ok, ov, loss):
    me = core[0]
    total = jnp.sum(jnp.sum(parts[...], axis=0, keepdims=True), axis=1, keepdims=True)
    loss[...] = total * (1.0 / (3 * H * tokens))
    half = HALO - BLOCK
    empty = jnp.zeros((BLOCK, 2 * SW - SP), F32)
    gap = jnp.zeros((BLOCK - half, SP), F32)
    for rel, out in enumerate((oq, ok, ov)):
        cols = slice(rel * SP, (rel + 1) * SP)
        late = recv[BLOCK:, cols]
        first = jnp.concatenate([late, gap], axis=0)
        last = jnp.concatenate([gap, late], axis=0)
        ours = keep[:BLOCK, cols] + jnp.where(me == 0, last, first)
        theirs = keep[BLOCK:, cols] + recv[:BLOCK, cols]
        ours = jnp.concatenate([ours, empty], axis=1)
        theirs = jnp.concatenate([theirs, empty], axis=1)
        low = jnp.where(me == 0, ours, theirs)
        high = jnp.where(me == 0, theirs, ours)
        off = S_OFF[rel]
        if off:
            low = pltpu.roll(low, 2 * SW - off, 1)
        out[...] = low + pltpu.roll(high, SW - off, 1)


def shape(rows, cols, dtype):
    return jax.ShapeDtypeStruct((rows, cols), dtype)


def call_relation(rel, core, starts, weight, loss, chunk):
    return call(
        functools.partial(relation_kernel, rel),
        [
            shape(HALO, SP, BF16),
            shape(OWN, SP, F32),
            shape(HALO, SP, BF16),
            shape(1, BLOCK, F32),
        ],
        [SMEM] + [VMEM] * (3 + len(chunk)),
        scratch=[
            pltpu.VMEM((WINDOW, REL), BF16),
            pltpu.VMEM((WINDOW, OWN), F32),
            pltpu.VMEM((HEADS, WINDOW, OWN), F32),
            pltpu.VMEM((HEADS, WINDOW, OWN), F32),
            pltpu.VMEM((WINDOW, HEADS * OWN), BF16),
            pltpu.VMEM((HEADS * OWN, SP), BF16),
            pltpu.VMEM((SP, WINDOW), BF16),
            pltpu.VMEM((WINDOW, SP), F32),
        ],
        flops=2 * 16 * WINDOW * OWN * 256,
        moved=2 << 20,
        exps=2 * HEADS * WINDOW * OWN,
        limit=20,
    )(core, starts, weight, loss, *chunk)


def body(teacher_q, teacher_k, teacher_v, student_q, student_k, student_v, doc_ids, row_weight):
    tok = ("y", "z", "parity", "core")
    count = lax.axis_size(tok)
    core = lax.axis_index("core").astype(jnp.int32).reshape(1)
    chip = lax.axis_index(("y", "z", "parity"))

    def other_core(value):
        return lax.ppermute(value, "core", [(0, 1), (1, 0)])

    def neighbours(value, way, cross=0):
        step = (2 * way, -2 * way)
        pairs = [(i, ((i + step[i % 2]) % count) ^ cross) for i in range(count)]
        return lax.ppermute(value, tok, pairs)

    arrays = (teacher_q, teacher_k, teacher_v, student_q, student_k, student_v)
    send, keep = call(
        split_kernel,
        [shape(BLOCK, WIDTH, BF16)] * 2,
        [SMEM] + [HBM] * 6,
        scratch=[pltpu.VMEM(a.shape, BF16) for a in arrays] + [pltpu.SemaphoreType.DMA((6,))],
        moved=4 << 20,
        limit=56,
    )(core, *arrays)
    recv = other_core(send)
    edges = call_edges(-1, core, keep, recv)
    two = [neighbours(edge, -1) for edge in edges]
    doc_ids, row_weight, _ = lax.optimization_barrier((doc_ids, row_weight, edges[0]))
    starts, weight = call(
        mask_kernel,
        [shape(1, OWN, jnp.int32), shape(1, OWN, F32)],
        [SMEM] + [VMEM] * 2,
        moved=1 << 17,
    )(
        chip.astype(jnp.int32).reshape(1),
        doc_ids.reshape(-1, BLOCK),
        row_weight.reshape(-1, BLOCK),
    )
    one = [neighbours(edge, 1) for edge in call_edges(1, core, keep, recv, weight)]
    loss = jnp.zeros((1, BLOCK), F32)
    grads = []
    for rel in range(3):
        chunk = (keep, recv, *two, *(one if rel else one[:1]))
        *grad, loss = call_relation(rel, core, starts, weight, loss, chunk)
        grads.append(grad)

    stages = (("z", "parity", "core"), ("y", "head"))
    copies = [shape(lax.axis_size(axes), BLOCK, F32) for axes in stages]

    def exchange(value, axes):
        return lax.all_to_all(value, axes, 0, 0, tiled=True)

    one, two, parts = call(
        join_kernel,
        [shape(HALO, 3 * SP, BF16)] * 2 + [copies[0]],
        [SMEM] + [VMEM] * 7,
        moved=1 << 20,
    )(core, loss, *(g[0] for g in grads), *(g[2] for g in grads))
    one = neighbours(one, 1)
    two = neighbours(two, -1, 1)
    parts = exchange(parts, stages[0])
    kept, sent, parts = call(
        merge_kernel,
        [shape(OWN, 3 * SP, F32), shape(HALO, 3 * SP, F32), copies[1]],
        [SMEM] + [VMEM] * 6,
        moved=2 << 20,
    )(core, parts, *(g[1] for g in grads), one, two)
    received = other_core(sent)
    parts = exchange(parts, stages[1])
    grad_q, grad_k, grad_v, loss = call(
        functools.partial(place_kernel, doc_ids.shape[0]),
        [shape(BLOCK, 2 * SW, F32)] * 3 + [shape(1, 1, F32)],
        [SMEM] + [VMEM] * 3,
        moved=1 << 20,
    )(core, parts, kept, received)
    return grad_q, grad_k, grad_v, loss[0, 0]


def solution(mesh):
    tok, head = mesh.devices.shape
    z = 4 if tok == 128 else 1
    axes = ("y", "z", "parity", "core", "head")
    fine = Mesh(mesh.devices.reshape(tok // (4 * z), z, 2, 2, head), axes)
    rows = axes[:4]
    placed = (P(rows, "head"),) * 6 + (P(), P())
    return jax.shard_map(
        body,
        mesh=fine,
        in_specs=placed,
        out_specs=(P(rows, "head"),) * 3 + (P(),),
        check_vma=False,
    )
```

```python
import functools
import math

import jax
import jax.numpy as jnp
from jax import lax
from jax.experimental import pallas as pl
from jax.experimental.pallas import tpu as pltpu
from jax.sharding import Mesh
from jax.sharding import PartitionSpec as P

H = 32
DT = 160
DS = 48
SPAN = 384

BLOCK = 128
OWN = 2 * BLOCK
HALO = 192
WINDOW = OWN + 2 * HALO
FIRST_QUERY = WINDOW - OWN
HEADS = 4
TW = HEADS * DT
SW = HEADS * DS
SP = 256
REL = TW + SP
PART = 2 * TW
WIDTH = 2 * PART
T_AT = (0, PART, PART + TW)
S_AT = (TW, TW + SP, TW + SP + 128)
S_OFF = (0, 0, SW - 128)
CT = DT ** (-0.5) * math.log2(math.e)
CS = DS ** (-0.5) * math.log2(math.e)
NT = (((1,), (1,)), ((), ()))
FAR = 4096
VMEM = pl.BlockSpec(memory_space=pltpu.VMEM)
SMEM = pl.BlockSpec(memory_space=pltpu.SMEM)
HBM = pl.BlockSpec(memory_space=pltpu.HBM)
F32 = jnp.float32
BF16 = jnp.bfloat16


def call(kernel, out_shape, in_specs, scratch=(), flops=0, moved=0, exps=0, limit=8):
    return pl.pallas_call(
        kernel,
        out_shape=out_shape,
        in_specs=in_specs,
        out_specs=jax.tree.map(lambda _: VMEM, out_shape),
        scratch_shapes=list(scratch),
        compiler_params=pltpu.CompilerParams(vmem_limit_bytes=limit << 20),
        cost_estimate=pl.CostEstimate(flops=flops, bytes_accessed=moved, transcendentals=exps),
    )


def split_kernel(own, core, *refs):
    arrays, out, buffers, sems = refs[:6], refs[-8], refs[-7:-1], refs[-1]
    which = core[0] if own else 1 - core[0]
    copies = [
        pltpu.make_async_copy(array, buffer, sems.at[i])
        for i, (array, buffer) in enumerate(zip(arrays, buffers))
    ]
    for copy in copies:
        copy.start()
    for copy in copies:
        copy.wait()
    lane = lax.broadcasted_iota(jnp.int32, (BLOCK, SP), 1)
    cols = pl.ds(pl.multiple_of(which * TW, 128), TW)
    halves = []
    for rel in range(3):
        teacher, student = buffers[rel], buffers[3 + rel]
        at = T_AT[rel]
        out[:, at : at + TW] = teacher[:, cols]
        low = jnp.where(lane < SW, student[:, :SP].astype(F32), 0.0)
        high = pltpu.roll(student[:, 128:].astype(F32), SP - (SW - 128), 1)
        high = jnp.where(lane < SW, high, 0.0)
        halves.append(jnp.where(which == 0, low, high))
    out[:, TW : TW + SP] = halves[0].astype(BF16)
    second = pltpu.roll(halves[2], S_OFF[2], 1)
    at = S_AT[1]
    out[:, at : at + 128] = halves[1][:, :128].astype(BF16)
    out[:, at + 128 : at + 256] = (halves[1][:, 128:] + second[:, :128]).astype(BF16)
    out[:, at + 256 : at + 384] = second[:, 128:].astype(BF16)


def mask_kernel(chip, docs, rows, starts, weights):
    count = docs.shape[0]
    first = 2 * chip[0] - 2

    def row_of(ref, r):
        at = first + r
        return ref[pl.ds(lax.rem(at + count, count), 1), :]

    lines = []
    for r in range(6):
        at = first + r
        shift = jnp.where(at < 0, -FAR, jnp.where(at >= count, FAR, 0))
        lines.append((row_of(docs, r) + shift).astype(F32))

    def queries(parts):
        joined = jnp.broadcast_to(jnp.concatenate(parts, axis=1), (8, 3 * BLOCK))
        return pltpu.roll(joined, 2 * BLOCK + 64, 1)[:1, :OWN]

    query = queries(lines[3:])
    before = jnp.zeros((1, OWN), F32)
    for line in lines:
        keys = jnp.broadcast_to(line, (BLOCK, BLOCK)).T
        keys = jnp.concatenate([keys, keys], axis=1)
        before = before + jnp.sum(jnp.where(keys < query, 1.0, 0.0), axis=0, keepdims=True)
    starts[...] = before.astype(jnp.int32) - 64
    weights[...] = queries([row_of(rows, r) for r in range(3, 6)])


def edges_kernel(way, core, keep, recv, *refs):
    outs = refs[-2:]
    half = HALO - BLOCK

    def write(first, second, late):
        for part, out in enumerate(outs):
            cols = slice(part * PART, (part + 1) * PART)
            if late:
                out[:half, :] = first[BLOCK - half :, cols]
                out[half:, :] = second[:, cols]
            else:
                out[:BLOCK, :] = first[:, cols]
                out[BLOCK:, :] = second[:half, cols]

    @pl.when(core[0] == 0)
    def _():
        write(keep, recv, way > 0)

    @pl.when(core[0] != 0)
    def _():
        write(recv, keep, way < 0)


def call_edges(way, core, keep, recv, *after):
    return call(
        functools.partial(edges_kernel, way),
        [shape(HALO, PART, BF16)] * 2,
        [SMEM] + [VMEM] * (2 + len(after)),
        moved=2 << 20,
    )(core, keep, recv, *after)


def fold(value, op):
    rows, lanes = value.shape
    return op(value.reshape(rows // 8, 8, lanes), axis=0)


def relation_kernel(
    rel,
    core,
    starts,
    weights,
    loss_in,
    *refs,
):
    keep, recv, *halo = refs[:-12]
    grad_left, grad_own, grad_right, loss_out, win, bias, rt, rs, gt, qs, bt, kg = refs[-12:]
    t_at, s_at, s_off = T_AT[rel], S_AT[rel], S_OFF[rel]
    me = core[0]

    def gather_all(*sources):
        at = 0
        for source in sources:
            t_source, s_source = source if isinstance(source, tuple) else (source, source)
            rows, width = t_source.shape
            win[at : at + rows, :TW] = t_source[:, t_at % width : t_at % width + TW]
            win[at : at + rows, TW:] = s_source[:, s_at : s_at + SP]
            at += rows

    two, one = (halo[1 if rel else 0], halo[0]), (halo[-1], halo[2])

    @pl.when(me == 0)
    def _():
        gather_all(one, keep, recv, two)

    @pl.when(me != 0)
    def _():
        gather_all(two, recv, keep, one)

    key = lax.broadcasted_iota(jnp.int32, (WINDOW, OWN), 0)
    query = lax.broadcasted_iota(jnp.int32, (WINDOW, OWN), 1) + FIRST_QUERY
    bias[...] = jnp.where((key >= starts[...]) & (key <= query), 0.0, -1e30)

    lane = lax.broadcasted_iota(jnp.int32, (OWN, SP), 1)
    student = slice(TW, REL)
    row = lax.broadcasted_iota(jnp.int32, (SP, SP), 0)
    col = lax.broadcasted_iota(jnp.int32, (SP, SP), 1)
    unit = jnp.where(row == col, 1.0, 0.0).astype(BF16)
    bt[...] = lax.dot_general(unit, win[:, student], NT, preferred_element_type=F32).astype(BF16)

    gt[:BLOCK, :] = jnp.zeros((BLOCK, HEADS * OWN), BF16)
    gt[WINDOW - BLOCK :, :] = jnp.zeros((BLOCK, HEADS * OWN), BF16)
    step = 64
    tiles = [
        (
            slice(tile * BLOCK, (tile + 1) * BLOCK),
            [slice(at, at + step) for at in range(tile * BLOCK, SPAN + (tile + 1) * BLOCK, step)],
        )
        for tile in range(2)
    ]
    tops, sums = {}, {}
    totals = []

    def scores(head):
        start = head * DT // 128 * 128
        inside = (lane >= head * DT - start) & (lane < (head + 1) * DT - start)
        t_cols = slice(start, start + 256)
        t_query = win[FIRST_QUERY:, t_cols] * jnp.where(inside, 1.0, 0.0).astype(BF16)
        s_start = s_off + head * DS
        inside = (lane >= s_start) & (lane < s_start + DS)
        s_query = win[FIRST_QUERY:, student] * jnp.where(inside, 1.0, 0.0).astype(BF16)
        qs[head * OWN : (head + 1) * OWN, :] = s_query
        rt[head] = (
            lax.dot_general(win[:, t_cols], t_query, NT, preferred_element_type=F32) + bias[...]
        )
        rs[head] = (
            lax.dot_general(win[:, student], s_query, NT, preferred_element_type=F32) + bias[...]
        )

    def maxima(head):
        for tile, (lanes, parts) in enumerate(tiles):
            for z, r, scale in ((0, rt, CT), (1, rs, CS)):
                top = fold(r[head, parts[0], lanes], jnp.max)
                for part in parts[1:]:
                    top = jnp.maximum(top, fold(r[head, part, lanes], jnp.max))
                tops[head, tile, z] = jnp.max(top, axis=0, keepdims=True) * scale

    def exponentials(head):
        for tile, (lanes, parts) in enumerate(tiles):
            top_t, top_s = tops[head, tile, 0], tops[head, tile, 1]
            sum_t = jnp.zeros((8, BLOCK), F32)
            sum_s = jnp.zeros((8, BLOCK), F32)
            cross = jnp.zeros((8, BLOCK), F32)
            for part in parts:
                ut = rt[head, part, lanes] * CT - top_t
                us = rs[head, part, lanes] * CS - top_s
                et = jnp.exp2(ut)
                es = jnp.exp2(us)
                sum_t = sum_t + fold(et, jnp.sum)
                sum_s = sum_s + fold(es, jnp.sum)
                cross = cross + fold(et * (ut - us), jnp.sum)
                rt[head, part, lanes] = et
                rs[head, part, lanes] = es
            sum_t = jnp.sum(sum_t, axis=0, keepdims=True)
            sum_s = jnp.sum(sum_s, axis=0, keepdims=True)
            cross = jnp.sum(cross, axis=0, keepdims=True)
            weight = weights[:, lanes]
            totals.append(weight * (cross / sum_t - jnp.log2(sum_t) + jnp.log2(sum_s)))
            sums[head, tile] = weight * DS ** (-0.5) / sum_t, weight * DS ** (-0.5) / sum_s

    def gradients(head):
        for tile, (lanes, parts) in enumerate(tiles):
            scale_t, scale_s = sums[head, tile]
            g_cols = slice(head * OWN + tile * BLOCK, head * OWN + (tile + 1) * BLOCK)
            for part in parts:
                gt[part, g_cols] = (
                    rs[head, part, lanes] * scale_s - rt[head, part, lanes] * scale_t
                ).astype(BF16)

    row_grads = []

    def products(head):
        row_grads.append(
            jnp.dot(
                bt[s_off + head * DS : s_off + (head + 1) * DS, :],
                gt[:, head * OWN : (head + 1) * OWN],
                preferred_element_type=F32,
            )
        )

    def key_product(first, last):
        return jnp.dot(
            gt[:, first * OWN : last * OWN],
            qs[first * OWN : last * OWN, :],
            preferred_element_type=F32,
        )

    scores(0)
    scores(1)
    maxima(0)
    exponentials(0)
    scores(2)
    maxima(1)
    gradients(0)
    exponentials(1)
    products(0)
    scores(3)
    maxima(2)
    gradients(1)
    exponentials(2)
    products(1)
    kg[...] = key_product(0, 2)
    maxima(3)
    gradients(2)
    exponentials(3)
    products(2)
    gradients(3)
    products(3)
    key_grad = kg[...] + key_product(2, 4)
    loss_out[...] = loss_in[...] + functools.reduce(jnp.add, totals) * math.log(2.0)
    row_grads.insert(HEADS if s_off == 0 else 0, jnp.zeros((SP - SW, OWN), F32))
    row_grad = jnp.concatenate(row_grads, axis=0).T
    late = HALO + OWN - FIRST_QUERY
    grad_left[...] = key_grad[:HALO].astype(BF16)
    grad_own[: OWN - late, :] = key_grad[HALO:FIRST_QUERY]
    grad_own[OWN - late :, :] = key_grad[FIRST_QUERY : HALO + OWN] + row_grad[:late]
    grad_right[...] = (key_grad[HALO + OWN :] + row_grad[late:]).astype(BF16)


def join_kernel(core, loss, l0, l1, l2, r0, r1, r2, one, two, copies):
    copies[...] = jnp.broadcast_to(loss[...], copies.shape)

    def write(after, before):
        for rel, (left, right) in enumerate(((l0, r0), (l1, r1), (l2, r2))):
            before[:, rel * SP : (rel + 1) * SP] = left[...]
            after[:, rel * SP : (rel + 1) * SP] = right[...]

    @pl.when(core[0] == 0)
    def _():
        write(one, two)

    @pl.when(core[0] != 0)
    def _():
        write(two, one)


def merge_kernel(core, parts, o0, o1, o2, mine, other, keep, send, copies):
    copies[...] = jnp.broadcast_to(jnp.sum(parts[...], axis=0, keepdims=True), copies.shape)
    half = HALO - BLOCK
    for rel, own in enumerate((o0, o1, o2)):
        cols = slice(rel * SP, (rel + 1) * SP)

        @pl.when(core[0] == 0)
        def _():
            keep[:BLOCK, cols] = own[:BLOCK, :] + mine[:BLOCK, cols].astype(F32)
            keep[BLOCK:, cols] = other[:BLOCK, cols].astype(F32)
            send[:half, cols] = own[BLOCK : BLOCK + half, :] + mine[BLOCK:, cols].astype(F32)
            send[half:BLOCK, cols] = own[BLOCK + half :, :]
            send[BLOCK:, cols] = other[BLOCK:, cols].astype(F32)

        @pl.when(core[0] != 0)
        def _():
            keep[:BLOCK, cols] = own[BLOCK:, :] + mine[half:, cols].astype(F32)
            keep[BLOCK:, cols] = other[half:, cols].astype(F32)
            send[: BLOCK - half, cols] = own[: BLOCK - half, :]
            send[BLOCK - half : BLOCK, cols] = own[BLOCK - half : BLOCK, :] + mine[
                :half, cols
            ].astype(F32)
            send[BLOCK:, cols] = other[:half, cols].astype(F32)


def place_kernel(tokens, core, parts, keep, recv, oq, ok, ov, loss):
    me = core[0]
    total = jnp.sum(jnp.sum(parts[...], axis=0, keepdims=True), axis=1, keepdims=True)
    loss[...] = total * (1.0 / (3 * H * tokens))
    half = HALO - BLOCK
    empty = jnp.zeros((BLOCK, 2 * SW - SP), F32)
    gap = jnp.zeros((BLOCK - half, SP), F32)
    for rel, out in enumerate((oq, ok, ov)):
        cols = slice(rel * SP, (rel + 1) * SP)
        late = recv[BLOCK:, cols]
        first = jnp.concatenate([late, gap], axis=0)
        last = jnp.concatenate([gap, late], axis=0)
        ours = keep[:BLOCK, cols] + jnp.where(me == 0, last, first)
        theirs = keep[BLOCK:, cols] + recv[:BLOCK, cols]
        ours = jnp.concatenate([ours, empty], axis=1)
        theirs = jnp.concatenate([theirs, empty], axis=1)
        low = jnp.where(me == 0, ours, theirs)
        high = jnp.where(me == 0, theirs, ours)
        off = S_OFF[rel]
        if off:
            low = pltpu.roll(low, 2 * SW - off, 1)
        out[...] = low + pltpu.roll(high, SW - off, 1)


def shape(rows, cols, dtype):
    return jax.ShapeDtypeStruct((rows, cols), dtype)


def call_relation(rel, core, starts, weight, loss, chunk):
    return call(
        functools.partial(relation_kernel, rel),
        [
            shape(HALO, SP, BF16),
            shape(OWN, SP, F32),
            shape(HALO, SP, BF16),
            shape(1, BLOCK, F32),
        ],
        [SMEM] + [VMEM] * (3 + len(chunk)),
        scratch=[
            pltpu.VMEM((WINDOW, REL), BF16),
            pltpu.VMEM((WINDOW, OWN), F32),
            pltpu.VMEM((HEADS, WINDOW, OWN), F32),
            pltpu.VMEM((HEADS, WINDOW, OWN), F32),
            pltpu.VMEM((WINDOW, HEADS * OWN), BF16),
            pltpu.VMEM((HEADS * OWN, SP), BF16),
            pltpu.VMEM((SP, WINDOW), BF16),
            pltpu.VMEM((WINDOW, SP), F32),
        ],
        flops=2 * 16 * WINDOW * OWN * 256,
        moved=2 << 20,
        exps=2 * HEADS * WINDOW * OWN,
        limit=20,
    )(core, starts, weight, loss, *chunk)


def body(teacher_q, teacher_k, teacher_v, student_q, student_k, student_v, doc_ids, row_weight):
    tok = ("y", "z", "parity", "core")
    count = lax.axis_size(tok)
    core = lax.axis_index("core").astype(jnp.int32).reshape(1)
    chip = lax.axis_index(("y", "z", "parity"))

    def other_core(value):
        return lax.ppermute(value, "core", [(0, 1), (1, 0)])

    def neighbours(value, way, cross=0):
        step = (2 * way, -2 * way)
        pairs = [(i, ((i + step[i % 2]) % count) ^ cross) for i in range(count)]
        return lax.ppermute(value, tok, pairs)

    arrays = (teacher_q, teacher_k, teacher_v, student_q, student_k, student_v)

    def split(own, *after):
        return call(
            functools.partial(split_kernel, own),
            shape(BLOCK, WIDTH, BF16),
            [SMEM] + [HBM] * (6 + len(after)),
            scratch=[pltpu.VMEM(a.shape, BF16) for a in arrays] + [pltpu.SemaphoreType.DMA((6,))],
            moved=4 << 20,
            limit=56,
        )(core, *arrays, *after)

    send = split(False)
    recv = other_core(send)
    keep = split(True, send)
    edges = call_edges(-1, core, keep, recv)
    two = [neighbours(edge, -1) for edge in edges]
    doc_ids, row_weight, _ = lax.optimization_barrier((doc_ids, row_weight, edges[0]))
    starts, weight = call(
        mask_kernel,
        [shape(1, OWN, jnp.int32), shape(1, OWN, F32)],
        [SMEM] + [VMEM] * 2,
        moved=1 << 17,
    )(
        chip.astype(jnp.int32).reshape(1),
        doc_ids.reshape(-1, BLOCK),
        row_weight.reshape(-1, BLOCK),
    )
    one = [neighbours(edge, 1) for edge in call_edges(1, core, keep, recv, weight)]
    loss = jnp.zeros((1, BLOCK), F32)
    grads = []
    for rel in range(3):
        chunk = (keep, recv, *two, *(one if rel else one[:1]))
        *grad, loss = call_relation(rel, core, starts, weight, loss, chunk)
        grads.append(grad)

    stages = (("z", "parity", "core", "head"), ("y",))
    copies = [shape(lax.axis_size(axes), BLOCK, F32) for axes in stages]

    def exchange(value, axes):
        return lax.all_to_all(value, axes, 0, 0, tiled=True)

    one, two, parts = call(
        join_kernel,
        [shape(HALO, 3 * SP, BF16)] * 2 + [copies[0]],
        [SMEM] + [VMEM] * 7,
        moved=1 << 20,
    )(core, loss, *(g[0] for g in grads), *(g[2] for g in grads))
    one = neighbours(one, 1)
    two = neighbours(two, -1, 1)
    parts = exchange(parts, stages[0])
    kept, sent, parts = call(
        merge_kernel,
        [shape(OWN, 3 * SP, F32), shape(HALO, 3 * SP, F32), copies[1]],
        [SMEM] + [VMEM] * 6,
        moved=2 << 20,
    )(core, parts, *(g[1] for g in grads), one, two)
    received = other_core(sent)
    parts = exchange(parts, stages[1])
    grad_q, grad_k, grad_v, loss = call(
        functools.partial(place_kernel, doc_ids.shape[0]),
        [shape(BLOCK, 2 * SW, F32)] * 3 + [shape(1, 1, F32)],
        [SMEM] + [VMEM] * 3,
        moved=1 << 20,
    )(core, parts, kept, received)
    return grad_q, grad_k, grad_v, loss[0, 0]


def solution(mesh):
    tok, head = mesh.devices.shape
    z = 4 if tok == 128 else 1
    axes = ("y", "z", "parity", "core", "head")
    fine = Mesh(mesh.devices.reshape(tok // (4 * z), z, 2, 2, head), axes)
    rows = axes[:4]
    placed = (P(rows, "head"),) * 6 + (P(), P())
    return jax.shard_map(
        body,
        mesh=fine,
        in_specs=placed,
        out_specs=(P(rows, "head"),) * 3 + (P(),),
        check_vma=False,
    )
```

```python
import functools
import math

import jax
import jax.numpy as jnp
from jax import lax
from jax.experimental import pallas as pl
from jax.experimental.pallas import tpu as pltpu
from jax.sharding import Mesh
from jax.sharding import PartitionSpec as P

H = 32
DT = 160
DS = 48
SPAN = 384

BLOCK = 128
OWN = 2 * BLOCK
HALO = 192
WINDOW = OWN + 2 * HALO
FIRST_QUERY = WINDOW - OWN
HEADS = 4
TW = HEADS * DT
SW = HEADS * DS
SP = 256
REL = TW + SP
WIDTH_A = 2 * TW + 2 * SW
WIDTH = WIDTH_A + REL
T_AT = (0, TW, 0)
S_AT = (2 * TW, 2 * TW + 128, TW)
CHUNK_AT = (0, 0, WIDTH_A)
S_OFF = (0, SW - 128, 0)
CT = DT ** (-0.5) * math.log2(math.e)
CS = DS ** (-0.5) * math.log2(math.e)
NT = (((1,), (1,)), ((), ()))
FAR = 4096
VMEM = pl.BlockSpec(memory_space=pltpu.VMEM)
SMEM = pl.BlockSpec(memory_space=pltpu.SMEM)
HBM = pl.BlockSpec(memory_space=pltpu.HBM)
F32 = jnp.float32
BF16 = jnp.bfloat16


def call(kernel, out_shape, in_specs, scratch=(), flops=0, moved=0, exps=0, limit=8):
    return pl.pallas_call(
        kernel,
        out_shape=out_shape,
        in_specs=in_specs,
        out_specs=jax.tree.map(lambda _: VMEM, out_shape),
        scratch_shapes=list(scratch),
        compiler_params=pltpu.CompilerParams(vmem_limit_bytes=limit << 20),
        cost_estimate=pl.CostEstimate(flops=flops, bytes_accessed=moved, transcendentals=exps),
    )


def split_kernel(core, *refs):
    arrays, (send, keep), buffers, sems = refs[:6], refs[6:8], refs[8:14], refs[14]
    me = core[0]
    copies = [
        pltpu.make_async_copy(array, buffer, sems.at[i])
        for i, (array, buffer) in enumerate(zip(arrays, buffers))
    ]
    for copy in copies:
        copy.start()
    for copy in copies:
        copy.wait()
    lane = lax.broadcasted_iota(jnp.int32, (BLOCK, SP), 1)
    mine = pl.ds(pl.multiple_of(me * TW, 128), TW)
    other = pl.ds(pl.multiple_of((1 - me) * TW, 128), TW)
    ours, theirs = [], []
    for rel in range(3):
        teacher, student = buffers[rel], buffers[3 + rel]
        at = CHUNK_AT[rel] + T_AT[rel]
        keep[:, at : at + TW] = teacher[:, mine]
        send[:, at : at + TW] = teacher[:, other]
        low = jnp.where(lane < SW, student[:, :SP].astype(F32), 0.0)
        high = pltpu.roll(student[:, 128:].astype(F32), SP - (SW - 128), 1)
        high = jnp.where(lane < SW, high, 0.0)
        ours.append(jnp.where(me == 0, low, high))
        theirs.append(jnp.where(me == 0, high, low))
    for halves, out in ((ours, keep), (theirs, send)):
        second = pltpu.roll(halves[1], S_OFF[1], 1)
        at = 2 * TW
        out[:, at : at + 128] = halves[0][:, :128].astype(BF16)
        out[:, at + 128 : at + 256] = (halves[0][:, 128:] + second[:, :128]).astype(BF16)
        out[:, at + 256 : at + 384] = second[:, 128:].astype(BF16)
        out[:, WIDTH_A + TW :] = halves[2].astype(BF16)


def mask_kernel(chip, docs, rows, starts, weights):
    count = docs.shape[0]
    first = 2 * chip[0] - 2

    def row_of(ref, r):
        at = first + r
        return ref[pl.ds(lax.rem(at + count, count), 1), :]

    lines = []
    for r in range(6):
        at = first + r
        shift = jnp.where(at < 0, -FAR, jnp.where(at >= count, FAR, 0))
        lines.append((row_of(docs, r) + shift).astype(F32))

    def queries(parts):
        joined = jnp.broadcast_to(jnp.concatenate(parts, axis=1), (8, 3 * BLOCK))
        return pltpu.roll(joined, 2 * BLOCK + 64, 1)[:1, :OWN]

    query = queries(lines[3:])
    before = jnp.zeros((1, OWN), F32)
    for line in lines:
        keys = jnp.broadcast_to(line, (BLOCK, BLOCK)).T
        keys = jnp.concatenate([keys, keys], axis=1)
        before = before + jnp.sum(jnp.where(keys < query, 1.0, 0.0), axis=0, keepdims=True)
    starts[...] = before.astype(jnp.int32) - 64
    weights[...] = queries([row_of(rows, r) for r in range(3, 6)])


def edges_kernel(cols, core, keep, recv, *refs):
    one, two = refs[-2:]
    half = HALO - BLOCK

    def write(first, second, after, before):
        after[:half, :] = first[BLOCK - half :, cols]
        after[half:, :] = second[:, cols]
        before[:BLOCK, :] = first[:, cols]
        before[BLOCK:, :] = second[:half, cols]

    @pl.when(core[0] == 0)
    def _():
        write(keep, recv, one, two)

    @pl.when(core[0] != 0)
    def _():
        write(recv, keep, two, one)


def call_edges(cols, core, keep, recv, *after):
    return call(
        functools.partial(edges_kernel, cols),
        [shape(HALO, cols.stop - cols.start, BF16)] * 2,
        [SMEM] + [VMEM] * (2 + len(after)),
        moved=2 << 20,
    )(core, keep, recv, *after)


def fold(value, op):
    rows, lanes = value.shape
    return op(value.reshape(rows // 8, 8, lanes), axis=0)


def relation_kernel(
    rel,
    core,
    starts,
    weights,
    loss_in,
    *refs,
):
    keep, recv, one, two = refs[:-12]
    t_at, s_at, s_off = T_AT[rel], S_AT[rel], S_OFF[rel]
    grad_left, grad_own, grad_right, loss_out, win, bias, rt, rs, gt, qs, bt, kg = refs[-12:]
    me = core[0]
    def gather(at, rows, source):
        base = CHUNK_AT[rel] if source.shape[1] == WIDTH else 0
        win[at : at + rows, :TW] = source[:, base + t_at : base + t_at + TW]
        win[at : at + rows, TW:] = source[:, base + s_at : base + s_at + SP]

    def gather_all(*sources):
        at = 0
        for source in sources:
            gather(at, source.shape[0], source)
            at += source.shape[0]

    @pl.when(me == 0)
    def _():
        gather_all(one, keep, recv, two)

    @pl.when(me != 0)
    def _():
        gather_all(two, recv, keep, one)

    key = lax.broadcasted_iota(jnp.int32, (WINDOW, OWN), 0)
    query = lax.broadcasted_iota(jnp.int32, (WINDOW, OWN), 1) + FIRST_QUERY
    bias[...] = jnp.where((key >= starts[...]) & (key <= query), 0.0, -1e30)

    lane = lax.broadcasted_iota(jnp.int32, (OWN, SP), 1)
    student = slice(TW, REL)
    row = lax.broadcasted_iota(jnp.int32, (SP, SP), 0)
    col = lax.broadcasted_iota(jnp.int32, (SP, SP), 1)
    unit = jnp.where(row == col, 1.0, 0.0).astype(BF16)
    bt[...] = lax.dot_general(unit, win[:, student], NT, preferred_element_type=F32).astype(BF16)

    gt[:BLOCK, :] = jnp.zeros((BLOCK, HEADS * OWN), BF16)
    gt[WINDOW - BLOCK :, :] = jnp.zeros((BLOCK, HEADS * OWN), BF16)
    step = 64
    tiles = [
        (
            slice(tile * BLOCK, (tile + 1) * BLOCK),
            [slice(at, at + step) for at in range(tile * BLOCK, SPAN + (tile + 1) * BLOCK, step)],
        )
        for tile in range(2)
    ]
    tops, sums = {}, {}
    totals = []

    def scores(head):
        start = head * DT // 128 * 128
        inside = (lane >= head * DT - start) & (lane < (head + 1) * DT - start)
        t_cols = slice(start, start + 256)
        t_query = win[FIRST_QUERY:, t_cols] * jnp.where(inside, 1.0, 0.0).astype(BF16)
        s_start = s_off + head * DS
        inside = (lane >= s_start) & (lane < s_start + DS)
        s_query = win[FIRST_QUERY:, student] * jnp.where(inside, 1.0, 0.0).astype(BF16)
        qs[head * OWN : (head + 1) * OWN, :] = s_query
        rt[head] = (
            lax.dot_general(win[:, t_cols], t_query, NT, preferred_element_type=F32) + bias[...]
        )
        rs[head] = (
            lax.dot_general(win[:, student], s_query, NT, preferred_element_type=F32) + bias[...]
        )

    def maxima(head):
        for tile, (lanes, parts) in enumerate(tiles):
            for z, r, scale in ((0, rt, CT), (1, rs, CS)):
                top = fold(r[head, parts[0], lanes], jnp.max)
                for part in parts[1:]:
                    top = jnp.maximum(top, fold(r[head, part, lanes], jnp.max))
                tops[head, tile, z] = jnp.max(top, axis=0, keepdims=True) * scale

    def exponentials(head):
        for tile, (lanes, parts) in enumerate(tiles):
            top_t, top_s = tops[head, tile, 0], tops[head, tile, 1]
            sum_t = jnp.zeros((8, BLOCK), F32)
            sum_s = jnp.zeros((8, BLOCK), F32)
            cross = jnp.zeros((8, BLOCK), F32)
            for part in parts:
                ut = rt[head, part, lanes] * CT - top_t
                us = rs[head, part, lanes] * CS - top_s
                et = jnp.exp2(ut)
                es = jnp.exp2(us)
                sum_t = sum_t + fold(et, jnp.sum)
                sum_s = sum_s + fold(es, jnp.sum)
                cross = cross + fold(et * (ut - us), jnp.sum)
                rt[head, part, lanes] = et
                rs[head, part, lanes] = es
            sum_t = jnp.sum(sum_t, axis=0, keepdims=True)
            sum_s = jnp.sum(sum_s, axis=0, keepdims=True)
            cross = jnp.sum(cross, axis=0, keepdims=True)
            weight = weights[:, lanes]
            totals.append(weight * (cross / sum_t - jnp.log2(sum_t) + jnp.log2(sum_s)))
            sums[head, tile] = weight * DS ** (-0.5) / sum_t, weight * DS ** (-0.5) / sum_s

    def gradients(head):
        for tile, (lanes, parts) in enumerate(tiles):
            scale_t, scale_s = sums[head, tile]
            g_cols = slice(head * OWN + tile * BLOCK, head * OWN + (tile + 1) * BLOCK)
            for part in parts:
                gt[part, g_cols] = (
                    rs[head, part, lanes] * scale_s - rt[head, part, lanes] * scale_t
                ).astype(BF16)

    row_grads = []

    def products(head):
        row_grads.append(
            jnp.dot(
                bt[s_off + head * DS : s_off + (head + 1) * DS, :],
                gt[:, head * OWN : (head + 1) * OWN],
                preferred_element_type=F32,
            )
        )

    def key_product(first, last):
        return jnp.dot(
            gt[:, first * OWN : last * OWN],
            qs[first * OWN : last * OWN, :],
            preferred_element_type=F32,
        )

    scores(0)
    scores(1)
    maxima(0)
    exponentials(0)
    scores(2)
    maxima(1)
    gradients(0)
    exponentials(1)
    products(0)
    scores(3)
    maxima(2)
    gradients(1)
    exponentials(2)
    products(1)
    kg[...] = key_product(0, 2)
    maxima(3)
    gradients(2)
    exponentials(3)
    products(2)
    gradients(3)
    products(3)
    key_grad = kg[...] + key_product(2, 4)
    loss_out[...] = loss_in[...] + functools.reduce(jnp.add, totals) * math.log(2.0)
    row_grads.insert(HEADS if s_off == 0 else 0, jnp.zeros((SP - SW, OWN), F32))
    row_grad = jnp.concatenate(row_grads, axis=0).T
    late = HALO + OWN - FIRST_QUERY
    grad_left[...] = key_grad[:HALO].astype(BF16)
    grad_own[: OWN - late, :] = key_grad[HALO:FIRST_QUERY]
    grad_own[OWN - late :, :] = key_grad[FIRST_QUERY : HALO + OWN] + row_grad[:late]
    grad_right[...] = (key_grad[HALO + OWN :] + row_grad[late:]).astype(BF16)


def join_kernel(core, loss, l0, l1, l2, r0, r1, r2, one, two, copies):
    copies[...] = jnp.broadcast_to(loss[...], copies.shape)

    def write(after, before):
        for rel, (left, right) in enumerate(((l0, r0), (l1, r1), (l2, r2))):
            before[:, rel * SP : (rel + 1) * SP] = left[...]
            after[:, rel * SP : (rel + 1) * SP] = right[...]

    @pl.when(core[0] == 0)
    def _():
        write(one, two)

    @pl.when(core[0] != 0)
    def _():
        write(two, one)


def merge_kernel(core, parts, o0, o1, o2, mine, other, keep, send, copies):
    copies[...] = jnp.broadcast_to(jnp.sum(parts[...], axis=0, keepdims=True), copies.shape)
    half = HALO - BLOCK
    for rel, own in enumerate((o0, o1, o2)):
        cols = slice(rel * SP, (rel + 1) * SP)

        @pl.when(core[0] == 0)
        def _():
            keep[:BLOCK, cols] = own[:BLOCK, :] + mine[:BLOCK, cols].astype(F32)
            keep[BLOCK:, cols] = other[:BLOCK, cols].astype(F32)
            send[:half, cols] = own[BLOCK : BLOCK + half, :] + mine[BLOCK:, cols].astype(F32)
            send[half:BLOCK, cols] = own[BLOCK + half :, :]
            send[BLOCK:, cols] = other[BLOCK:, cols].astype(F32)

        @pl.when(core[0] != 0)
        def _():
            keep[:BLOCK, cols] = own[BLOCK:, :] + mine[half:, cols].astype(F32)
            keep[BLOCK:, cols] = other[half:, cols].astype(F32)
            send[: BLOCK - half, cols] = own[: BLOCK - half, :]
            send[BLOCK - half : BLOCK, cols] = own[BLOCK - half : BLOCK, :] + mine[
                :half, cols
            ].astype(F32)
            send[BLOCK:, cols] = other[:half, cols].astype(F32)


def place_kernel(tokens, core, parts, keep, recv, oq, ok, ov, loss):
    me = core[0]
    total = jnp.sum(jnp.sum(parts[...], axis=0, keepdims=True), axis=1, keepdims=True)
    loss[...] = total * (1.0 / (3 * H * tokens))
    half = HALO - BLOCK
    empty = jnp.zeros((BLOCK, 2 * SW - SP), F32)
    gap = jnp.zeros((BLOCK - half, SP), F32)
    for rel, out in enumerate((oq, ok, ov)):
        cols = slice(rel * SP, (rel + 1) * SP)
        late = recv[BLOCK:, cols]
        first = jnp.concatenate([late, gap], axis=0)
        last = jnp.concatenate([gap, late], axis=0)
        ours = keep[:BLOCK, cols] + jnp.where(me == 0, last, first)
        theirs = keep[BLOCK:, cols] + recv[:BLOCK, cols]
        ours = jnp.concatenate([ours, empty], axis=1)
        theirs = jnp.concatenate([theirs, empty], axis=1)
        low = jnp.where(me == 0, ours, theirs)
        high = jnp.where(me == 0, theirs, ours)
        off = S_OFF[rel]
        if off:
            low = pltpu.roll(low, 2 * SW - off, 1)
        out[...] = low + pltpu.roll(high, SW - off, 1)


def shape(rows, cols, dtype):
    return jax.ShapeDtypeStruct((rows, cols), dtype)


def call_relation(rel, core, starts, weight, loss, chunk):
    return call(
        functools.partial(relation_kernel, rel),
        [
            shape(HALO, SP, BF16),
            shape(OWN, SP, F32),
            shape(HALO, SP, BF16),
            shape(1, BLOCK, F32),
        ],
        [SMEM] + [VMEM] * (3 + len(chunk)),
        scratch=[
            pltpu.VMEM((WINDOW, REL), BF16),
            pltpu.VMEM((WINDOW, OWN), F32),
            pltpu.VMEM((HEADS, WINDOW, OWN), F32),
            pltpu.VMEM((HEADS, WINDOW, OWN), F32),
            pltpu.VMEM((WINDOW, HEADS * OWN), BF16),
            pltpu.VMEM((HEADS * OWN, SP), BF16),
            pltpu.VMEM((SP, WINDOW), BF16),
            pltpu.VMEM((WINDOW, SP), F32),
        ],
        flops=2 * 16 * WINDOW * OWN * 256,
        moved=2 << 20,
        exps=2 * HEADS * WINDOW * OWN,
        limit=20,
    )(core, starts, weight, loss, *chunk)


def body(teacher_q, teacher_k, teacher_v, student_q, student_k, student_v, doc_ids, row_weight):
    tok = ("y", "z", "parity", "core")
    count = lax.axis_size(tok)
    core = lax.axis_index("core").astype(jnp.int32).reshape(1)
    chip = lax.axis_index(("y", "z", "parity"))

    def other_core(value):
        return lax.ppermute(value, "core", [(0, 1), (1, 0)])

    def neighbours(value, way, cross=0):
        step = (2 * way, -2 * way)
        pairs = [(i, ((i + step[i % 2]) % count) ^ cross) for i in range(count)]
        return lax.ppermute(value, tok, pairs)

    arrays = (teacher_q, teacher_k, teacher_v, student_q, student_k, student_v)
    send, keep = call(
        split_kernel,
        [shape(BLOCK, WIDTH, BF16)] * 2,
        [SMEM] + [HBM] * 6,
        scratch=[pltpu.VMEM(a.shape, BF16) for a in arrays] + [pltpu.SemaphoreType.DMA((6,))],
        moved=4 << 20,
        limit=56,
    )(core, *arrays)
    recv = other_core(send)
    edges_a = call_edges(slice(0, WIDTH_A), core, keep, recv)
    halo_a = [neighbours(edges_a[0], 1), neighbours(edges_a[1], -1)]
    doc_ids, row_weight, _ = lax.optimization_barrier((doc_ids, row_weight, edges_a[0]))
    starts, weight = call(
        mask_kernel,
        [shape(1, OWN, jnp.int32), shape(1, OWN, F32)],
        [SMEM] + [VMEM] * 2,
        moved=1 << 17,
    )(
        chip.astype(jnp.int32).reshape(1),
        doc_ids.reshape(-1, BLOCK),
        row_weight.reshape(-1, BLOCK),
    )
    edges_b = call_edges(slice(WIDTH_A, WIDTH), core, keep, recv, weight)
    halo_b = [neighbours(edges_b[0], 1), neighbours(edges_b[1], -1)]
    loss = jnp.zeros((1, BLOCK), F32)
    grads = []
    for rel in range(3):
        chunk = (keep, recv, *(halo_b if rel == 2 else halo_a))
        *grad, loss = call_relation(rel, core, starts, weight, loss, chunk)
        grads.append(grad)

    stages = (("z", "parity", "core"), ("y", "head"))
    copies = [shape(lax.axis_size(axes), BLOCK, F32) for axes in stages]

    def exchange(value, axes):
        return lax.all_to_all(value, axes, 0, 0, tiled=True)

    one, two, parts = call(
        join_kernel,
        [shape(HALO, 3 * SP, BF16)] * 2 + [copies[0]],
        [SMEM] + [VMEM] * 7,
        moved=1 << 20,
    )(core, loss, *(g[0] for g in grads), *(g[2] for g in grads))
    one = neighbours(one, 1)
    two = neighbours(two, -1, 1)
    parts = exchange(parts, stages[0])
    kept, sent, parts = call(
        merge_kernel,
        [shape(OWN, 3 * SP, F32), shape(HALO, 3 * SP, F32), copies[1]],
        [SMEM] + [VMEM] * 6,
        moved=2 << 20,
    )(core, parts, *(g[1] for g in grads), one, two)
    received = other_core(sent)
    parts = exchange(parts, stages[1])
    grad_q, grad_k, grad_v, loss = call(
        functools.partial(place_kernel, doc_ids.shape[0]),
        [shape(BLOCK, 2 * SW, F32)] * 3 + [shape(1, 1, F32)],
        [SMEM] + [VMEM] * 3,
        moved=1 << 20,
    )(core, parts, kept, received)
    return grad_q, grad_k, grad_v, loss[0, 0]


def solution(mesh):
    tok, head = mesh.devices.shape
    z = 4 if tok == 128 else 1
    axes = ("y", "z", "parity", "core", "head")
    fine = Mesh(mesh.devices.reshape(tok // (4 * z), z, 2, 2, head), axes)
    rows = axes[:4]
    placed = (P(rows, "head"),) * 6 + (P(), P())
    return jax.shard_map(
        body,
        mesh=fine,
        in_specs=placed,
        out_specs=(P(rows, "head"),) * 3 + (P(),),
        check_vma=False,
    )
```

```python
import functools
import math

import jax
import jax.numpy as jnp
from jax import lax
from jax.experimental import pallas as pl
from jax.experimental.pallas import tpu as pltpu
from jax.sharding import Mesh
from jax.sharding import PartitionSpec as P

H = 32
DT = 160
DS = 48
SPAN = 384

BLOCK = 128
OWN = 2 * BLOCK
HALO = 192
WINDOW = OWN + 2 * HALO
FIRST_QUERY = WINDOW - OWN
HEADS = 4
TW = HEADS * DT
SW = HEADS * DS
SP = 256
REL = TW + SP
WIDTH_A = 2 * TW + 2 * SW
WIDTH = WIDTH_A + REL
T_AT = (0, TW, 0)
S_AT = (2 * TW, 2 * TW + 128, TW)
CHUNK_AT = (0, 0, WIDTH_A)
S_OFF = (0, SW - 128, 0)
CT = DT ** (-0.5) * math.log2(math.e)
CS = DS ** (-0.5) * math.log2(math.e)
NT = (((1,), (1,)), ((), ()))
FAR = 4096
VMEM = pl.BlockSpec(memory_space=pltpu.VMEM)
SMEM = pl.BlockSpec(memory_space=pltpu.SMEM)
HBM = pl.BlockSpec(memory_space=pltpu.HBM)
F32 = jnp.float32
BF16 = jnp.bfloat16


def call(kernel, out_shape, in_specs, scratch=(), flops=0, moved=0, exps=0, limit=8):
    return pl.pallas_call(
        kernel,
        out_shape=out_shape,
        in_specs=in_specs,
        out_specs=jax.tree.map(lambda _: VMEM, out_shape),
        scratch_shapes=list(scratch),
        compiler_params=pltpu.CompilerParams(vmem_limit_bytes=limit << 20),
        cost_estimate=pl.CostEstimate(flops=flops, bytes_accessed=moved, transcendentals=exps),
    )


def split_kernel(core, *refs):
    arrays, (send, keep), buffers, sems = refs[:6], refs[6:8], refs[8:14], refs[14]
    me = core[0]
    copies = [
        pltpu.make_async_copy(array, buffer, sems.at[i])
        for i, (array, buffer) in enumerate(zip(arrays, buffers))
    ]
    for copy in copies:
        copy.start()
    for copy in copies:
        copy.wait()
    lane = lax.broadcasted_iota(jnp.int32, (BLOCK, SP), 1)
    mine = pl.ds(pl.multiple_of(me * TW, 128), TW)
    other = pl.ds(pl.multiple_of((1 - me) * TW, 128), TW)
    ours, theirs = [], []
    for rel in range(3):
        teacher, student = buffers[rel], buffers[3 + rel]
        at = CHUNK_AT[rel] + T_AT[rel]
        keep[:, at : at + TW] = teacher[:, mine]
        send[:, at : at + TW] = teacher[:, other]
        low = jnp.where(lane < SW, student[:, :SP].astype(F32), 0.0)
        high = pltpu.roll(student[:, 128:].astype(F32), SP - (SW - 128), 1)
        high = jnp.where(lane < SW, high, 0.0)
        ours.append(jnp.where(me == 0, low, high))
        theirs.append(jnp.where(me == 0, high, low))
    for halves, out in ((ours, keep), (theirs, send)):
        second = pltpu.roll(halves[1], S_OFF[1], 1)
        at = 2 * TW
        out[:, at : at + 128] = halves[0][:, :128].astype(BF16)
        out[:, at + 128 : at + 256] = (halves[0][:, 128:] + second[:, :128]).astype(BF16)
        out[:, at + 256 : at + 384] = second[:, 128:].astype(BF16)
        out[:, WIDTH_A + TW :] = halves[2].astype(BF16)


def mask_kernel(chip, docs, rows, starts, weights):
    count = docs.shape[0]
    first = 2 * chip[0] - 2

    def row_of(ref, r):
        at = first + r
        return ref[pl.ds(lax.rem(at + count, count), 1), :]

    lines = []
    for r in range(6):
        at = first + r
        shift = jnp.where(at < 0, -FAR, jnp.where(at >= count, FAR, 0))
        lines.append((row_of(docs, r) + shift).astype(F32))

    def queries(parts):
        joined = jnp.broadcast_to(jnp.concatenate(parts, axis=1), (8, 3 * BLOCK))
        return pltpu.roll(joined, 2 * BLOCK + 64, 1)[:1, :OWN]

    query = queries(lines[3:])
    before = jnp.zeros((1, OWN), F32)
    for line in lines:
        keys = jnp.broadcast_to(line, (BLOCK, BLOCK)).T
        keys = jnp.concatenate([keys, keys], axis=1)
        before = before + jnp.sum(jnp.where(keys < query, 1.0, 0.0), axis=0, keepdims=True)
    starts[...] = before.astype(jnp.int32) - 64
    weights[...] = queries([row_of(rows, r) for r in range(3, 6)])


def edges_kernel(cols, core, keep, recv, *refs):
    one, two = refs[-2:]
    half = HALO - BLOCK

    def write(first, second, after, before):
        after[:half, :] = first[BLOCK - half :, cols]
        after[half:, :] = second[:, cols]
        before[:BLOCK, :] = first[:, cols]
        before[BLOCK:, :] = second[:half, cols]

    @pl.when(core[0] == 0)
    def _():
        write(keep, recv, one, two)

    @pl.when(core[0] != 0)
    def _():
        write(recv, keep, two, one)


def edge_kernel(way, cols, core, keep, recv, *refs):
    out = refs[-1]
    half = HALO - BLOCK

    def write(first, second, late):
        if late:
            out[:half, :] = first[BLOCK - half :, cols]
            out[half:, :] = second[:, cols]
        else:
            out[:BLOCK, :] = first[:, cols]
            out[BLOCK:, :] = second[:half, cols]

    @pl.when(core[0] == 0)
    def _():
        write(keep, recv, way > 0)

    @pl.when(core[0] != 0)
    def _():
        write(recv, keep, way < 0)


def call_edge(way, cols, core, keep, recv):
    return call(
        functools.partial(edge_kernel, way, cols),
        shape(HALO, cols.stop - cols.start, BF16),
        [SMEM] + [VMEM] * 2,
        moved=1 << 20,
    )(core, keep, recv)


def call_edges(cols, core, keep, recv, *after):
    return call(
        functools.partial(edges_kernel, cols),
        [shape(HALO, cols.stop - cols.start, BF16)] * 2,
        [SMEM] + [VMEM] * (2 + len(after)),
        moved=2 << 20,
    )(core, keep, recv, *after)


def fold(value, op):
    rows, lanes = value.shape
    return op(value.reshape(rows // 8, 8, lanes), axis=0)


def relation_kernel(
    rel,
    core,
    starts,
    weights,
    loss_in,
    *refs,
):
    keep, recv, one, two = refs[:-12]
    if rel == 2:
        one, two = two, one
    t_at, s_at, s_off = T_AT[rel], S_AT[rel], S_OFF[rel]
    grad_left, grad_own, grad_right, loss_out, win, bias, rt, rs, gt, qs, bt, kg = refs[-12:]
    me = core[0]
    def gather(at, rows, source):
        base = CHUNK_AT[rel] if source.shape[1] == WIDTH else 0
        win[at : at + rows, :TW] = source[:, base + t_at : base + t_at + TW]
        win[at : at + rows, TW:] = source[:, base + s_at : base + s_at + SP]

    def gather_all(*sources):
        at = 0
        for source in sources:
            gather(at, source.shape[0], source)
            at += source.shape[0]

    @pl.when(me == 0)
    def _():
        gather_all(one, keep, recv, two)

    @pl.when(me != 0)
    def _():
        gather_all(two, recv, keep, one)

    key = lax.broadcasted_iota(jnp.int32, (WINDOW, OWN), 0)
    query = lax.broadcasted_iota(jnp.int32, (WINDOW, OWN), 1) + FIRST_QUERY
    bias[...] = jnp.where((key >= starts[...]) & (key <= query), 0.0, -1e30)

    lane = lax.broadcasted_iota(jnp.int32, (OWN, SP), 1)
    student = slice(TW, REL)
    row = lax.broadcasted_iota(jnp.int32, (SP, SP), 0)
    col = lax.broadcasted_iota(jnp.int32, (SP, SP), 1)
    unit = jnp.where(row == col, 1.0, 0.0).astype(BF16)
    bt[...] = lax.dot_general(unit, win[:, student], NT, preferred_element_type=F32).astype(BF16)

    gt[:BLOCK, :] = jnp.zeros((BLOCK, HEADS * OWN), BF16)
    gt[WINDOW - BLOCK :, :] = jnp.zeros((BLOCK, HEADS * OWN), BF16)
    step = 64
    tiles = [
        (
            slice(tile * BLOCK, (tile + 1) * BLOCK),
            [slice(at, at + step) for at in range(tile * BLOCK, SPAN + (tile + 1) * BLOCK, step)],
        )
        for tile in range(2)
    ]
    tops, sums = {}, {}
    totals = []

    def scores(head):
        start = head * DT // 128 * 128
        inside = (lane >= head * DT - start) & (lane < (head + 1) * DT - start)
        t_cols = slice(start, start + 256)
        t_query = win[FIRST_QUERY:, t_cols] * jnp.where(inside, 1.0, 0.0).astype(BF16)
        s_start = s_off + head * DS
        inside = (lane >= s_start) & (lane < s_start + DS)
        s_query = win[FIRST_QUERY:, student] * jnp.where(inside, 1.0, 0.0).astype(BF16)
        qs[head * OWN : (head + 1) * OWN, :] = s_query
        rt[head] = (
            lax.dot_general(win[:, t_cols], t_query, NT, preferred_element_type=F32) + bias[...]
        )
        rs[head] = (
            lax.dot_general(win[:, student], s_query, NT, preferred_element_type=F32) + bias[...]
        )

    def maxima(head):
        for tile, (lanes, parts) in enumerate(tiles):
            for z, r, scale in ((0, rt, CT), (1, rs, CS)):
                top = fold(r[head, parts[0], lanes], jnp.max)
                for part in parts[1:]:
                    top = jnp.maximum(top, fold(r[head, part, lanes], jnp.max))
                tops[head, tile, z] = jnp.max(top, axis=0, keepdims=True) * scale

    def exponentials(head):
        for tile, (lanes, parts) in enumerate(tiles):
            top_t, top_s = tops[head, tile, 0], tops[head, tile, 1]
            sum_t = jnp.zeros((8, BLOCK), F32)
            sum_s = jnp.zeros((8, BLOCK), F32)
            cross = jnp.zeros((8, BLOCK), F32)
            for part in parts:
                ut = rt[head, part, lanes] * CT - top_t
                us = rs[head, part, lanes] * CS - top_s
                et = jnp.exp2(ut)
                es = jnp.exp2(us)
                sum_t = sum_t + fold(et, jnp.sum)
                sum_s = sum_s + fold(es, jnp.sum)
                cross = cross + fold(et * (ut - us), jnp.sum)
                rt[head, part, lanes] = et
                rs[head, part, lanes] = es
            sum_t = jnp.sum(sum_t, axis=0, keepdims=True)
            sum_s = jnp.sum(sum_s, axis=0, keepdims=True)
            cross = jnp.sum(cross, axis=0, keepdims=True)
            weight = weights[:, lanes]
            totals.append(weight * (cross / sum_t - jnp.log2(sum_t) + jnp.log2(sum_s)))
            sums[head, tile] = weight * DS ** (-0.5) / sum_t, weight * DS ** (-0.5) / sum_s

    def gradients(head):
        for tile, (lanes, parts) in enumerate(tiles):
            scale_t, scale_s = sums[head, tile]
            g_cols = slice(head * OWN + tile * BLOCK, head * OWN + (tile + 1) * BLOCK)
            for part in parts:
                gt[part, g_cols] = (
                    rs[head, part, lanes] * scale_s - rt[head, part, lanes] * scale_t
                ).astype(BF16)

    row_grads = []

    def products(head):
        row_grads.append(
            jnp.dot(
                bt[s_off + head * DS : s_off + (head + 1) * DS, :],
                gt[:, head * OWN : (head + 1) * OWN],
                preferred_element_type=F32,
            )
        )

    def key_product(first, last):
        return jnp.dot(
            gt[:, first * OWN : last * OWN],
            qs[first * OWN : last * OWN, :],
            preferred_element_type=F32,
        )

    scores(0)
    scores(1)
    maxima(0)
    exponentials(0)
    scores(2)
    maxima(1)
    gradients(0)
    exponentials(1)
    products(0)
    scores(3)
    maxima(2)
    gradients(1)
    exponentials(2)
    products(1)
    kg[...] = key_product(0, 2)
    maxima(3)
    gradients(2)
    exponentials(3)
    products(2)
    gradients(3)
    products(3)
    key_grad = kg[...] + key_product(2, 4)
    loss_out[...] = loss_in[...] + functools.reduce(jnp.add, totals) * math.log(2.0)
    row_grads.insert(HEADS if s_off == 0 else 0, jnp.zeros((SP - SW, OWN), F32))
    row_grad = jnp.concatenate(row_grads, axis=0).T
    late = HALO + OWN - FIRST_QUERY
    grad_left[...] = key_grad[:HALO].astype(BF16)
    grad_own[: OWN - late, :] = key_grad[HALO:FIRST_QUERY]
    grad_own[OWN - late :, :] = key_grad[FIRST_QUERY : HALO + OWN] + row_grad[:late]
    grad_right[...] = (key_grad[HALO + OWN :] + row_grad[late:]).astype(BF16)


def join_kernel(core, loss, l0, l1, l2, r0, r1, r2, one, two, copies):
    copies[...] = jnp.broadcast_to(loss[...], copies.shape)

    def write(after, before):
        for rel, (left, right) in enumerate(((l0, r0), (l1, r1), (l2, r2))):
            before[:, rel * SP : (rel + 1) * SP] = left[...]
            after[:, rel * SP : (rel + 1) * SP] = right[...]

    @pl.when(core[0] == 0)
    def _():
        write(one, two)

    @pl.when(core[0] != 0)
    def _():
        write(two, one)


def merge_kernel(core, parts, o0, o1, o2, mine, other, keep, send, copies):
    copies[...] = jnp.broadcast_to(jnp.sum(parts[...], axis=0, keepdims=True), copies.shape)
    half = HALO - BLOCK
    for rel, own in enumerate((o0, o1, o2)):
        cols = slice(rel * SP, (rel + 1) * SP)

        @pl.when(core[0] == 0)
        def _():
            keep[:BLOCK, cols] = own[:BLOCK, :] + mine[:BLOCK, cols].astype(F32)
            keep[BLOCK:, cols] = other[:BLOCK, cols].astype(F32)
            send[:half, cols] = own[BLOCK : BLOCK + half, :] + mine[BLOCK:, cols].astype(F32)
            send[half:BLOCK, cols] = own[BLOCK + half :, :]
            send[BLOCK:, cols] = other[BLOCK:, cols].astype(F32)

        @pl.when(core[0] != 0)
        def _():
            keep[:BLOCK, cols] = own[BLOCK:, :] + mine[half:, cols].astype(F32)
            keep[BLOCK:, cols] = other[half:, cols].astype(F32)
            send[: BLOCK - half, cols] = own[: BLOCK - half, :]
            send[BLOCK - half : BLOCK, cols] = own[BLOCK - half : BLOCK, :] + mine[
                :half, cols
            ].astype(F32)
            send[BLOCK:, cols] = other[:half, cols].astype(F32)


def place_kernel(tokens, core, parts, keep, recv, oq, ok, ov, loss):
    me = core[0]
    total = jnp.sum(jnp.sum(parts[...], axis=0, keepdims=True), axis=1, keepdims=True)
    loss[...] = total * (1.0 / (3 * H * tokens))
    half = HALO - BLOCK
    empty = jnp.zeros((BLOCK, 2 * SW - SP), F32)
    gap = jnp.zeros((BLOCK - half, SP), F32)
    for rel, out in enumerate((oq, ok, ov)):
        cols = slice(rel * SP, (rel + 1) * SP)
        late = recv[BLOCK:, cols]
        first = jnp.concatenate([late, gap], axis=0)
        last = jnp.concatenate([gap, late], axis=0)
        ours = keep[:BLOCK, cols] + jnp.where(me == 0, last, first)
        theirs = keep[BLOCK:, cols] + recv[:BLOCK, cols]
        ours = jnp.concatenate([ours, empty], axis=1)
        theirs = jnp.concatenate([theirs, empty], axis=1)
        low = jnp.where(me == 0, ours, theirs)
        high = jnp.where(me == 0, theirs, ours)
        off = S_OFF[rel]
        if off:
            low = pltpu.roll(low, 2 * SW - off, 1)
        out[...] = low + pltpu.roll(high, SW - off, 1)


def shape(rows, cols, dtype):
    return jax.ShapeDtypeStruct((rows, cols), dtype)


def call_relation(rel, core, starts, weight, loss, chunk):
    return call(
        functools.partial(relation_kernel, rel),
        [
            shape(HALO, SP, BF16),
            shape(OWN, SP, F32),
            shape(HALO, SP, BF16),
            shape(1, BLOCK, F32),
        ],
        [SMEM] + [VMEM] * (3 + len(chunk)),
        scratch=[
            pltpu.VMEM((WINDOW, REL), BF16),
            pltpu.VMEM((WINDOW, OWN), F32),
            pltpu.VMEM((HEADS, WINDOW, OWN), F32),
            pltpu.VMEM((HEADS, WINDOW, OWN), F32),
            pltpu.VMEM((WINDOW, HEADS * OWN), BF16),
            pltpu.VMEM((HEADS * OWN, SP), BF16),
            pltpu.VMEM((SP, WINDOW), BF16),
            pltpu.VMEM((WINDOW, SP), F32),
        ],
        flops=2 * 16 * WINDOW * OWN * 256,
        moved=2 << 20,
        exps=2 * HEADS * WINDOW * OWN,
        limit=20,
    )(core, starts, weight, loss, *chunk)


def body(teacher_q, teacher_k, teacher_v, student_q, student_k, student_v, doc_ids, row_weight):
    tok = ("y", "z", "parity", "core")
    count = lax.axis_size(tok)
    core = lax.axis_index("core").astype(jnp.int32).reshape(1)
    chip = lax.axis_index(("y", "z", "parity"))

    def other_core(value):
        return lax.ppermute(value, "core", [(0, 1), (1, 0)])

    def neighbours(value, way, cross=0):
        step = (2 * way, -2 * way)
        pairs = [(i, ((i + step[i % 2]) % count) ^ cross) for i in range(count)]
        return lax.ppermute(value, tok, pairs)

    arrays = (teacher_q, teacher_k, teacher_v, student_q, student_k, student_v)
    send, keep = call(
        split_kernel,
        [shape(BLOCK, WIDTH, BF16)] * 2,
        [SMEM] + [HBM] * 6,
        scratch=[pltpu.VMEM(a.shape, BF16) for a in arrays] + [pltpu.SemaphoreType.DMA((6,))],
        moved=4 << 20,
        limit=56,
    )(core, *arrays)
    recv = other_core(send)
    back = call_edge(-1, slice(0, WIDTH_A), core, keep, recv)
    keep, recv, back = lax.optimization_barrier((keep, recv, back))
    edges_a = call_edge(1, slice(0, WIDTH_A), core, keep, recv), back
    halo_a = [neighbours(edges_a[0], 1), neighbours(edges_a[1], -1)]
    doc_ids, row_weight, _ = lax.optimization_barrier((doc_ids, row_weight, edges_a[0]))
    starts, weight = call(
        mask_kernel,
        [shape(1, OWN, jnp.int32), shape(1, OWN, F32)],
        [SMEM] + [VMEM] * 2,
        moved=1 << 17,
    )(
        chip.astype(jnp.int32).reshape(1),
        doc_ids.reshape(-1, BLOCK),
        row_weight.reshape(-1, BLOCK),
    )
    edges_b = call_edges(slice(WIDTH_A, WIDTH), core, keep, recv, weight)
    halo_b = [neighbours(edges_b[1], -1), neighbours(edges_b[0], 1)]
    loss = jnp.zeros((1, BLOCK), F32)
    grads = []
    for rel in range(3):
        chunk = (keep, recv, *(halo_b if rel == 2 else halo_a))
        *grad, loss = call_relation(rel, core, starts, weight, loss, chunk)
        grads.append(grad)

    stages = (("z", "parity", "core"), ("y", "head"))
    copies = [shape(lax.axis_size(axes), BLOCK, F32) for axes in stages]

    def exchange(value, axes):
        return lax.all_to_all(value, axes, 0, 0, tiled=True)

    one, two, parts = call(
        join_kernel,
        [shape(HALO, 3 * SP, BF16)] * 2 + [copies[0]],
        [SMEM] + [VMEM] * 7,
        moved=1 << 20,
    )(core, loss, *(g[0] for g in grads), *(g[2] for g in grads))
    one = neighbours(one, 1)
    two = neighbours(two, -1, 1)
    parts = exchange(parts, stages[0])
    kept, sent, parts = call(
        merge_kernel,
        [shape(OWN, 3 * SP, F32), shape(HALO, 3 * SP, F32), copies[1]],
        [SMEM] + [VMEM] * 6,
        moved=2 << 20,
    )(core, parts, *(g[1] for g in grads), one, two)
    received = other_core(sent)
    parts = exchange(parts, stages[1])
    grad_q, grad_k, grad_v, loss = call(
        functools.partial(place_kernel, doc_ids.shape[0]),
        [shape(BLOCK, 2 * SW, F32)] * 3 + [shape(1, 1, F32)],
        [SMEM] + [VMEM] * 3,
        moved=1 << 20,
    )(core, parts, kept, received)
    return grad_q, grad_k, grad_v, loss[0, 0]


def solution(mesh):
    tok, head = mesh.devices.shape
    z = 4 if tok == 128 else 1
    axes = ("y", "z", "parity", "core", "head")
    fine = Mesh(mesh.devices.reshape(tok // (4 * z), z, 2, 2, head), axes)
    rows = axes[:4]
    placed = (P(rows, "head"),) * 6 + (P(), P())
    return jax.shard_map(
        body,
        mesh=fine,
        in_specs=placed,
        out_specs=(P(rows, "head"),) * 3 + (P(),),
        check_vma=False,
    )
```
